32 devices in a mesh: gx: 8 (over z, x), gy: 4 (over y, core).
Axes of the slice: x: 2, y: 2, z: 4, core: 2. Of those that a mesh axis runs over, the one named last changes fastest.
Arguments:
- order_params: float32 [24, 12, 64, 512], P(None, None, 'gx', 'gy'), may hold values from 0 to 1, as said below
- grain_ids: int32 [8, 4, 24], P('gx', 'gy'), may hold values from -1 to 1151, as said below
- channel_maps: int32 [8, 4, 4, 24], P('gx', 'gy'), may hold values from -1 to 23, as said below
- zplanes: int32 [2, 64, 512], P(None, 'gx', 'gy'), may hold values from 0 to 1151, as said below
Outputs:
- evolved: float32 [24, 12, 64, 512], P(None, None, 'gx', 'gy')
The draws below stay inside these ranges and needn't reach their ends.
Inputs may be any that keep to these rules, and one draw needn't show every extreme that they name: `order_params`: zero in every slot whose grain id is -1. `grain_ids`: grain ids are distinct within a block; -1 marks an empty slot. `channel_maps`: A non-negative entry for face f of a block names the adjacent block's slot with the same grain; the entries for face f of a block and for the opposite face of the adjacent block are inverse one-to-one matchings. At most 6 slots of a block have an entry for any one face, and in every draw some face of some block has exactly 6. A slot has an entry for at most one face. `zplanes`: each cell names one of the non-negative grain ids of its block.
All inputs are finite; a program needn't handle non-finite values.
Results may differ from the reference program's by a relative error of at most 0.00018.
Values sent between devices are 32-bit elements; how exact they have to be, the bound alone decides.
No kernel may reach another device: no remote copies, remote signals or barrier semaphores. Data moves between devices by JAX's collectives and lax.ppermute only.
A program may use at most 64 MiB of HBM per device.

```python
import jax
import jax.numpy as jnp
from jax import lax

SLOTS = 24
SHARED = 6
CZ = 12
CX = 8
CY = 128
STEPS = 3
PX = 8
PY = 4
NX = 64
NY = 512


def grain_layout(key):
    pair_x = jax.random.randint(jax.random.fold_in(key, 11), (PX, PY), 1, SHARED + 1)
    pair_x = pair_x.at[0, 0].set(SHARED)
    pair_x = pair_x.at[PX - 1, 0].set(1)
    pair_y = jax.random.randint(jax.random.fold_in(key, 12), (PX, PY), 1, SHARED + 1)
    pair_y = pair_y.at[0, 0].set(SHARED)
    pair_y = pair_y.at[PX - 1, PY - 1].set(1)
    counts = jnp.stack([jnp.roll(pair_x, 1, 0), pair_x, jnp.roll(pair_y, 1, 1), pair_y], axis=2)
    within = jnp.arange(SHARED, dtype=jnp.int32)
    linked = within[None, None, None, :] < counts[..., None]
    rows_grid = jnp.arange(PX, dtype=jnp.int32)[:, None] + jnp.zeros((PX, PY), jnp.int32)
    cols_grid = jnp.arange(PY, dtype=jnp.int32)[None, :] + jnp.zeros((PX, PY), jnp.int32)
    face_x_up = rows_grid * PY + cols_grid
    face_x_low = (rows_grid - 1) % PX * PY + cols_grid
    face_y_up = PX * PY + rows_grid * PY + cols_grid
    face_y_low = PX * PY + rows_grid * PY + (cols_grid - 1) % PY
    face_code = jnp.stack([face_x_low, face_x_up, face_y_low, face_y_up], axis=2)
    shared_code = face_code[..., None] * SHARED + within
    block_code = (rows_grid * PY + cols_grid)[..., None] * 4 + jnp.arange(4, dtype=jnp.int32)
    own_code = 2 * PX * PY * SHARED + block_code[..., None] * SHARED + within
    extra = jax.random.randint(jax.random.fold_in(key, 13), (PX, PY, 4, SHARED), 0, 2)
    extra = extra.at[PX - 1, PY - 1, 3, SHARED - 1].set(1)
    extra = extra.at[0, 0, 0, SHARED - 1].set(0)
    codes = jnp.where(linked, shared_code, jnp.where(extra == 1, own_code, -1)).reshape(PX, PY, SLOTS)
    keys = jax.random.split(jax.random.fold_in(key, 14), PX * PY)
    order = jax.vmap(lambda one_key: jax.random.permutation(one_key, SLOTS))(keys)
    order = order.reshape(PX, PY, SLOTS).astype(jnp.int32)
    inverse = jnp.argsort(order, axis=2, stable=True).astype(jnp.int32)
    slot_grains = jnp.take_along_axis(codes, inverse, axis=2)
    segments = order.reshape(PX, PY, 4, SHARED)
    partner = jnp.stack([jnp.roll(segments[:, :, 1], 1, 0), jnp.roll(segments[:, :, 0], -1, 0), jnp.roll(segments[:, :, 3], 1, 1), jnp.roll(segments[:, :, 2], -1, 1)], axis=2)
    target = jnp.where(linked, partner, -1)
    same_face = jnp.arange(4)[:, None] == jnp.arange(4)[None, :]
    table = jnp.where(same_face[None, None, :, :, None], target[:, :, None, :, :], -1)
    table = table.reshape(PX, PY, 4, SLOTS).astype(jnp.int32)
    face_maps = jnp.take_along_axis(table, inverse[:, :, None, :], axis=3)
    return (slot_grains.astype(jnp.int32), face_maps.astype(jnp.int32))


def draw_grain_ids(key, part):
    slot_grains, face_maps = grain_layout(key)
    return slot_grains


def draw_channel_maps(key, part):
    slot_grains, face_maps = grain_layout(key)
    return face_maps


def draw_zplanes(key, part):
    slot_grains, face_maps = grain_layout(key)
    active = (slot_grains >= 0).astype(jnp.int32)
    ranks = jnp.cumsum(active, axis=2) - active
    live = jnp.sum(active, axis=2)
    cell_live = jnp.repeat(jnp.repeat(live, CX, axis=0), CY, axis=1)
    picks = jax.random.randint(jax.random.fold_in(key, 15), (2, NX, NY), 0, cell_live[None])
    cell_grains = jnp.repeat(jnp.repeat(slot_grains, CX, axis=0), CY, axis=1)
    cell_ranks = jnp.repeat(jnp.repeat(ranks, CX, axis=0), CY, axis=1)
    cell_active = jnp.repeat(jnp.repeat(active, CX, axis=0), CY, axis=1)
    chosen = (cell_ranks[None] == picks[..., None]) & (cell_active[None] == 1)
    planes = jnp.sum(jnp.where(chosen, cell_grains[None], 0), axis=3)
    top_grain = jnp.max(slot_grains[PX - 1, PY - 1])
    big_code = 6 * PX * PY * SHARED
    low_grain = jnp.min(jnp.where(slot_grains[0, 0] >= 0, slot_grains[0, 0], big_code))
    planes = planes.at[0, NX - 1, NY - 1].set(top_grain)
    planes = planes.at[1, 0, 0].set(low_grain)
    return planes.astype(jnp.int32)


def draw_order_params(key, part):
    slot_grains, face_maps = grain_layout(key)
    active = (slot_grains >= 0).astype(jnp.float32)
    cell_active = jnp.repeat(jnp.repeat(active, CX, axis=0), CY, axis=1)
    cell_active = jnp.transpose(cell_active, (2, 0, 1))[:, None, :, :]
    raw = jax.random.uniform(jax.random.fold_in(key, 16), (SLOTS, CZ, NX, NY), jnp.float32)
    values = raw ** 3
    return (values * cell_active).astype(jnp.float32)


def setup_inputs(seed: int = 0) -> dict:
    key_list = jax.random.split(jax.random.key(seed), 5)
    return {
        "order_params": draw_order_params(jax.random.fold_in(key_list[4], 71), 0),
        "grain_ids": draw_grain_ids(jax.random.fold_in(key_list[4], 71), 0),
        "channel_maps": draw_channel_maps(jax.random.fold_in(key_list[4], 71), 0),
        "zplanes": draw_zplanes(jax.random.fold_in(key_list[4], 71), 0),
    }


time_step = 0.05
mobility = 1.0
alpha_coef = 1.0
beta_coef = 1.0
gamma_coef = 1.5
kappa_coef = 2.0


def remap(plane, index):
    valid = index >= 0
    safe = jnp.where(valid, index, 0).astype(jnp.int32)
    gather_index = jnp.broadcast_to(jnp.transpose(safe, (2, 0, 1))[:, None, :, :, None], plane.shape)
    picked = jnp.take_along_axis(plane, gather_index, axis=0)
    keep = jnp.transpose(valid, (2, 0, 1))[:, None, :, :, None]
    return jnp.where(keep, picked, jnp.float32(0.0))


def advance(field6, channel_maps, frozen6):
    lower_x = remap(jnp.roll(field6[:, :, :, -1], 1, axis=2), channel_maps[:, :, 0])
    upper_x = remap(jnp.roll(field6[:, :, :, 0], -1, axis=2), channel_maps[:, :, 1])
    last_y = jnp.transpose(field6[..., -1], (0, 1, 2, 4, 3))
    first_y = jnp.transpose(field6[..., 0], (0, 1, 2, 4, 3))
    lower_y = remap(jnp.roll(last_y, 1, axis=3), channel_maps[:, :, 2])
    upper_y = remap(jnp.roll(first_y, -1, axis=3), channel_maps[:, :, 3])
    total = jnp.sum(field6 * field6, axis=0)

    def one_slot(pieces):
        value, low_x, up_x, low_y, up_y, planes = pieces
        low_y = jnp.transpose(low_y, (0, 1, 3, 2))
        up_y = jnp.transpose(up_y, (0, 1, 3, 2))
        above_x = jnp.concatenate([value[:, :, 1:], up_x[:, :, None]], axis=2)
        below_x = jnp.concatenate([low_x[:, :, None], value[:, :, :-1]], axis=2)
        above_y = jnp.concatenate([value[..., 1:], up_y[..., None]], axis=4)
        below_y = jnp.concatenate([low_y[..., None], value[..., :-1]], axis=4)
        above_z = jnp.concatenate([value[1:], planes[1][None]], axis=0)
        below_z = jnp.concatenate([planes[0][None], value[:-1]], axis=0)
        laplace = above_x + below_x + above_y + below_y + above_z + below_z - 6.0 * value
        rate = (-alpha_coef * value + beta_coef * value ** 3
                + 2.0 * gamma_coef * value * (total - value * value) - kappa_coef * laplace)
        return value - time_step * mobility * rate

    return lax.map(one_slot, (field6, lower_x, upper_x, lower_y, upper_y, frozen6))


def reference(order_params, grain_ids, channel_maps, zplanes):
    field6 = order_params.reshape(SLOTS, CZ, PX, CX, PY, CY)
    planes6 = zplanes.reshape(2, PX, CX, PY, CY)
    slot_codes = jnp.transpose(grain_ids, (2, 0, 1))[:, None, :, None, :, None]
    frozen6 = ((planes6[None] == slot_codes) & (slot_codes >= 0)).astype(jnp.float32)
    for repeat_index in range(STEPS):
        field6 = advance(field6, channel_maps, frozen6)
    return field6.reshape(SLOTS, CZ, NX, NY)
```

```python
import functools

import jax
import jax.numpy as jnp
from jax import lax
from jax.experimental import pallas as pl
from jax.experimental.pallas import tpu as pltpu
from jax.sharding import PartitionSpec as P


LINKS = 6
SPAN = 8
GROUP = 16
RATE = 0.1
UNROLL = 4


def row_and_lane(rows, cols):
    row = lax.broadcasted_iota(jnp.int32, (rows, cols), 0)
    lane = lax.broadcasted_iota(jnp.int32, (rows, cols), 1)
    return row, lane


def spin(tile, amount):
    cols = tile.shape[1]
    amount = amount % cols
    return tile if amount == 0 else pltpu.roll(tile, amount, 1)


def group_sum(tile):
    shift = GROUP
    while shift < tile.shape[1]:
        tile = tile + spin(tile, shift)
        shift *= 2
    return tile


def step(src, dst, slots, depth, rows, cols, squares=None):
    row, lane = row_and_lane(rows, cols)
    first_row, last_row = row == 0, row == rows - 1
    first_lane, last_lane = lane == 0, lane == cols - 1

    def add(parts, s, term):
        parts[s % 4] = term if parts[s % 4] is None else parts[s % 4] + term

    def total(parts):
        return (parts[0] + parts[1]) + (parts[2] + parts[3])

    def at(z):
        return pl.ds(pl.multiple_of((z + 1) * rows, rows), rows)

    def layer(z, factor):
        following, parts = [None] * 4, [None] * 4
        for s in range(slots):
            v, below, above = src[s, at(z), :], src[s, at(z - 1), :], src[s, at(z + 1), :]
            add(following, s, above * above)
            x_sum = jnp.where(first_row, 0.0, pltpu.roll(v, 1, 0)) + jnp.where(
                last_row, 0.0, pltpu.roll(v, rows - 1, 0)
            )
            y_sum = jnp.where(first_lane, 0.0, pltpu.roll(v, 1, 1)) + jnp.where(
                last_lane, 0.0, pltpu.roll(v, cols - 1, 1)
            )
            new = RATE * (v * (factor + v * v) + ((x_sum + y_sum) + (below + above)))
            dst[s, at(z), :] = new
            if squares is not None:
                add(parts, s, new * new)
        if squares is not None:
            squares[pl.ds(pl.multiple_of(z * rows, rows), rows), :] = total(parts)
        return 4.5 - 1.5 * total(following)

    def layers(i, factor):
        for j in range(UNROLL):
            factor = layer(i * UNROLL + j, factor)
        return factor

    first = [None] * 4
    for s in range(slots):
        v = src[s, at(0), :]
        add(first, s, v * v)
    lax.fori_loop(0, depth // UNROLL, layers, 4.5 - 1.5 * total(first))


def gather_columns(tile_of, c, depth, rows, cols, beside=0):
    _, lane = row_and_lane(rows, cols)
    result, other = jnp.zeros((rows, cols), jnp.float32), jnp.zeros((rows, cols), jnp.float32)
    for k in range(LINKS):
        near, far = jnp.zeros_like(result), jnp.zeros_like(other)
        for z in range(depth):
            place = GROUP * k + z
            moved = spin(tile_of(k, z), place - c)
            near = jnp.where(lane == place, moved, near)
            if beside:
                far = jnp.where(lane == (place + beside) % cols, moved, far)
        result = result + near
        other = other + far
    return result, spin(other, -beside)


def raw_kernel(
    slots, depth, rows, cols,
    field, planes, grains, maps,
    now, y_low, y_up, lists,
    planes_in, grains_in, maps_in, inverse, arrived,
):
    copies = [
        pltpu.make_async_copy(maps, maps_in, arrived.at[0]),
        pltpu.make_async_copy(grains, grains_in, arrived.at[1]),
        pltpu.make_async_copy(planes, planes_in, arrived.at[2]),
        pltpu.make_async_copy(field, now.at[pl.ds(0, slots), pl.ds(rows, depth * rows), :], arrived.at[3]),
    ]
    for copy in copies:
        copy.start()
    now[slots] = jnp.zeros(((depth + 2) * rows, cols), jnp.float32)
    for face in range(4):
        for place in range(SPAN):
            lists[face * SPAN + place] = slots
    for t in range(slots + 1):
        inverse[t] = slots
        inverse[slots + 1 + t] = slots

    copies[0].wait()
    for s in range(slots):
        for face in (0, 2):
            partner = maps_in[0, 0, face, s]
            inverse[face // 2 * (slots + 1) + jnp.where(partner >= 0, partner, slots)] = s
    counts = [jnp.int32(face * SPAN) for face in range(4)]
    for s in range(slots):
        for face in range(4):
            if face in (1, 3):
                valid = maps_in[0, 0, face, s] >= 0
                slot = jnp.where(valid, s, slots)
            else:
                slot = inverse[face // 2 * (slots + 1) + s]
                valid = slot < slots
            lists[counts[face]] = slot
            counts[face] = counts[face] + valid.astype(jnp.int32)

    top = (depth + 1) * rows
    copies[1].wait()
    copies[2].wait()
    for s in range(slots):
        grain = grains_in[0, 0, s]
        now[s, pl.ds(0, rows), :] = jnp.where(planes_in[0] == grain, 1.0, 0.0)
        now[s, pl.ds(top, rows), :] = jnp.where(planes_in[1] == grain, 1.0, 0.0)
    copies[3].wait()

    y_low[pl.ds(0, rows), :], _ = gather_columns(
        lambda k, z: now[lists[2 * SPAN + k], pl.ds((z + 1) * rows, rows), :], 0, depth, rows, cols
    )
    y_up[pl.ds(0, rows), :], _ = gather_columns(
        lambda k, z: now[lists[3 * SPAN + k], pl.ds((z + 1) * rows, rows), :], cols - 1, depth, rows, cols
    )
    y_low[pl.ds(rows, rows), :], y_up[pl.ds(rows, rows), :] = gather_corners(now, lists, depth, rows, cols)


def gather_corners(ref, lists, depth, rows, cols):
    row, _ = row_and_lane(rows, cols)

    def both(k, z):
        at = pl.ds((z + 1) * rows, rows)
        return jnp.where(row < rows // 2, ref[lists[k], at, :], ref[lists[SPAN + k], at, :])

    return gather_columns(both, 0, depth, rows, cols, beside=-1)


def first_kernel(
    slots, depth, rows, cols,
    now, lists,
    stepped, x_low, x_up, y_low, y_up,
    squares,
):
    top = (depth + 1) * rows
    for s in range(slots):
        for at in (0, top):
            stepped[s, pl.ds(at, rows), :] = now[s, pl.ds(at, rows), :]
    stepped[slots] = jnp.zeros(((depth + 2) * rows, cols), jnp.float32)

    step(now, stepped, slots, depth, rows, cols, squares)

    row, lane = row_and_lane(rows, cols)
    block = LINKS * depth
    last_group = (lane >= LINKS * GROUP) & (lane < (LINKS + 1) * GROUP)

    partials = []
    for side, out in ((0, y_low), (1, y_up)):
        c, inward = (0, 1) if side == 0 else (cols - 1, -1)
        base = (2 + side) * SPAN
        partial, inner = gather_columns(
            lambda k, z: stepped[lists[base + k], pl.ds((z + 1) * rows, rows), :], c, depth, rows, cols, beside=inward
        )
        for k in range(LINKS):
            for z, at in ((0, 0), (depth - 1, top)):
                place = GROUP * k + z
                frozen = spin(now[lists[base + k], pl.ds(at, rows), :], place - c)
                inner = inner + jnp.where(lane == place, frozen, 0.0)
        total = jnp.zeros((rows, cols), jnp.float32)
        for z in range(depth):
            place = LINKS * GROUP + z
            total = jnp.where(lane == place, spin(squares[pl.ds(z * rows, rows), :], place - c), total)
        inner = jnp.where(last_group, total - group_sum(partial * partial), inner)
        out[pl.ds(0, rows), :] = partial
        out[pl.ds(rows, rows), :] = inner
        partials.append(partial)
    y_low[pl.ds(2 * rows, rows), :], y_up[pl.ds(2 * rows, rows), :] = gather_corners(stepped, lists, depth, rows, cols)

    for face, out in ((0, x_low), (1, x_up)):
        r, inner_r = (0, 1) if face == 0 else (rows - 1, rows - 2)
        out[pl.ds(3 * block, out.shape[0] - 3 * block), :] = jnp.zeros((out.shape[0] - 3 * block, cols), jnp.float32)
        rest = squares[pl.ds(r, depth, stride=rows), :]
        edge_row, _ = row_and_lane(depth, cols)
        for k in range(LINKS):
            slot = lists[face * SPAN + k]
            rim = now[slot, pl.ds(rows + r, depth, stride=rows), :]
            partial = stepped[slot, pl.ds(rows + r, depth, stride=rows), :]
            inner = stepped[slot, pl.ds(rows + inner_r, depth, stride=rows), :]
            below = jnp.broadcast_to(now[slot, pl.ds(r, 1), :], (depth, cols))
            above = jnp.broadcast_to(now[slot, pl.ds(top + r, 1), :], (depth, cols))
            inner = inner + jnp.where(edge_row == 0, below, jnp.where(edge_row == depth - 1, above, 0.0))
            rest = rest - partial * partial
            out[pl.ds(k * depth, depth), :] = rim
            out[pl.ds(block + k * depth, depth), :] = partial
            out[pl.ds(2 * block + k * depth, depth), :] = inner
        out[pl.ds(3 * block, depth), :] = rest
        for side in range(2):
            out[pl.ds(3 * block + depth + side, 1), :] = partials[side][r : r + 1]


def corner_kernel(depth, rows, cols, x_low_in, x_up_in, y_low, y_up, x_low, x_up):
    start = 3 * LINKS * depth + depth + 2
    for r, out in ((0, x_low), (rows - 1, x_up)):
        for side, got in ((0, y_low), (1, y_up)):
            out[pl.ds(start + side, 1), :] = got[pl.ds(r, 1), :]
            out[pl.ds(start + 2 + side, 1), :] = got[pl.ds(rows + r, 1), :]


def second_kernel(
    slots, depth, rows, cols,
    stepped_in, x_low_own, x_up_own, x_low, x_up, raw_low_own, raw_up_own, raw_low, raw_up,
    y_low_own, y_up_own, y_low, y_up, lists,
    now, result,
    later, x_one, x_two, sent,
):
    row, lane = row_and_lane(rows, cols)
    block = LINKS * depth
    tail = 3 * block + depth
    top = (depth + 1) * rows

    for s in range(slots):
        for at in (0, top):
            later[s, pl.ds(at, rows), :] = now[s, pl.ds(at, rows), :]
    later[slots] = jnp.zeros(((depth + 2) * rows, cols), jnp.float32)

    x_one[...] = jnp.zeros(x_one.shape, jnp.float32)
    tall_row, tall_lane = row_and_lane(GROUP, cols)
    for face, own, got in ((0, x_low_own, x_low), (1, x_up_own, x_up)):
        r = 0 if face == 0 else rows - 1
        total = got[pl.ds(3 * block, depth), :]
        ones, own_ones = [], []
        for k in range(LINKS):
            one = got[pl.ds(block + k * depth, depth), :] + RATE * own[pl.ds(k * depth, depth), :]
            own_one = own[pl.ds(block + k * depth, depth), :] + RATE * got[pl.ds(k * depth, depth), :]
            total = total + one * one
            x_one[face, pl.ds(k * GROUP + 1, depth), :] = one
            ones.append(one)
            own_ones.append(own_one)
        for k in range(LINKS):
            now[lists[face * SPAN + k], pl.ds(rows + r, depth, stride=rows), :] = own_ones[k]
        for side in range(2):
            c = 0 if side == 0 else cols - 1
            term = RATE * got[pl.ds(tail + 2 + side, 1), :]
            term = group_sum(term * (2.0 * got[pl.ds(tail + side, 1), :] + term))
            spread = jnp.where(tall_row == tall_lane, jnp.broadcast_to(term, (GROUP, cols)), 0.0)
            column = jnp.sum(spread, axis=1, keepdims=True)
            total = total + jnp.where(tall_lane == c, column, 0.0)[:depth]
        factor = 4.5 - 1.5 * total
        for k in range(LINKS):
            one = ones[k]
            z_sum = x_one[face, pl.ds(k * GROUP, depth), :] + x_one[face, pl.ds(k * GROUP + 2, depth), :]
            y_sum = jnp.where(tall_lane[:depth] == 0, 0.0, pltpu.roll(one, 1, 1)) + jnp.where(
                tall_lane[:depth] == cols - 1, 0.0, pltpu.roll(one, cols - 1, 1)
            )
            inner = got[pl.ds(2 * block + k * depth, depth), :]
            x_two[face, pl.ds(k * GROUP, depth), :] = RATE * (
                one * (factor + one * one) + ((inner + own_ones[k]) + (z_sum + y_sum))
            )

    y_own_one, y_one, y_two = [], [], []
    for side, raw_own, raw_got, own, got in (
        (0, raw_low_own, raw_low, y_low_own, y_low),
        (1, raw_up_own, raw_up, y_up_own, y_up),
    ):
        tile = lambda ref, i: ref[pl.ds(i * rows, rows), :]
        own_one = tile(own, 0) + RATE * tile(raw_got, 0)
        one = tile(got, 0) + RATE * tile(raw_own, 0)
        inner = tile(got, 1)
        term = RATE * jnp.where(
            row == 0,
            jnp.broadcast_to(x_low[pl.ds(tail + 4 + side, 1), :], (rows, cols)),
            jnp.where(
                row == rows - 1, jnp.broadcast_to(x_up[pl.ds(tail + 4 + side, 1), :], (rows, cols)), 0.0
            ),
        )
        rest = jnp.where((lane >= LINKS * GROUP) & (lane < (LINKS + 1) * GROUP), inner, 0.0)
        total = group_sum((one * one + rest) + term * (2.0 * tile(got, 2) + term))
        x_sum = jnp.where(row == 0, 0.0, pltpu.roll(one, 1, 0)) + jnp.where(
            row == rows - 1, 0.0, pltpu.roll(one, rows - 1, 0)
        )
        z_sum = spin(one, 1) + spin(one, -1)
        two = RATE * (one * ((4.5 - 1.5 * total) + one * one) + ((inner + own_one) + (x_sum + z_sum)))
        y_own_one.append(own_one)
        y_one.append(RATE * one)
        y_two.append(RATE * two)

    def y_faces(ref, tiles, replace):
        for k in range(LINKS):
            for side in range(2):
                c = 0 if side == 0 else cols - 1
                slot = lists[(2 + side) * SPAN + k]
                old = [ref[slot, pl.ds((z + 1) * rows, rows), :] for z in range(depth)]
                for z in range(depth):
                    moved = spin(tiles[side], c - GROUP * k - z)
                    new = jnp.where(lane == c, moved if replace else old[z] + moved, old[z])
                    ref[slot, pl.ds((z + 1) * rows, rows), :] = new

    def x_faces(ref, rim, offset):
        for face in range(2):
            at = pl.ds(rows + (0 if face == 0 else rows - 1), depth, stride=rows)
            old = [ref[lists[face * SPAN + k], at, :] for k in range(LINKS)]
            for k in range(LINKS):
                ref[lists[face * SPAN + k], at, :] = old[k] + RATE * rim[face, pl.ds(k * GROUP + offset, depth), :]

    y_faces(now, y_own_one, True)
    step(now, later, slots, depth, rows, cols)
    x_faces(later, x_one, 1)
    y_faces(later, y_one, False)
    step(later, now, slots, depth, rows, cols)
    x_faces(now, x_two, 0)
    y_faces(now, y_two, False)
    copy = pltpu.make_async_copy(now.at[pl.ds(0, slots), pl.ds(rows, depth * rows), :], result, sent)
    copy.start()
    copy.wait()


def shifted(block, axis, distance):
    size = lax.axis_size(axis)
    return lax.ppermute(block, axis, [((i - distance) % size, i) for i in range(size)])


def on_device(order_params, grain_ids, channel_maps, zplanes):
    slots, depth, rows, cols = order_params.shape
    f32 = jnp.float32
    shape = jax.ShapeDtypeStruct
    padded = pltpu.VMEM((slots + 1, (depth + 2) * rows, cols), f32)
    x_pack = shape((-(-(3 * LINKS * depth + depth + 6) // rows) * rows, cols), f32)
    vmem = pl.BlockSpec(memory_space=pltpu.VMEM)
    smem = pl.BlockSpec(memory_space=pltpu.SMEM)
    hbm = pl.BlockSpec(memory_space=pltpu.HBM)
    params = pltpu.CompilerParams(vmem_limit_bytes=24 * 1024 * 1024)
    field = order_params.reshape(slots, depth * rows, cols)
    sizes = (slots, depth, rows, cols)

    now, raw_low, raw_up, lists = pl.pallas_call(
        functools.partial(raw_kernel, *sizes),
        out_shape=[padded, shape((2 * rows, cols), f32), shape((2 * rows, cols), f32), shape((4 * SPAN,), jnp.int32)],
        in_specs=[hbm] * 4,
        out_specs=[vmem] * 3 + [smem],
        scratch_shapes=[
            pltpu.VMEM(zplanes.shape, jnp.int32),
            pltpu.SMEM(grain_ids.shape, jnp.int32),
            pltpu.SMEM(channel_maps.shape, jnp.int32),
            pltpu.SMEM((2 * (slots + 1),), jnp.int32),
            pltpu.SemaphoreType.DMA((4,)),
        ],
        compiler_params=params,
        name="raw_rims",
    )(*(pltpu.with_memory_space_constraint(x, pltpu.HBM) for x in (field, zplanes, grain_ids, channel_maps)))

    raw_from_right = shifted(raw_low, "gy", -1)
    raw_from_left = shifted(raw_up, "gy", 1)

    stepped, x_low, x_up, y_low, y_up = pl.pallas_call(
        functools.partial(first_kernel, *sizes),
        out_shape=[padded, x_pack, x_pack, shape((3 * rows, cols), f32), shape((3 * rows, cols), f32)],
        in_specs=[vmem, smem],
        out_specs=[vmem] * 5,
        scratch_shapes=[pltpu.VMEM((depth * rows, cols), f32)],
        compiler_params=params,
        name="first_step",
    )(now, lists)

    x_low, x_up = pl.pallas_call(
        functools.partial(corner_kernel, depth, rows, cols),
        out_shape=[x_pack, x_pack],
        in_specs=[vmem] * 4,
        out_specs=[vmem] * 2,
        input_output_aliases={0: 0, 1: 1},
        compiler_params=params,
        name="corners",
    )(x_low, x_up, raw_from_left, raw_from_right)

    from_up = shifted(x_low, "gx", -1)
    from_low = shifted(x_up, "gx", 1)
    from_right = shifted(y_low, "gy", -1)
    from_left = shifted(y_up, "gy", 1)

    _, result = pl.pallas_call(
        functools.partial(second_kernel, *sizes),
        out_shape=[padded, shape(field.shape, f32)],
        in_specs=[vmem] * 13 + [smem],
        out_specs=[vmem, hbm],
        scratch_shapes=[
            padded,
            pltpu.VMEM((2, LINKS * GROUP, cols), f32),
            pltpu.VMEM((2, LINKS * GROUP, cols), f32),
            pltpu.SemaphoreType.DMA,
        ],
        input_output_aliases={0: 0},
        compiler_params=params,
        name="later_steps",
    )(
        stepped, x_low, x_up, from_low, from_up, raw_low, raw_up, raw_from_left, raw_from_right,
        y_low, y_up, from_left, from_right, lists,
    )
    return result.reshape(order_params.shape)


def solution(mesh):
    in_specs = (
        P(None, None, "gx", "gy"),
        P("gx", "gy", None),
        P("gx", "gy", None, None),
        P(None, "gx", "gy"),
    )
    return jax.shard_map(
        on_device, mesh=mesh, in_specs=in_specs, out_specs=P(None, None, "gx", "gy"), check_vma=False
    )
```

```python
import functools

import jax
import jax.numpy as jnp
from jax import lax
from jax.experimental import pallas as pl
from jax.experimental.pallas import tpu as pltpu
from jax.sharding import PartitionSpec as P


LINKS = 6
SPAN = 8
GROUP = 16
RATE = 0.1
UNROLL = 4


def row_and_lane(rows, cols):
    row = lax.broadcasted_iota(jnp.int32, (rows, cols), 0)
    lane = lax.broadcasted_iota(jnp.int32, (rows, cols), 1)
    return row, lane


def spin(tile, amount):
    cols = tile.shape[1]
    amount = amount % cols
    return tile if amount == 0 else pltpu.roll(tile, amount, 1)


def group_sum(tile):
    shift = GROUP
    while shift < tile.shape[1]:
        tile = tile + spin(tile, shift)
        shift *= 2
    return tile


def step(src, dst, slots, depth, rows, cols, squares=None):
    row, lane = row_and_lane(rows, cols)
    first_row, last_row = row == 0, row == rows - 1
    first_lane, last_lane = lane == 0, lane == cols - 1

    def add(parts, s, term):
        parts[s % 4] = term if parts[s % 4] is None else parts[s % 4] + term

    def total(parts):
        return (parts[0] + parts[1]) + (parts[2] + parts[3])

    def at(z):
        return pl.ds(pl.multiple_of((z + 1) * rows, rows), rows)

    def layer(z, factor):
        following, parts = [None] * 4, [None] * 4
        for s in range(slots):
            v, below, above = src[s, at(z), :], src[s, at(z - 1), :], src[s, at(z + 1), :]
            add(following, s, above * above)
            x_sum = jnp.where(first_row, 0.0, pltpu.roll(v, 1, 0)) + jnp.where(
                last_row, 0.0, pltpu.roll(v, rows - 1, 0)
            )
            y_sum = jnp.where(first_lane, 0.0, pltpu.roll(v, 1, 1)) + jnp.where(
                last_lane, 0.0, pltpu.roll(v, cols - 1, 1)
            )
            new = RATE * (v * (factor + v * v) + ((x_sum + y_sum) + (below + above)))
            dst[s, at(z), :] = new
            if squares is not None:
                add(parts, s, new * new)
        if squares is not None:
            squares[pl.ds(pl.multiple_of(z * rows, rows), rows), :] = total(parts)
        return 4.5 - 1.5 * total(following)

    def layers(i, factor):
        for j in range(UNROLL):
            factor = layer(i * UNROLL + j, factor)
        return factor

    first = [None] * 4
    for s in range(slots):
        v = src[s, at(0), :]
        add(first, s, v * v)
    lax.fori_loop(0, depth // UNROLL, layers, 4.5 - 1.5 * total(first))


def gather_columns(tile_of, c, depth, rows, cols, beside=0):
    _, lane = row_and_lane(rows, cols)
    result, other = jnp.zeros((rows, cols), jnp.float32), jnp.zeros((rows, cols), jnp.float32)
    for k in range(LINKS):
        near, far = jnp.zeros_like(result), jnp.zeros_like(other)
        for z in range(depth):
            place = GROUP * k + z
            moved = spin(tile_of(k, z), place - c)
            near = jnp.where(lane == place, moved, near)
            if beside:
                far = jnp.where(lane == (place + beside) % cols, moved, far)
        result = result + near
        other = other + far
    return result, spin(other, -beside)


def first_kernel(
    slots, depth, rows, cols,
    field, planes, grains, maps,
    now, stepped, squares, x_low, x_up, lists,
    planes_in, grains_in, maps_in, inverse, arrived,
):
    copies = [
        pltpu.make_async_copy(maps, maps_in, arrived.at[0]),
        pltpu.make_async_copy(grains, grains_in, arrived.at[1]),
        pltpu.make_async_copy(planes, planes_in, arrived.at[2]),
        pltpu.make_async_copy(field, now.at[pl.ds(0, slots), pl.ds(rows, depth * rows), :], arrived.at[3]),
    ]
    for copy in copies:
        copy.start()
    for ref in (now, stepped):
        ref[slots] = jnp.zeros(((depth + 2) * rows, cols), jnp.float32)
    for face in range(4):
        for place in range(SPAN):
            lists[face * SPAN + place] = slots
    for t in range(slots + 1):
        inverse[t] = slots
        inverse[slots + 1 + t] = slots

    copies[0].wait()
    for s in range(slots):
        for face in (0, 2):
            partner = maps_in[0, 0, face, s]
            inverse[face // 2 * (slots + 1) + jnp.where(partner >= 0, partner, slots)] = s
    counts = [jnp.int32(face * SPAN) for face in range(4)]
    for s in range(slots):
        for face in range(4):
            if face in (1, 3):
                valid = maps_in[0, 0, face, s] >= 0
                slot = jnp.where(valid, s, slots)
            else:
                slot = inverse[face // 2 * (slots + 1) + s]
                valid = slot < slots
            lists[counts[face]] = slot
            counts[face] = counts[face] + valid.astype(jnp.int32)

    top = (depth + 1) * rows
    copies[1].wait()
    copies[2].wait()
    for s in range(slots):
        grain = grains_in[0, 0, s]
        below = jnp.where(planes_in[0] == grain, 1.0, 0.0)
        above = jnp.where(planes_in[1] == grain, 1.0, 0.0)
        for ref in (now, stepped):
            ref[s, pl.ds(0, rows), :] = below
            ref[s, pl.ds(top, rows), :] = above
    copies[3].wait()

    step(now, stepped, slots, depth, rows, cols, squares)

    block = LINKS * depth
    edge_row, _ = row_and_lane(depth, cols)
    for face, out in ((0, x_low), (1, x_up)):
        r, inner_r = (0, 1) if face == 0 else (rows - 1, rows - 2)
        out[pl.ds(3 * block, out.shape[0] - 3 * block), :] = jnp.zeros((out.shape[0] - 3 * block, cols), jnp.float32)
        rest = squares[pl.ds(r, depth, stride=rows), :]
        for k in range(LINKS):
            slot = lists[face * SPAN + k]
            rim = now[slot, pl.ds(rows + r, depth, stride=rows), :]
            partial = stepped[slot, pl.ds(rows + r, depth, stride=rows), :]
            inner = stepped[slot, pl.ds(rows + inner_r, depth, stride=rows), :]
            below = jnp.broadcast_to(now[slot, pl.ds(r, 1), :], (depth, cols))
            above = jnp.broadcast_to(now[slot, pl.ds(top + r, 1), :], (depth, cols))
            inner = inner + jnp.where(edge_row == 0, below, jnp.where(edge_row == depth - 1, above, 0.0))
            rest = rest - partial * partial
            out[pl.ds(k * depth, depth), :] = rim
            out[pl.ds(block + k * depth, depth), :] = partial
            out[pl.ds(2 * block + k * depth, depth), :] = inner
        out[pl.ds(3 * block, depth), :] = rest


def gather_corners(ref, lists, depth, rows, cols):
    row, _ = row_and_lane(rows, cols)

    def both(k, z):
        at = pl.ds((z + 1) * rows, rows)
        return jnp.where(row < rows // 2, ref[lists[k], at, :], ref[lists[SPAN + k], at, :])

    return gather_columns(both, 0, depth, rows, cols, beside=-1)


def y_kernel(slots, depth, rows, cols, now, stepped, squares, lists, y_low, y_up):
    top = (depth + 1) * rows
    _, lane = row_and_lane(rows, cols)
    last_group = (lane >= LINKS * GROUP) & (lane < (LINKS + 1) * GROUP)
    for side, out in ((0, y_low), (1, y_up)):
        c, inward = (0, 1) if side == 0 else (cols - 1, -1)
        base = (2 + side) * SPAN
        rim, _ = gather_columns(
            lambda k, z: now[lists[base + k], pl.ds((z + 1) * rows, rows), :], c, depth, rows, cols
        )
        partial, inner = gather_columns(
            lambda k, z: stepped[lists[base + k], pl.ds((z + 1) * rows, rows), :], c, depth, rows, cols, beside=inward
        )
        for k in range(LINKS):
            for z, at in ((0, 0), (depth - 1, top)):
                place = GROUP * k + z
                frozen = spin(now[lists[base + k], pl.ds(at, rows), :], place - c)
                inner = inner + jnp.where(lane == place, frozen, 0.0)
        total = jnp.zeros((rows, cols), jnp.float32)
        for z in range(depth):
            place = LINKS * GROUP + z
            total = jnp.where(lane == place, spin(squares[pl.ds(z * rows, rows), :], place - c), total)
        inner = jnp.where(last_group, total - group_sum(partial * partial), inner)
        out[pl.ds(0, rows), :] = rim
        out[pl.ds(2 * rows, rows), :] = partial
        out[pl.ds(3 * rows, rows), :] = inner
    for i, ref in ((1, now), (4, stepped)):
        y_low[pl.ds(i * rows, rows), :], y_up[pl.ds(i * rows, rows), :] = gather_corners(ref, lists, depth, rows, cols)


def corner_kernel(rows, cols, y_low_own, y_up_own, y_low, y_up, c_low, c_up):
    for r, out in ((0, c_low), (rows - 1, c_up)):
        out[...] = jnp.zeros((rows, cols), jnp.float32)
        for side, own, got in ((0, y_low_own, y_low), (1, y_up_own, y_up)):
            out[pl.ds(side, 1), :] = own[pl.ds(2 * rows + r, 1), :]
            out[pl.ds(2 + side, 1), :] = got[pl.ds(r, 1), :]
            out[pl.ds(4 + side, 1), :] = got[pl.ds(rows + r, 1), :]


def y_faces(ref, tiles, lists, depth, rows, cols, replace):
    _, lane = row_and_lane(rows, cols)
    for k in range(LINKS):
        for side in range(2):
            c = 0 if side == 0 else cols - 1
            slot = lists[(2 + side) * SPAN + k]
            old = [ref[slot, pl.ds((z + 1) * rows, rows), :] for z in range(depth)]
            for z in range(depth):
                moved = spin(tiles[side], c - GROUP * k - z)
                new = jnp.where(lane == c, moved if replace else old[z] + moved, old[z])
                ref[slot, pl.ds((z + 1) * rows, rows), :] = new


def tile(ref, i, rows):
    return ref[pl.ds(i * rows, rows), :]


def middle_kernel(
    slots, depth, rows, cols,
    stepped_in, y_low_own, y_up_own, y_low, y_up, lists,
    now, later,
):
    top = (depth + 1) * rows
    for s in range(slots):
        for at in (0, top):
            later[s, pl.ds(at, rows), :] = now[s, pl.ds(at, rows), :]
    later[slots] = jnp.zeros(((depth + 2) * rows, cols), jnp.float32)
    pairs = ((y_low_own, y_low), (y_up_own, y_up))
    own_one = [tile(own, 2, rows) + RATE * tile(got, 0, rows) for own, got in pairs]
    one = [RATE * (tile(got, 2, rows) + RATE * tile(own, 0, rows)) for own, got in pairs]
    y_faces(now, own_one, lists, depth, rows, cols, True)
    step(now, later, slots, depth, rows, cols)
    y_faces(later, one, lists, depth, rows, cols, False)


def last_kernel(
    slots, depth, rows, cols,
    now, later_in, x_low_own, x_up_own, x_low, x_up, c_low, c_up, y_low_own, y_up_own, y_low, y_up, lists,
    later, result,
    last, x_one, x_own_one, x_two, sent,
):
    row, lane = row_and_lane(rows, cols)
    block = LINKS * depth
    last[slots] = jnp.zeros(((depth + 2) * rows, cols), jnp.float32)

    x_one[...] = jnp.zeros(x_one.shape, jnp.float32)
    x_own_one[...] = jnp.zeros(x_own_one.shape, jnp.float32)
    tall_row, tall_lane = row_and_lane(GROUP, cols)
    low_lane, high_lane = tall_lane[:depth] == 0, tall_lane[:depth] == cols - 1
    for face, own, got, corner in ((0, x_low_own, x_low, c_low), (1, x_up_own, x_up, c_up)):
        r, inner_r = (0, 1) if face == 0 else (rows - 1, rows - 2)
        rim_rows = pl.ds(rows + r, depth, stride=rows)
        total = got[pl.ds(3 * block, depth), :]
        ones, own_ones = [], []
        change = jnp.zeros((depth, cols), jnp.float32)
        for k in range(LINKS):
            partial = own[pl.ds(block + k * depth, depth), :]
            one = got[pl.ds(block + k * depth, depth), :] + RATE * own[pl.ds(k * depth, depth), :]
            own_one = partial + RATE * got[pl.ds(k * depth, depth), :]
            total = total + one * one
            change = change + (own_one * own_one - partial * partial)
            x_one[face, pl.ds(k * GROUP + 1, depth), :] = one
            x_own_one[face, pl.ds(k * GROUP + 1, depth), :] = own_one
            ones.append(one)
            own_ones.append(own_one)
        for side in range(2):
            c = 0 if side == 0 else cols - 1
            term = RATE * corner[pl.ds(2 + side, 1), :]
            term = group_sum(term * (2.0 * corner[pl.ds(side, 1), :] + term))
            spread = jnp.where(tall_row == tall_lane, jnp.broadcast_to(term, (GROUP, cols)), 0.0)
            column = jnp.sum(spread, axis=1, keepdims=True)
            total = total + jnp.where(tall_lane == c, column, 0.0)[:depth]

        scaled = 0.15 * change
        own_total = change
        for s in range(slots):
            v = now[s, rim_rows, :]
            own_total = own_total + v * v
            later[s, rim_rows, :] = later[s, rim_rows, :] - scaled * v

        def rim_step(padded, k, one, factor, outer):
            z_sum = padded[face, pl.ds(k * GROUP, depth), :] + padded[face, pl.ds(k * GROUP + 2, depth), :]
            y_sum = jnp.where(low_lane, 0.0, pltpu.roll(one, 1, 1)) + jnp.where(
                high_lane, 0.0, pltpu.roll(one, cols - 1, 1)
            )
            return RATE * (one * (factor + one * one) + (outer + (z_sum + y_sum)))

        factor, own_factor = 4.5 - 1.5 * total, 4.5 - 1.5 * own_total
        for k in range(LINKS):
            inner = pl.ds(2 * block + k * depth, depth)
            x_two[face, pl.ds(k * GROUP, depth), :] = rim_step(x_one, k, ones[k], factor, got[inner, :] + own_ones[k])
            own_two = rim_step(x_own_one, k, own_ones[k], own_factor, own[inner, :] + ones[k])
            slot = lists[face * SPAN + k]
            inner_rows = pl.ds(rows + inner_r, depth, stride=rows)
            beside = later[slot, inner_rows, :] + RATE * RATE * got[pl.ds(k * depth, depth), :]
            later[slot, rim_rows, :] = own_two
            later[slot, inner_rows, :] = beside

    y_two = []
    for side, own, got in ((0, y_low_own, y_low), (1, y_up_own, y_up)):
        own_one = tile(own, 2, rows) + RATE * tile(got, 0, rows)
        one = tile(got, 2, rows) + RATE * tile(own, 0, rows)
        inner = tile(got, 3, rows)
        low = jnp.broadcast_to(c_low[pl.ds(4 + side, 1), :], (rows, cols))
        high = jnp.broadcast_to(c_up[pl.ds(4 + side, 1), :], (rows, cols))
        term = RATE * jnp.where(row == 0, low, jnp.where(row == rows - 1, high, 0.0))
        rest = jnp.where((lane >= LINKS * GROUP) & (lane < (LINKS + 1) * GROUP), inner, 0.0)
        total = group_sum((one * one + rest) + term * (2.0 * tile(got, 4, rows) + term))
        x_sum = jnp.where(row == 0, 0.0, pltpu.roll(one, 1, 0)) + jnp.where(
            row == rows - 1, 0.0, pltpu.roll(one, rows - 1, 0)
        )
        z_sum = spin(one, 1) + spin(one, -1)
        two = RATE * (one * ((4.5 - 1.5 * total) + one * one) + ((inner + own_one) + (x_sum + z_sum)))
        y_two.append(RATE * two)

    step(later, last, slots, depth, rows, cols)
    for face in range(2):
        rim_rows = pl.ds(rows + (0 if face == 0 else rows - 1), depth, stride=rows)
        old = [last[lists[face * SPAN + k], rim_rows, :] for k in range(LINKS)]
        for k in range(LINKS):
            last[lists[face * SPAN + k], rim_rows, :] = old[k] + RATE * x_two[face, pl.ds(k * GROUP, depth), :]
    y_faces(last, y_two, lists, depth, rows, cols, False)
    copy = pltpu.make_async_copy(last.at[pl.ds(0, slots), pl.ds(rows, depth * rows), :], result, sent)
    copy.start()
    copy.wait()


def shifted(block, axis, distance):
    size = lax.axis_size(axis)
    return lax.ppermute(block, axis, [((i - distance) % size, i) for i in range(size)])


def on_device(order_params, grain_ids, channel_maps, zplanes):
    slots, depth, rows, cols = order_params.shape
    f32 = jnp.float32
    shape = jax.ShapeDtypeStruct
    padded = pltpu.VMEM((slots + 1, (depth + 2) * rows, cols), f32)
    x_pack = shape((-(-(3 * LINKS * depth + depth) // rows) * rows, cols), f32)
    y_pack = shape((5 * rows, cols), f32)
    corner_pack = shape((rows, cols), f32)
    vmem = pl.BlockSpec(memory_space=pltpu.VMEM)
    smem = pl.BlockSpec(memory_space=pltpu.SMEM)
    hbm = pl.BlockSpec(memory_space=pltpu.HBM)
    params = pltpu.CompilerParams(vmem_limit_bytes=24 * 1024 * 1024)
    field = order_params.reshape(slots, depth * rows, cols)
    sizes = (slots, depth, rows, cols)

    now, stepped, squares, x_low, x_up, lists = pl.pallas_call(
        functools.partial(first_kernel, *sizes),
        out_shape=[
            padded, padded, pltpu.VMEM((depth * rows, cols), f32), x_pack, x_pack, shape((4 * SPAN,), jnp.int32)
        ],
        in_specs=[hbm] * 4,
        out_specs=[vmem] * 5 + [smem],
        scratch_shapes=[
            pltpu.VMEM(zplanes.shape, jnp.int32),
            pltpu.SMEM(grain_ids.shape, jnp.int32),
            pltpu.SMEM(channel_maps.shape, jnp.int32),
            pltpu.SMEM((2 * (slots + 1),), jnp.int32),
            pltpu.SemaphoreType.DMA((4,)),
        ],
        compiler_params=params,
        name="first_step",
    )(*(pltpu.with_memory_space_constraint(x, pltpu.HBM) for x in (field, zplanes, grain_ids, channel_maps)))

    from_up = shifted(x_low, "gx", -1)
    from_low = shifted(x_up, "gx", 1)

    y_low, y_up = pl.pallas_call(
        functools.partial(y_kernel, *sizes),
        out_shape=[y_pack, y_pack],
        in_specs=[vmem] * 3 + [smem],
        out_specs=[vmem] * 2,
        compiler_params=params,
        name="y_rims",
    )(now, stepped, squares, lists)

    from_right = shifted(y_low, "gy", -1)
    from_left = shifted(y_up, "gy", 1)

    c_low, c_up = pl.pallas_call(
        functools.partial(corner_kernel, rows, cols),
        out_shape=[corner_pack, corner_pack],
        in_specs=[vmem] * 4,
        out_specs=[vmem] * 2,
        compiler_params=params,
        name="corners",
    )(y_low, y_up, from_left, from_right)

    corner_from_up = shifted(c_low, "gx", -1)
    corner_from_low = shifted(c_up, "gx", 1)

    fixed, later = pl.pallas_call(
        functools.partial(middle_kernel, *sizes),
        out_shape=[padded, padded],
        in_specs=[vmem] * 5 + [smem],
        out_specs=[vmem] * 2,
        input_output_aliases={0: 0},
        compiler_params=params,
        name="second_step",
    )(stepped, y_low, y_up, from_left, from_right, lists)

    _, result = pl.pallas_call(
        functools.partial(last_kernel, *sizes),
        out_shape=[padded, shape(field.shape, f32)],
        in_specs=[vmem] * 12 + [smem],
        out_specs=[vmem, hbm],
        scratch_shapes=[padded]
        + [pltpu.VMEM((2, LINKS * GROUP, cols), f32)] * 3
        + [pltpu.SemaphoreType.DMA],
        input_output_aliases={1: 0},
        compiler_params=params,
        name="third_step",
    )(
        fixed, later, x_low, x_up, from_low, from_up, corner_from_low, corner_from_up,
        y_low, y_up, from_left, from_right, lists,
    )
    return result.reshape(order_params.shape)


def solution(mesh):
    in_specs = (
        P(None, None, "gx", "gy"),
        P("gx", "gy", None),
        P("gx", "gy", None, None),
        P(None, "gx", "gy"),
    )
    return jax.shard_map(
        on_device, mesh=mesh, in_specs=in_specs, out_specs=P(None, None, "gx", "gy"), check_vma=False
    )
```

```python
import functools

import jax
import jax.numpy as jnp
from jax import lax
from jax.experimental import pallas as pl
from jax.experimental.pallas import tpu as pltpu
from jax.sharding import PartitionSpec as P


LINKS = 6
SPAN = 8
GROUP = 16
RATE = 0.1
UNROLL = 4


def row_and_lane(rows, cols):
    row = lax.broadcasted_iota(jnp.int32, (rows, cols), 0)
    lane = lax.broadcasted_iota(jnp.int32, (rows, cols), 1)
    return row, lane


def spin(tile, amount):
    cols = tile.shape[1]
    amount = amount % cols
    return tile if amount == 0 else pltpu.roll(tile, amount, 1)


def group_sum(tile):
    shift = GROUP
    while shift < tile.shape[1]:
        tile = tile + spin(tile, shift)
        shift *= 2
    return tile


def step(src, dst, slots, depth, rows, cols, squares=None, wait=None):
    row, lane = row_and_lane(rows, cols)
    first_row, last_row = row == 0, row == rows - 1
    first_lane, last_lane = lane == 0, lane == cols - 1

    def add(parts, s, term):
        parts[s % 4] = term if parts[s % 4] is None else parts[s % 4] + term

    def total(parts):
        return (parts[0] + parts[1]) + (parts[2] + parts[3])

    def at(z):
        return pl.ds(pl.multiple_of((z + 1) * rows, rows), rows)

    def layer(z, factor):
        following, parts = [None] * 4, [None] * 4
        for s in range(slots):
            v, below, above = src[s, at(z), :], src[s, at(z - 1), :], src[s, at(z + 1), :]
            add(following, s, above * above)
            x_sum = jnp.where(first_row, 0.0, pltpu.roll(v, 1, 0)) + jnp.where(
                last_row, 0.0, pltpu.roll(v, rows - 1, 0)
            )
            y_sum = jnp.where(first_lane, 0.0, pltpu.roll(v, 1, 1)) + jnp.where(
                last_lane, 0.0, pltpu.roll(v, cols - 1, 1)
            )
            new = RATE * (v * (factor + v * v) + ((x_sum + y_sum) + (below + above)))
            dst[s, at(z), :] = new
            if squares is not None:
                add(parts, s, new * new)
        if squares is not None:
            squares[pl.ds(pl.multiple_of(z * rows, rows), rows), :] = total(parts)
        return 4.5 - 1.5 * total(following)

    def layers(i, factor):
        if wait is not None:
            pl.when(i + 1 < depth // UNROLL)(lambda: wait(i + 1))
        for j in range(UNROLL):
            factor = layer(i * UNROLL + j, factor)
        return factor

    first = [None] * 4
    for s in range(slots):
        v = src[s, at(0), :]
        add(first, s, v * v)
    lax.fori_loop(0, depth // UNROLL, layers, 4.5 - 1.5 * total(first))


def gather_columns(tile_of, c, depth, rows, cols, beside=0):
    _, lane = row_and_lane(rows, cols)
    result, other = jnp.zeros((rows, cols), jnp.float32), jnp.zeros((rows, cols), jnp.float32)
    for k in range(LINKS):
        near, far = jnp.zeros_like(result), jnp.zeros_like(other)
        for z in range(depth):
            place = GROUP * k + z
            moved = spin(tile_of(k, z), place - c)
            near = jnp.where(lane == place, moved, near)
            if beside:
                far = jnp.where(lane == (place + beside) % cols, moved, far)
        result = result + near
        other = other + far
    return result, spin(other, -beside)


def first_kernel(
    slots, depth, rows, cols,
    field, planes, grains, maps,
    now, stepped, squares, x_up, lists,
    planes_in, grains_in, maps_in, inverse, arrived,
):
    copies = [
        pltpu.make_async_copy(maps, maps_in, arrived.at[0]),
        pltpu.make_async_copy(grains, grains_in, arrived.at[1]),
        pltpu.make_async_copy(planes, planes_in, arrived.at[2]),
    ]
    part = UNROLL * rows

    def field_part(i):
        to = pl.ds(pl.multiple_of(i * part + rows, rows), part)
        source = field.at[:, pl.ds(pl.multiple_of(i * part, rows), part), :]
        return pltpu.make_async_copy(source, now.at[pl.ds(0, slots), to, :], arrived.at[3 + i])

    for copy in copies:
        copy.start()
    for i in range(depth // UNROLL):
        field_part(i).start()
    for ref in (now, stepped):
        ref[slots] = jnp.zeros(((depth + 2) * rows, cols), jnp.float32)
    for face in range(4):
        for place in range(SPAN):
            lists[face * SPAN + place] = slots
    for t in range(slots + 1):
        inverse[t] = slots
        inverse[slots + 1 + t] = slots

    copies[0].wait()
    for s in range(slots):
        for face in (0, 2):
            partner = maps_in[0, 0, face, s]
            inverse[face // 2 * (slots + 1) + jnp.where(partner >= 0, partner, slots)] = s
    counts = [jnp.int32(face * SPAN) for face in range(4)]
    for s in range(slots):
        partners = [maps_in[0, 0, face, s] for face in range(4)]
        best = jnp.maximum(jnp.maximum(partners[0], partners[1]), jnp.maximum(partners[2], partners[3]))
        lists[4 * SPAN + s] = (best >= 0).astype(jnp.int32)
        for face in range(4):
            if face in (1, 3):
                valid = partners[face] >= 0
                slot = jnp.where(valid, s, slots)
            else:
                slot = inverse[face // 2 * (slots + 1) + s]
                valid = slot < slots
            lists[counts[face]] = slot
            counts[face] = counts[face] + valid.astype(jnp.int32)

    top = (depth + 1) * rows
    copies[1].wait()
    copies[2].wait()
    for s in range(slots):
        grain = grains_in[0, 0, s]
        below = jnp.where(planes_in[0] == grain, 1.0, 0.0)
        above = jnp.where(planes_in[1] == grain, 1.0, 0.0)
        for ref in (now, stepped):
            ref[s, pl.ds(0, rows), :] = below
            ref[s, pl.ds(top, rows), :] = above
    field_part(0).wait()

    step(now, stepped, slots, depth, rows, cols, squares, lambda i: field_part(i).wait())
    pack_x(1, now, stepped, squares, lists, x_up, depth, rows, cols)


def x_low_kernel(depth, rows, cols, now, stepped, squares, lists, x_low):
    pack_x(0, now, stepped, squares, lists, x_low, depth, rows, cols)


def pack_x(face, now, stepped, squares, lists, out, depth, rows, cols):
    block = LINKS * depth
    edge_row, edge_lane = row_and_lane(depth, cols)
    top = (depth + 1) * rows
    r, inner_r = (0, 1) if face == 0 else (rows - 1, rows - 2)
    rim_rows = pl.ds(rows + r, depth, stride=rows)
    rest = squares[pl.ds(r, depth, stride=rows), :]
    for k in range(LINKS):
        slot = lists[face * SPAN + k]
        partial = stepped[slot, rim_rows, :]
        inner = stepped[slot, pl.ds(rows + inner_r, depth, stride=rows), :]
        below = jnp.broadcast_to(now[slot, pl.ds(r, 1), :], (depth, cols))
        above = jnp.broadcast_to(now[slot, pl.ds(top + r, 1), :], (depth, cols))
        inner = inner + jnp.where(edge_row == 0, below, jnp.where(edge_row == depth - 1, above, 0.0))
        rest = rest - partial * partial
        out[pl.ds(k * depth, depth), :] = now[slot, rim_rows, :]
        out[pl.ds(block + k * depth, depth), :] = partial
        out[pl.ds(2 * block + k * depth, depth), :] = inner
    out[pl.ds(3 * block + depth, depth), :] = rest
    corners = jnp.zeros((depth, cols), jnp.float32)
    for i, ref in enumerate((stepped, now)):
        for side in range(2):
            for k in range(LINKS):
                place = (2 * i + side) * LINKS + k
                moved = spin(ref[lists[(2 + side) * SPAN + k], rim_rows, :], place - side * (cols - 1))
                corners = jnp.where(edge_lane == place, moved, corners)
    out[pl.ds(3 * block, depth), :] = corners
    end = 3 * block + 2 * depth
    if out.shape[0] > end:
        out[pl.ds(end, out.shape[0] - end), :] = jnp.zeros((out.shape[0] - end, cols), jnp.float32)


def y_kernel(slots, depth, rows, cols, now, stepped, squares, lists, y_low, y_up):
    top = (depth + 1) * rows
    _, lane = row_and_lane(rows, cols)
    for side, out in ((0, y_low), (1, y_up)):
        c, inward = (0, 1) if side == 0 else (cols - 1, -1)
        base = (2 + side) * SPAN
        rim, _ = gather_columns(
            lambda k, z: now[lists[base + k], pl.ds((z + 1) * rows, rows), :], c, depth, rows, cols
        )
        partial, inner = gather_columns(
            lambda k, z: stepped[lists[base + k], pl.ds((z + 1) * rows, rows), :], c, depth, rows, cols, beside=inward
        )
        for k in range(LINKS):
            for z, at in ((0, 0), (depth - 1, top)):
                place = GROUP * k + z
                frozen = spin(now[lists[base + k], pl.ds(at, rows), :], place - c)
                inner = inner + jnp.where(lane == place, frozen, 0.0)
        total = jnp.zeros((rows, cols), jnp.float32)
        for z in range(depth):
            place = LINKS * GROUP + z
            total = jnp.where(lane == place, spin(tile(squares, z, rows), place - c), total)
        inner = jnp.where(in_last_group(lane), total - group_sum(partial * partial), inner)
        out[pl.ds(0, rows), :] = rim
        out[pl.ds(rows, rows), :] = partial
        out[pl.ds(2 * rows, rows), :] = inner


def in_last_group(lane):
    return (lane >= LINKS * GROUP) & (lane < (LINKS + 1) * GROUP)


def tile(ref, i, rows):
    return ref[pl.ds(i * rows, rows), :]


def y_faces(ref, tiles, lists, depth, rows, cols, replace=False, done=None):
    _, lane = row_and_lane(rows, cols)
    for k in range(LINKS):
        for side in range(2):
            c = side * (cols - 1)
            slot = lists[(2 + side) * SPAN + k]
            ats = [pl.ds((z + 1) * rows, rows) for z in range(depth)]
            old = [ref[slot, at, :] for at in ats]
            for z in range(depth):
                moved = spin(tiles[side], c - GROUP * k - z)
                ref[slot, ats[z], :] = jnp.where(lane == c, moved if replace else old[z] + moved, old[z])
            if done is not None:
                done(slot)


def second_kernel(
    slots, depth, rows, cols, stepped_in, y_low_own, y_up_own, y_low, y_up, lists, now, later
):
    for s in range(slots):
        for at in (0, (depth + 1) * rows):
            later[s, pl.ds(at, rows), :] = now[s, pl.ds(at, rows), :]
    later[slots] = jnp.zeros(((depth + 2) * rows, cols), jnp.float32)
    pairs = ((y_low_own, y_low), (y_up_own, y_up))
    own_one = [tile(own, 1, rows) + RATE * tile(got, 0, rows) for own, got in pairs]
    one = [RATE * (tile(got, 1, rows) + RATE * tile(own, 0, rows)) for own, got in pairs]
    y_faces(now, own_one, lists, depth, rows, cols, replace=True)
    step(now, later, slots, depth, rows, cols)
    y_faces(later, one, lists, depth, rows, cols)


def x_rims(own, got, k, depth):
    zero, one = pl.ds(k * depth, depth), pl.ds((LINKS + k) * depth, depth)
    return own[one, :] + RATE * got[zero, :], got[one, :] + RATE * own[zero, :]


def change_kernel(depth, cols, own, got, before, out):
    change = jnp.zeros((depth, cols), jnp.float32)
    for k in range(LINKS):
        own_one, _ = x_rims(own, got, k, depth)
        partial = own[pl.ds((LINKS + k) * depth, depth), :]
        change = change + (own_one * own_one - partial * partial)
    out[pl.ds(0, depth), :] = change
    out[pl.ds(depth, depth), :] = got[pl.ds(3 * LINKS * depth, depth), :]


def both_changes_kernel(depth, cols, own, got, before, out):
    out[pl.ds(0, 2 * depth), :] = before[...]
    change_kernel(depth, cols, own, got, None, out.at[pl.ds(2 * depth, 2 * depth), :])


def x_rim_step(padded, face, k, one, factor, outer, depth, cols):
    _, lane = row_and_lane(depth, cols)
    z_sum = padded[face, pl.ds(k * GROUP, depth), :] + padded[face, pl.ds(k * GROUP + 2, depth), :]
    y_sum = jnp.where(lane == 0, 0.0, pltpu.roll(one, 1, 1)) + jnp.where(
        lane == cols - 1, 0.0, pltpu.roll(one, cols - 1, 1)
    )
    return RATE * (one * (factor + one * one) + (outer + (z_sum + y_sum)))


def y_rim_step(one, factor, outer):
    rows, cols = one.shape
    row, _ = row_and_lane(rows, cols)
    x_sum = jnp.where(row == 0, 0.0, pltpu.roll(one, 1, 0)) + jnp.where(
        row == rows - 1, 0.0, pltpu.roll(one, rows - 1, 0)
    )
    z_sum = spin(one, 1) + spin(one, -1)
    return RATE * (one * (factor + one * one) + (outer + (x_sum + z_sum)))


def third_kernel(
    slots, depth, rows, cols,
    now, later_in, x_low_own, x_up_own, x_low, x_up, changes, lists,
    later, last,
    x_own_one,
):
    last[slots] = jnp.zeros(((depth + 2) * rows, cols), jnp.float32)
    x_own_one[...] = jnp.zeros(x_own_one.shape, jnp.float32)
    for face, own, got in ((0, x_low_own, x_low), (1, x_up_own, x_up)):
        r, inner_r = (0, 1) if face == 0 else (rows - 1, rows - 2)
        rim_rows = pl.ds(rows + r, depth, stride=rows)
        inner_rows = pl.ds(rows + inner_r, depth, stride=rows)
        rims = [x_rims(own, got, k, depth) for k in range(LINKS)]
        for k in range(LINKS):
            x_own_one[face, pl.ds(k * GROUP + 1, depth), :] = rims[k][0]

        change = changes[pl.ds(2 * face * depth, depth), :]
        scaled = 0.15 * change
        parts = [change, None, None, None]
        for first in range(0, slots, 4):
            rim = [now[first + i, rim_rows, :] for i in range(4)]
            old = [later[first + i, rim_rows, :] for i in range(4)]
            for i in range(4):
                parts[i] = rim[i] * rim[i] if parts[i] is None else parts[i] + rim[i] * rim[i]
                later[first + i, rim_rows, :] = old[i] - scaled * rim[i]
        factor = 4.5 - 1.5 * ((parts[0] + parts[1]) + (parts[2] + parts[3]))

        beside = [later[lists[face * SPAN + k], inner_rows, :] for k in range(LINKS)]
        two = []
        for k in range(LINKS):
            outer = own[pl.ds((2 * LINKS + k) * depth, depth), :] + rims[k][1]
            two.append(x_rim_step(x_own_one, face, k, rims[k][0], factor, outer, depth, cols))
        for k in range(LINKS):
            slot = lists[face * SPAN + k]
            later[slot, rim_rows, :] = two[k]
            later[slot, inner_rows, :] = beside[k] + RATE * RATE * got[pl.ds(k * depth, depth), :]

    step(later, last, slots, depth, rows, cols)


def last_kernel(
    slots, depth, rows, cols,
    last_in, x_low_own, x_up_own, x_low, x_up, y_low_own, y_up_own, y_low, y_up, from_left, from_right,
    lists,
    last, result,
    x_one, sent,
):
    whole = last.at[pl.ds(0, slots), pl.ds(rows, depth * rows), :]

    def send(slot):
        pltpu.make_async_copy(last.at[slot, pl.ds(rows, depth * rows), :], result.at[slot], sent).start()

    def send_linked(slot):
        pl.when(slot < slots)(lambda: send(slot))

    for s in range(slots):
        pl.when(lists[4 * SPAN + s] == 0)(functools.partial(send, s))

    row, lane = row_and_lane(rows, cols)
    _, flat_lane = row_and_lane(depth, cols)
    tall_row, tall_lane = row_and_lane(GROUP, cols)
    block = LINKS * depth
    passed_on = (from_left, from_right)
    x_one[...] = jnp.zeros(x_one.shape, jnp.float32)
    for face, own, got in ((0, x_low_own, x_low), (1, x_up_own, x_up)):
        rims = [x_rims(own, got, k, depth) for k in range(LINKS)]
        total = got[pl.ds(3 * block + depth, depth), :]
        for k in range(LINKS):
            total = total + rims[k][1] * rims[k][1]
            x_one[face, pl.ds(k * GROUP + 1, depth), :] = rims[k][1]
        corners = got[pl.ds(3 * block, depth), :]
        for side in range(2):
            place = side * LINKS
            came_from = (3 - side) * LINKS
            term = RATE * spin(passed_on[side][pl.ds((2 * face + 1) * depth, depth), :], place - came_from)
            term = term * (2.0 * corners + term)
            term = jnp.where((flat_lane >= place) & (flat_lane < place + LINKS), term, 0.0)
            column = jnp.sum(term, axis=1, keepdims=True)
            total = total + jnp.where(flat_lane == side * (cols - 1), column, 0.0)
        factor = 4.5 - 1.5 * total
        rim_rows = pl.ds(rows + (0 if face == 0 else rows - 1), depth, stride=rows)
        old = [last[lists[face * SPAN + k], rim_rows, :] for k in range(LINKS)]
        for k in range(LINKS):
            outer = got[pl.ds(2 * block + k * depth, depth), :] + rims[k][0]
            two = x_rim_step(x_one, face, k, rims[k][1], factor, outer, depth, cols)
            last[lists[face * SPAN + k], rim_rows, :] = old[k] + RATE * two
        for k in range(LINKS):
            send_linked(lists[face * SPAN + k])

    twos = []
    for side, own, got in ((0, y_low_own, y_low), (1, y_up_own, y_up)):
        c = side * (cols - 1)
        own_one = tile(own, 1, rows) + RATE * tile(got, 0, rows)
        one = tile(got, 1, rows) + RATE * tile(own, 0, rows)
        inner = tile(got, 2, rows)
        squares = one * one + jnp.where(in_last_group(lane), inner, 0.0)
        for face in range(2):
            change = passed_on[side][pl.ds(2 * face * depth, depth), :]
            column = jnp.sum(jnp.where(flat_lane == cols - 1 - c, change, 0.0), axis=1, keepdims=True)
            line = jnp.sum(jnp.where(tall_row == tall_lane, 1.0, 0.0)[:depth] * column, axis=0, keepdims=True)
            at_row = row == (0 if face == 0 else rows - 1)
            squares = squares + jnp.where(at_row, jnp.broadcast_to(line, (rows, cols)), 0.0)
        factor = 4.5 - 1.5 * group_sum(squares)
        twos.append(RATE * y_rim_step(one, factor, inner + own_one))
    y_faces(last, twos, lists, depth, rows, cols, done=send_linked)
    pltpu.make_async_copy(whole, result, sent).wait()


def shifted(block, axis, distance):
    size = lax.axis_size(axis)
    return lax.ppermute(block, axis, [((i - distance) % size, i) for i in range(size)])


def on_device(order_params, grain_ids, channel_maps, zplanes):
    slots, depth, rows, cols = order_params.shape
    f32 = jnp.float32
    shape = jax.ShapeDtypeStruct
    padded = pltpu.VMEM((slots + 1, (depth + 2) * rows, cols), f32)
    planes = pltpu.VMEM((depth * rows, cols), f32)
    x_pack = shape((-(-(3 * LINKS + 2) * depth // rows) * rows, cols), f32)
    y_pack = shape((3 * rows, cols), f32)
    rims = pltpu.VMEM((2, LINKS * GROUP, cols), f32)
    vmem = pl.BlockSpec(memory_space=pltpu.VMEM)
    smem = pl.BlockSpec(memory_space=pltpu.SMEM)
    hbm = pl.BlockSpec(memory_space=pltpu.HBM)
    params = pltpu.CompilerParams(vmem_limit_bytes=24 * 1024 * 1024)
    field = order_params.reshape(slots, depth * rows, cols)
    sizes = (slots, depth, rows, cols)
    work = pl.CostEstimate(flops=20 * field.size, bytes_accessed=2 * 4 * field.size, transcendentals=0)

    now, stepped, squares, x_up, lists = pl.pallas_call(
        functools.partial(first_kernel, *sizes),
        out_shape=[padded, padded, planes, x_pack, shape((4 * SPAN + slots,), jnp.int32)],
        in_specs=[hbm] * 4,
        out_specs=[vmem] * 4 + [smem],
        scratch_shapes=[
            pltpu.VMEM(zplanes.shape, jnp.int32),
            pltpu.SMEM(grain_ids.shape, jnp.int32),
            pltpu.SMEM(channel_maps.shape, jnp.int32),
            pltpu.SMEM((2 * (slots + 1),), jnp.int32),
            pltpu.SemaphoreType.DMA((3 + depth // UNROLL,)),
        ],
        compiler_params=params,
        name="first_step",
    )(*(pltpu.with_memory_space_constraint(x, pltpu.HBM) for x in (field, zplanes, grain_ids, channel_maps)))

    from_low = shifted(x_up, "gx", 1)

    x_low = pl.pallas_call(
        functools.partial(x_low_kernel, depth, rows, cols),
        out_shape=x_pack,
        in_specs=[vmem] * 3 + [smem],
        out_specs=vmem,
        compiler_params=params,
        cost_estimate=work,
        name="x_low_rims",
    )(now, stepped, squares, lists)

    from_up = shifted(x_low, "gx", -1)

    y_low, y_up = pl.pallas_call(
        functools.partial(y_kernel, *sizes),
        out_shape=[y_pack, y_pack],
        in_specs=[vmem] * 3 + [smem],
        out_specs=[vmem] * 2,
        compiler_params=params,
        cost_estimate=work,
        name="y_rims",
    )(now, stepped, squares, lists)

    from_right = shifted(y_low, "gy", -1)
    from_left = shifted(y_up, "gy", 1)

    fixed, later = pl.pallas_call(
        functools.partial(second_kernel, *sizes),
        out_shape=[padded, padded],
        in_specs=[vmem] * 5 + [smem],
        out_specs=[vmem] * 2,
        input_output_aliases={0: 0},
        compiler_params=params,
        cost_estimate=work,
        name="second_step",
    )(stepped, y_low, y_up, from_left, from_right, lists)

    changes = later
    for body, own, got, name in (
        (change_kernel, x_low, from_low, "corners_low"),
        (both_changes_kernel, x_up, from_up, "corners_up"),
    ):
        changes = pl.pallas_call(
            functools.partial(body, depth, cols),
            out_shape=shape(((2 if body is change_kernel else 4) * depth, cols), f32),
            in_specs=[vmem] * 3,
            out_specs=vmem,
            compiler_params=params,
            name=name,
        )(own, got, changes)

    changes_from_right = shifted(changes, "gy", -1)
    changes_from_left = shifted(changes, "gy", 1)

    _, last = pl.pallas_call(
        functools.partial(third_kernel, *sizes),
        out_shape=[padded, padded],
        in_specs=[vmem] * 7 + [smem],
        out_specs=[vmem] * 2,
        scratch_shapes=[rims],
        input_output_aliases={1: 0},
        compiler_params=params,
        name="third_step",
    )(
        fixed, later, x_low, x_up, from_low, from_up, changes, lists,
    )

    _, result = pl.pallas_call(
        functools.partial(last_kernel, *sizes),
        out_shape=[padded, shape(field.shape, f32)],
        in_specs=[vmem] * 11 + [smem],
        out_specs=[vmem, hbm],
        scratch_shapes=[rims, pltpu.SemaphoreType.DMA],
        input_output_aliases={0: 0},
        compiler_params=params,
        name="last_rims",
    )(
        last, x_low, x_up, from_low, from_up,
        y_low, y_up, from_left, from_right, changes_from_left, changes_from_right, lists,
    )
    return result.reshape(order_params.shape)


def solution(mesh):
    in_specs = (
        P(None, None, "gx", "gy"),
        P("gx", "gy", None),
        P("gx", "gy", None, None),
        P(None, "gx", "gy"),
    )
    return jax.shard_map(
        on_device, mesh=mesh, in_specs=in_specs, out_specs=P(None, None, "gx", "gy"), check_vma=False
    )
```

```python
import functools

import jax
import jax.numpy as jnp
from jax import lax
from jax.experimental import pallas as pl
from jax.experimental.pallas import tpu as pltpu
from jax.sharding import PartitionSpec as P


LINKS = 6
SPAN = 8
GROUP = 16
RATE = 0.1
UNROLL = 4


def row_and_lane(rows, cols):
    row = lax.broadcasted_iota(jnp.int32, (rows, cols), 0)
    lane = lax.broadcasted_iota(jnp.int32, (rows, cols), 1)
    return row, lane


def spin(tile, amount):
    cols = tile.shape[1]
    amount = amount % cols
    return tile if amount == 0 else pltpu.roll(tile, amount, 1)


def group_sum(tile):
    shift = GROUP
    while shift < tile.shape[1]:
        tile = tile + spin(tile, shift)
        shift *= 2
    return tile


def step(src, dst, slots, depth, rows, cols, squares=None, wait=None):
    row, lane = row_and_lane(rows, cols)
    first_row, last_row = row == 0, row == rows - 1
    first_lane, last_lane = lane == 0, lane == cols - 1

    def add(parts, s, term):
        parts[s % 4] = term if parts[s % 4] is None else parts[s % 4] + term

    def total(parts):
        return (parts[0] + parts[1]) + (parts[2] + parts[3])

    def at(z):
        return pl.ds(pl.multiple_of((z + 1) * rows, rows), rows)

    def layer(z, factor):
        following, parts = [None] * 4, [None] * 4
        for s in range(slots):
            v, below, above = src[s, at(z), :], src[s, at(z - 1), :], src[s, at(z + 1), :]
            add(following, s, above * above)
            x_sum = jnp.where(first_row, 0.0, pltpu.roll(v, 1, 0)) + jnp.where(
                last_row, 0.0, pltpu.roll(v, rows - 1, 0)
            )
            y_sum = jnp.where(first_lane, 0.0, pltpu.roll(v, 1, 1)) + jnp.where(
                last_lane, 0.0, pltpu.roll(v, cols - 1, 1)
            )
            new = RATE * (v * (factor + v * v) + ((x_sum + y_sum) + (below + above)))
            dst[s, at(z), :] = new
            if squares is not None:
                add(parts, s, new * new)
        if squares is not None:
            squares[pl.ds(pl.multiple_of(z * rows, rows), rows), :] = total(parts)
        return 4.5 - 1.5 * total(following)

    def layers(i, factor):
        if wait is not None:
            pl.when(i + 1 < depth // UNROLL)(lambda: wait(i + 1))
        for j in range(UNROLL):
            factor = layer(i * UNROLL + j, factor)
        return factor

    first = [None] * 4
    for s in range(slots):
        v = src[s, at(0), :]
        add(first, s, v * v)
    lax.fori_loop(0, depth // UNROLL, layers, 4.5 - 1.5 * total(first))


def gather_columns(ref, linked, c, depth, rows, cols, beside=0):
    _, lane = row_and_lane(rows, cols)
    result, other = jnp.zeros((rows, cols), jnp.float32), jnp.zeros((rows, cols), jnp.float32)
    for k in range(LINKS):
        slot = linked[k]
        near, far = jnp.zeros_like(result), jnp.zeros_like(other)
        for z in range(depth):
            place = GROUP * k + z
            moved = spin(ref[slot, pl.ds((z + 1) * rows, rows), :], place - c)
            near = jnp.where(lane == place, moved, near)
            if beside:
                far = jnp.where(lane == (place + beside) % cols, moved, far)
        result = result + near
        other = other + far
    return result, spin(other, -beside)


def x_rows(part, k, depth):
    return pl.ds(part * LINKS * depth + k, depth, stride=LINKS)


def first_kernel(
    slots, depth, rows, cols,
    field, planes, grains, maps,
    now, stepped, squares, x_low, x_up, lists,
    planes_in, grains_in, maps_in, inverse, arrived,
):
    copies = [
        pltpu.make_async_copy(maps, maps_in, arrived.at[0]),
        pltpu.make_async_copy(grains, grains_in, arrived.at[1]),
        pltpu.make_async_copy(planes, planes_in, arrived.at[2]),
    ]
    part = UNROLL * rows

    def field_part(i):
        to = pl.ds(pl.multiple_of(i * part + rows, rows), part)
        source = field.at[:, pl.ds(pl.multiple_of(i * part, rows), part), :]
        return pltpu.make_async_copy(source, now.at[pl.ds(0, slots), to, :], arrived.at[3 + i])

    for copy in copies:
        copy.start()
    for i in range(depth // UNROLL):
        field_part(i).start()
    for ref in (now, stepped):
        ref[slots] = jnp.zeros(((depth + 2) * rows, cols), jnp.float32)
    for face in range(4):
        for place in range(SPAN):
            lists[face * SPAN + place] = slots
    for t in range(slots + 1):
        inverse[t] = slots
        inverse[slots + 1 + t] = slots

    copies[0].wait()
    for s in range(slots):
        for face in (0, 2):
            partner = maps_in[0, 0, face, s]
            inverse[face // 2 * (slots + 1) + jnp.where(partner >= 0, partner, slots)] = s
    counts = [jnp.int32(face * SPAN) for face in range(4)]
    for s in range(slots):
        partners = [maps_in[0, 0, face, s] for face in range(4)]
        best = jnp.maximum(jnp.maximum(partners[0], partners[1]), jnp.maximum(partners[2], partners[3]))
        lists[4 * SPAN + s] = (best >= 0).astype(jnp.int32)
        for face in range(4):
            if face in (1, 3):
                valid = partners[face] >= 0
                slot = jnp.where(valid, s, slots)
            else:
                slot = inverse[face // 2 * (slots + 1) + s]
                valid = slot < slots
            lists[counts[face]] = slot
            counts[face] = counts[face] + valid.astype(jnp.int32)

    top = (depth + 1) * rows
    copies[1].wait()
    copies[2].wait()
    for s in range(slots):
        grain = grains_in[0, 0, s]
        below = jnp.where(planes_in[0] == grain, 1.0, 0.0)
        above = jnp.where(planes_in[1] == grain, 1.0, 0.0)
        for ref in (now, stepped):
            ref[s, pl.ds(0, rows), :] = below
            ref[s, pl.ds(top, rows), :] = above
    field_part(0).wait()

    step(now, stepped, slots, depth, rows, cols, squares, lambda i: field_part(i).wait())

    linked = [[lists[face * SPAN + k] for k in range(LINKS)] for face in range(4)]
    end = 3 * LINKS * depth
    edge_row, edge_lane = row_and_lane(depth, cols)
    for face, out in ((1, x_up), (0, x_low)):
        r, inner_r = (0, 1) if face == 0 else (rows - 1, rows - 2)
        rim_rows = pl.ds(rows + r, depth, stride=rows)
        rest = squares[pl.ds(r, depth, stride=rows), :]
        for k in range(LINKS):
            slot = linked[face][k]
            partial = stepped[slot, rim_rows, :]
            inner = stepped[slot, pl.ds(rows + inner_r, depth, stride=rows), :]
            below = jnp.broadcast_to(now[slot, pl.ds(r, 1), :], (depth, cols))
            above = jnp.broadcast_to(now[slot, pl.ds(top + r, 1), :], (depth, cols))
            inner = inner + jnp.where(edge_row == 0, below, jnp.where(edge_row == depth - 1, above, 0.0))
            rest = rest - partial * partial
            out[x_rows(0, k, depth), :] = now[slot, rim_rows, :]
            out[x_rows(1, k, depth), :] = partial
            out[x_rows(2, k, depth), :] = inner
        corners = [jnp.zeros((depth, cols), jnp.float32)] * 4
        for k in range(LINKS):
            for side in range(2):
                slot = linked[2 + side][k]
                for i, ref in enumerate((stepped, now)):
                    place = (2 * i + side) * LINKS + k
                    moved = spin(ref[slot, rim_rows, :], place - side * (cols - 1))
                    corners[2 * i + side] = jnp.where(edge_lane == place, moved, corners[2 * i + side])
        out[pl.ds(end, depth), :] = (corners[0] + corners[1]) + (corners[2] + corners[3])
        out[pl.ds(end + depth, depth), :] = rest
        if out.shape[0] > end + 2 * depth:
            left = out.shape[0] - end - 2 * depth
            out[pl.ds(end + 2 * depth, left), :] = jnp.zeros((left, cols), jnp.float32)


def y_kernel(slots, depth, rows, cols, now, stepped, squares, lists, y_low, y_up):
    top = (depth + 1) * rows
    _, lane = row_and_lane(rows, cols)
    for side, out in ((0, y_low), (1, y_up)):
        c, inward = (0, 1) if side == 0 else (cols - 1, -1)
        linked = [lists[(2 + side) * SPAN + k] for k in range(LINKS)]
        rim, _ = gather_columns(now, linked, c, depth, rows, cols)
        partial, inner = gather_columns(stepped, linked, c, depth, rows, cols, beside=inward)
        for k in range(LINKS):
            for z, at in ((0, 0), (depth - 1, top)):
                place = GROUP * k + z
                frozen = spin(now[linked[k], pl.ds(at, rows), :], place - c)
                inner = inner + jnp.where(lane == place, frozen, 0.0)
        total = jnp.zeros((rows, cols), jnp.float32)
        for z in range(depth):
            place = LINKS * GROUP + z
            total = jnp.where(lane == place, spin(tile(squares, z, rows), place - c), total)
        inner = jnp.where(in_last_group(lane), total - group_sum(partial * partial), inner)
        out[pl.ds(0, rows), :] = rim
        out[pl.ds(rows, rows), :] = partial
        out[pl.ds(2 * rows, rows), :] = inner


def in_last_group(lane):
    return (lane >= LINKS * GROUP) & (lane < (LINKS + 1) * GROUP)


def tile(ref, i, rows):
    return ref[pl.ds(i * rows, rows), :]


def y_faces(ref, tiles, lists, depth, rows, cols, replace=False, done=None):
    _, lane = row_and_lane(rows, cols)
    for k in range(LINKS):
        for side in range(2):
            c = side * (cols - 1)
            slot = lists[(2 + side) * SPAN + k]
            ats = [pl.ds((z + 1) * rows, rows) for z in range(depth)]
            old = [ref[slot, at, :] for at in ats]
            for z in range(depth):
                moved = spin(tiles[side], c - GROUP * k - z)
                ref[slot, ats[z], :] = jnp.where(lane == c, moved if replace else old[z] + moved, old[z])
            if done is not None:
                done(slot)


def second_kernel(
    slots, depth, rows, cols, stepped_in, y_low_own, y_up_own, y_low, y_up, lists, now, later
):
    for s in range(slots):
        for at in (0, (depth + 1) * rows):
            later[s, pl.ds(at, rows), :] = now[s, pl.ds(at, rows), :]
    later[slots] = jnp.zeros(((depth + 2) * rows, cols), jnp.float32)
    pairs = ((y_low_own, y_low), (y_up_own, y_up))
    own_one = [tile(own, 1, rows) + RATE * tile(got, 0, rows) for own, got in pairs]
    one = [RATE * (tile(got, 1, rows) + RATE * tile(own, 0, rows)) for own, got in pairs]
    y_faces(now, own_one, lists, depth, rows, cols, replace=True)
    step(now, later, slots, depth, rows, cols)
    y_faces(later, one, lists, depth, rows, cols)


def x_rims(own, got, k, depth):
    zero, one = x_rows(0, k, depth), x_rows(1, k, depth)
    return own[one, :] + RATE * got[zero, :], got[one, :] + RATE * own[zero, :]


def change_kernel(depth, cols, own, got, before, out):
    change = jnp.zeros((depth, cols), jnp.float32)
    for k in range(LINKS):
        own_one, _ = x_rims(own, got, k, depth)
        partial = own[x_rows(1, k, depth), :]
        change = change + (own_one * own_one - partial * partial)
    out[pl.ds(0, depth), :] = change
    out[pl.ds(depth, depth), :] = got[pl.ds(3 * LINKS * depth, depth), :]


def both_changes_kernel(depth, cols, own, got, before, out):
    out[pl.ds(0, 2 * depth), :] = before[...]
    change_kernel(depth, cols, own, got, None, out.at[pl.ds(2 * depth, 2 * depth), :])


def x_rim_step(padded, face, k, one, factor, outer, depth, cols):
    _, lane = row_and_lane(depth, cols)
    z_sum = padded[face, pl.ds(k, depth, stride=SPAN), :] + padded[face, pl.ds(2 * SPAN + k, depth, stride=SPAN), :]
    y_sum = jnp.where(lane == 0, 0.0, pltpu.roll(one, 1, 1)) + jnp.where(
        lane == cols - 1, 0.0, pltpu.roll(one, cols - 1, 1)
    )
    return RATE * (one * (factor + one * one) + (outer + (z_sum + y_sum)))


def y_rim_step(one, factor, outer):
    rows, cols = one.shape
    row, _ = row_and_lane(rows, cols)
    x_sum = jnp.where(row == 0, 0.0, pltpu.roll(one, 1, 0)) + jnp.where(
        row == rows - 1, 0.0, pltpu.roll(one, rows - 1, 0)
    )
    z_sum = spin(one, 1) + spin(one, -1)
    return RATE * (one * (factor + one * one) + (outer + (x_sum + z_sum)))


def third_kernel(
    slots, depth, rows, cols,
    now, later_in, x_low_own, x_up_own, x_low, x_up, changes, lists,
    later, last,
    x_own_one,
):
    last[slots] = jnp.zeros(((depth + 2) * rows, cols), jnp.float32)
    x_own_one[...] = jnp.zeros(x_own_one.shape, jnp.float32)
    for face, own, got in ((0, x_low_own, x_low), (1, x_up_own, x_up)):
        r, inner_r = (0, 1) if face == 0 else (rows - 1, rows - 2)
        rim_rows = pl.ds(rows + r, depth, stride=rows)
        inner_rows = pl.ds(rows + inner_r, depth, stride=rows)
        rims = [x_rims(own, got, k, depth) for k in range(LINKS)]
        for k in range(LINKS):
            x_own_one[face, pl.ds(SPAN + k, depth, stride=SPAN), :] = rims[k][0]

        change = changes[pl.ds(2 * face * depth, depth), :]
        scaled = 0.15 * change
        parts = [change, None, None, None]
        for first in range(0, slots, 4):
            rim = [now[first + i, rim_rows, :] for i in range(4)]
            old = [later[first + i, rim_rows, :] for i in range(4)]
            for i in range(4):
                parts[i] = rim[i] * rim[i] if parts[i] is None else parts[i] + rim[i] * rim[i]
                later[first + i, rim_rows, :] = old[i] - scaled * rim[i]
        factor = 4.5 - 1.5 * ((parts[0] + parts[1]) + (parts[2] + parts[3]))

        linked = [lists[face * SPAN + k] for k in range(LINKS)]
        beside = [later[slot, inner_rows, :] for slot in linked]
        two = []
        for k in range(LINKS):
            outer = own[x_rows(2, k, depth), :] + rims[k][1]
            two.append(x_rim_step(x_own_one, face, k, rims[k][0], factor, outer, depth, cols))
        for k in range(LINKS):
            later[linked[k], rim_rows, :] = two[k]
            later[linked[k], inner_rows, :] = beside[k] + RATE * RATE * got[x_rows(0, k, depth), :]

    step(later, last, slots, depth, rows, cols)


def last_kernel(
    slots, depth, rows, cols,
    last_in, x_low_own, x_up_own, x_low, x_up, y_low_own, y_up_own, y_low, y_up, from_left, from_right,
    lists,
    last, result,
    x_one, sent,
):
    whole = last.at[pl.ds(0, slots), pl.ds(rows, depth * rows), :]

    def send(slot):
        pltpu.make_async_copy(last.at[slot, pl.ds(rows, depth * rows), :], result.at[slot], sent).start()

    def send_linked(slot):
        pl.when(slot < slots)(lambda: send(slot))

    for s in range(slots):
        pl.when(lists[4 * SPAN + s] == 0)(functools.partial(send, s))

    row, lane = row_and_lane(rows, cols)
    _, flat_lane = row_and_lane(depth, cols)
    tall_row, tall_lane = row_and_lane(GROUP, cols)
    block = LINKS * depth
    passed_on = (from_left, from_right)
    x_one[...] = jnp.zeros(x_one.shape, jnp.float32)
    for face, own, got in ((0, x_low_own, x_low), (1, x_up_own, x_up)):
        rims = [x_rims(own, got, k, depth) for k in range(LINKS)]
        total = got[pl.ds(3 * block + depth, depth), :]
        for k in range(LINKS):
            total = total + rims[k][1] * rims[k][1]
            x_one[face, pl.ds(SPAN + k, depth, stride=SPAN), :] = rims[k][1]
        corners = got[pl.ds(3 * block, depth), :]
        for side in range(2):
            place = side * LINKS
            came_from = (3 - side) * LINKS
            term = RATE * spin(passed_on[side][pl.ds((2 * face + 1) * depth, depth), :], place - came_from)
            term = term * (2.0 * corners + term)
            term = jnp.where((flat_lane >= place) & (flat_lane < place + LINKS), term, 0.0)
            column = jnp.sum(term, axis=1, keepdims=True)
            total = total + jnp.where(flat_lane == side * (cols - 1), column, 0.0)
        factor = 4.5 - 1.5 * total
        rim_rows = pl.ds(rows + (0 if face == 0 else rows - 1), depth, stride=rows)
        linked = [lists[face * SPAN + k] for k in range(LINKS)]
        old = [last[slot, rim_rows, :] for slot in linked]
        for k in range(LINKS):
            outer = got[x_rows(2, k, depth), :] + rims[k][0]
            two = x_rim_step(x_one, face, k, rims[k][1], factor, outer, depth, cols)
            last[linked[k], rim_rows, :] = old[k] + RATE * two
        for slot in linked:
            send_linked(slot)

    twos = []
    for side, own, got in ((0, y_low_own, y_low), (1, y_up_own, y_up)):
        c = side * (cols - 1)
        own_one = tile(own, 1, rows) + RATE * tile(got, 0, rows)
        one = tile(got, 1, rows) + RATE * tile(own, 0, rows)
        inner = tile(got, 2, rows)
        squares = one * one + jnp.where(in_last_group(lane), inner, 0.0)
        for face in range(2):
            change = passed_on[side][pl.ds(2 * face * depth, depth), :]
            column = jnp.sum(jnp.where(flat_lane == cols - 1 - c, change, 0.0), axis=1, keepdims=True)
            line = jnp.sum(jnp.where(tall_row == tall_lane, 1.0, 0.0)[:depth] * column, axis=0, keepdims=True)
            at_row = row == (0 if face == 0 else rows - 1)
            squares = squares + jnp.where(at_row, jnp.broadcast_to(line, (rows, cols)), 0.0)
        factor = 4.5 - 1.5 * group_sum(squares)
        twos.append(RATE * y_rim_step(one, factor, inner + own_one))
    y_faces(last, twos, lists, depth, rows, cols, done=send_linked)
    pltpu.make_async_copy(whole, result, sent).wait()


def shifted(block, axis, distance):
    size = lax.axis_size(axis)
    return lax.ppermute(block, axis, [((i - distance) % size, i) for i in range(size)])


def on_device(order_params, grain_ids, channel_maps, zplanes):
    slots, depth, rows, cols = order_params.shape
    f32 = jnp.float32
    shape = jax.ShapeDtypeStruct
    padded = pltpu.VMEM((slots + 1, (depth + 2) * rows, cols), f32)
    planes = pltpu.VMEM((depth * rows, cols), f32)
    x_pack = shape((-(-(3 * LINKS + 2) * depth // rows) * rows, cols), f32)
    y_pack = shape((3 * rows, cols), f32)
    rims = pltpu.VMEM((2, (depth + 2) * SPAN, cols), f32)
    vmem = pl.BlockSpec(memory_space=pltpu.VMEM)
    smem = pl.BlockSpec(memory_space=pltpu.SMEM)
    hbm = pl.BlockSpec(memory_space=pltpu.HBM)
    params = pltpu.CompilerParams(vmem_limit_bytes=24 * 1024 * 1024)
    field = order_params.reshape(slots, depth * rows, cols)
    sizes = (slots, depth, rows, cols)
    work = pl.CostEstimate(flops=20 * field.size, bytes_accessed=2 * 4 * field.size, transcendentals=0)

    now, stepped, squares, x_low, x_up, lists = pl.pallas_call(
        functools.partial(first_kernel, *sizes),
        out_shape=[padded, padded, planes, x_pack, x_pack, shape((4 * SPAN + slots,), jnp.int32)],
        in_specs=[hbm] * 4,
        out_specs=[vmem] * 5 + [smem],
        scratch_shapes=[
            pltpu.VMEM(zplanes.shape, jnp.int32),
            pltpu.SMEM(grain_ids.shape, jnp.int32),
            pltpu.SMEM(channel_maps.shape, jnp.int32),
            pltpu.SMEM((2 * (slots + 1),), jnp.int32),
            pltpu.SemaphoreType.DMA((3 + depth // UNROLL,)),
        ],
        compiler_params=params,
        name="first_step",
    )(*(pltpu.with_memory_space_constraint(x, pltpu.HBM) for x in (field, zplanes, grain_ids, channel_maps)))

    from_low = shifted(x_up, "gx", 1)
    from_up = shifted(x_low, "gx", -1)

    y_low, y_up = pl.pallas_call(
        functools.partial(y_kernel, *sizes),
        out_shape=[y_pack, y_pack],
        in_specs=[vmem] * 3 + [smem],
        out_specs=[vmem] * 2,
        compiler_params=params,
        cost_estimate=work,
        name="y_rims",
    )(now, stepped, squares, lists)

    from_right = shifted(y_low, "gy", -1)
    from_left = shifted(y_up, "gy", 1)

    fixed, later = pl.pallas_call(
        functools.partial(second_kernel, *sizes),
        out_shape=[padded, padded],
        in_specs=[vmem] * 5 + [smem],
        out_specs=[vmem] * 2,
        input_output_aliases={0: 0},
        compiler_params=params,
        cost_estimate=work,
        name="second_step",
    )(stepped, y_low, y_up, from_left, from_right, lists)

    changes = later
    for body, own, got, name in (
        (change_kernel, x_low, from_low, "corners_low"),
        (both_changes_kernel, x_up, from_up, "corners_up"),
    ):
        changes = pl.pallas_call(
            functools.partial(body, depth, cols),
            out_shape=shape(((2 if body is change_kernel else 4) * depth, cols), f32),
            in_specs=[vmem] * 3,
            out_specs=vmem,
            compiler_params=params,
            name=name,
        )(own, got, changes)

    changes_from_right = shifted(changes, "gy", -1)
    changes_from_left = shifted(changes, "gy", 1)

    _, last = pl.pallas_call(
        functools.partial(third_kernel, *sizes),
        out_shape=[padded, padded],
        in_specs=[vmem] * 7 + [smem],
        out_specs=[vmem] * 2,
        scratch_shapes=[rims],
        input_output_aliases={1: 0},
        compiler_params=params,
        name="third_step",
    )(
        fixed, later, x_low, x_up, from_low, from_up, changes, lists,
    )

    _, result = pl.pallas_call(
        functools.partial(last_kernel, *sizes),
        out_shape=[padded, shape(field.shape, f32)],
        in_specs=[vmem] * 11 + [smem],
        out_specs=[vmem, hbm],
        scratch_shapes=[rims, pltpu.SemaphoreType.DMA],
        input_output_aliases={0: 0},
        compiler_params=params,
        name="last_rims",
    )(
        last, x_low, x_up, from_low, from_up,
        y_low, y_up, from_left, from_right, changes_from_left, changes_from_right, lists,
    )
    return result.reshape(order_params.shape)


def solution(mesh):
    in_specs = (
        P(None, None, "gx", "gy"),
        P("gx", "gy", None),
        P("gx", "gy", None, None),
        P(None, "gx", "gy"),
    )
    return jax.shard_map(
        on_device, mesh=mesh, in_specs=in_specs, out_specs=P(None, None, "gx", "gy"), check_vma=False
    )
```

```python
import functools

import jax
import jax.numpy as jnp
from jax import lax
from jax.experimental import pallas as pl
from jax.experimental.pallas import tpu as pltpu
from jax.sharding import PartitionSpec as P


LINKS = 6
SPAN = 8
GROUP = 16
RATE = 0.1
UNROLL = 4


def row_and_lane(rows, cols):
    row = lax.broadcasted_iota(jnp.int32, (rows, cols), 0)
    lane = lax.broadcasted_iota(jnp.int32, (rows, cols), 1)
    return row, lane


def spin(tile, amount):
    cols = tile.shape[1]
    amount = amount % cols
    return tile if amount == 0 else pltpu.roll(tile, amount, 1)


def group_sum(tile):
    shift = GROUP
    while shift < tile.shape[1]:
        tile = tile + spin(tile, shift)
        shift *= 2
    return tile


def step(src, dst, slots, depth, rows, cols, squares=None, wait=None, beside=None, carried=()):
    row, lane = row_and_lane(rows, cols)
    first_row, last_row = row == 0, row == rows - 1
    first_lane, last_lane = lane == 0, lane == cols - 1

    def add(parts, s, term):
        parts[s % 4] = term if parts[s % 4] is None else parts[s % 4] + term

    def total(parts):
        return (parts[0] + parts[1]) + (parts[2] + parts[3])

    def at(z):
        return pl.ds(pl.multiple_of((z + 1) * rows, rows), rows)

    def layer(z, factor):
        following, parts = [None] * 4, [None] * 4
        for s in range(slots):
            v, below, above = src[s, at(z), :], src[s, at(z - 1), :], src[s, at(z + 1), :]
            add(following, s, above * above)
            x_sum = jnp.where(first_row, 0.0, pltpu.roll(v, 1, 0)) + jnp.where(
                last_row, 0.0, pltpu.roll(v, rows - 1, 0)
            )
            y_sum = jnp.where(first_lane, 0.0, pltpu.roll(v, 1, 1)) + jnp.where(
                last_lane, 0.0, pltpu.roll(v, cols - 1, 1)
            )
            new = RATE * (v * (factor + v * v) + ((x_sum + y_sum) + (below + above)))
            dst[s, at(z), :] = new
            if squares is not None:
                add(parts, s, new * new)
        if squares is not None:
            squares[pl.ds(pl.multiple_of(z * rows, rows), rows), :] = total(parts)
        return 4.5 - 1.5 * total(following)

    def layers(i, carry):
        factor, *carried = carry
        if wait is not None:
            pl.when(i + 1 < depth // UNROLL)(lambda: wait(i + 1))
        if beside is not None:
            carried = beside(i, carried)
        for j in range(UNROLL):
            factor = layer(i * UNROLL + j, factor)
        return (factor, *carried)

    first = [None] * 4
    for s in range(slots):
        v = src[s, at(0), :]
        add(first, s, v * v)
    lax.fori_loop(0, depth // UNROLL, layers, (4.5 - 1.5 * total(first), *carried))


def gather_columns(ref, low, up, depth, rows, cols, beside=False):
    _, lane = row_and_lane(rows, cols)
    shifts = (0, -1, 1, -2) if beside else (0, -1)
    results = [jnp.zeros((rows, cols), jnp.float32)] * len(shifts)
    for k in range(LINKS):
        parts = [jnp.zeros((rows, cols), jnp.float32)] * len(shifts)
        for z in range(depth):
            at = pl.ds((z + 1) * rows, rows)
            place = GROUP * k + z
            moved = spin(jnp.where(lane < cols // 2, ref[low[k], at, :], ref[up[k], at, :]), place)
            for i, shift in enumerate(shifts):
                parts[i] = jnp.where(lane == (place + shift) % cols, moved, parts[i])
        results = [result + part for result, part in zip(results, parts)]
    return [spin(result, -shift) for result, shift in zip(results, shifts)]


def x_rows(part, k, depth):
    return pl.ds(part * LINKS * depth + k, depth, stride=LINKS)


def first_kernel(
    slots, depth, rows, cols,
    field, planes, grains, maps,
    now, stepped, squares, x_low, x_up, lists,
    planes_in, grains_in, maps_in, inverse, arrived,
):
    copies = [
        pltpu.make_async_copy(maps, maps_in, arrived.at[0]),
        pltpu.make_async_copy(grains, grains_in, arrived.at[1]),
        pltpu.make_async_copy(planes, planes_in, arrived.at[2]),
    ]
    part = UNROLL * rows

    def field_part(i):
        to = pl.ds(pl.multiple_of(i * part + rows, rows), part)
        source = field.at[:, pl.ds(pl.multiple_of(i * part, rows), part), :]
        return pltpu.make_async_copy(source, now.at[pl.ds(0, slots), to, :], arrived.at[3 + i])

    for copy in copies:
        copy.start()
    for i in range(depth // UNROLL):
        field_part(i).start()
    for ref in (now, stepped):
        ref[slots] = jnp.zeros(((depth + 2) * rows, cols), jnp.float32)
    for face in range(4):
        for place in range(SPAN):
            lists[face * SPAN + place] = slots
    for t in range(slots + 1):
        inverse[t] = slots
        inverse[slots + 1 + t] = slots

    copies[0].wait()
    for s in range(slots):
        for face in (0, 2):
            partner = maps_in[0, 0, face, s]
            inverse[face // 2 * (slots + 1) + jnp.where(partner >= 0, partner, slots)] = s
    top = (depth + 1) * rows
    copies[1].wait()
    copies[2].wait()
    for s in range(slots):
        grain = grains_in[0, 0, s]
        below = jnp.where(planes_in[0] == grain, 1.0, 0.0)
        above = jnp.where(planes_in[1] == grain, 1.0, 0.0)
        for ref in (now, stepped):
            ref[s, pl.ds(0, rows), :] = below
            ref[s, pl.ds(top, rows), :] = above
    field_part(0).wait()

    share = -(-slots // (depth // UNROLL))

    def enlist(i, counts):
        for j in range(share):
            s = i * share + j
            s = s if slots % share == 0 else jnp.minimum(s, slots - 1)
            fresh = True if slots % share == 0 else i * share + j < slots
            partners = [maps_in[0, 0, face, s] for face in range(4)]
            best = jnp.maximum(jnp.maximum(partners[0], partners[1]), jnp.maximum(partners[2], partners[3]))
            lists[4 * SPAN + s] = (best >= 0).astype(jnp.int32)
            for face in range(4):
                if face in (1, 3):
                    valid = partners[face] >= 0
                    slot = jnp.where(valid, s, slots)
                else:
                    slot = inverse[face // 2 * (slots + 1) + s]
                    valid = slot < slots
                lists[counts[face]] = slot
                counts[face] = counts[face] + (valid & fresh).astype(jnp.int32)
        return counts

    step(
        now, stepped, slots, depth, rows, cols, squares,
        lambda i: field_part(i).wait(), enlist, [jnp.int32(face * SPAN) for face in range(4)],
    )

    linked = [[lists[face * SPAN + k] for k in range(LINKS)] for face in range(4)]
    end = 3 * LINKS * depth
    edge_row, edge_lane = row_and_lane(depth, cols)
    for face, out in ((1, x_up), (0, x_low)):
        r, inner_r = (0, 1) if face == 0 else (rows - 1, rows - 2)
        rim_rows = pl.ds(rows + r, depth, stride=rows)
        rest = squares[pl.ds(r, depth, stride=rows), :]
        for k in range(LINKS):
            slot = linked[face][k]
            partial = stepped[slot, rim_rows, :]
            inner = stepped[slot, pl.ds(rows + inner_r, depth, stride=rows), :]
            below = jnp.broadcast_to(now[slot, pl.ds(r, 1), :], (depth, cols))
            above = jnp.broadcast_to(now[slot, pl.ds(top + r, 1), :], (depth, cols))
            inner = inner + jnp.where(edge_row == 0, below, jnp.where(edge_row == depth - 1, above, 0.0))
            rest = rest - partial * partial
            out[x_rows(0, k, depth), :] = now[slot, rim_rows, :]
            out[x_rows(1, k, depth), :] = partial
            out[x_rows(2, k, depth), :] = inner
        corners = [jnp.zeros((depth, cols), jnp.float32)] * 4
        for k in range(LINKS):
            for side in range(2):
                slot = linked[2 + side][k]
                for i, ref in enumerate((stepped, now)):
                    place = (2 * i + side) * LINKS + k
                    moved = spin(ref[slot, rim_rows, :], place - side * (cols - 1))
                    corners[2 * i + side] = jnp.where(edge_lane == place, moved, corners[2 * i + side])
        out[pl.ds(end, depth), :] = (corners[0] + corners[1]) + (corners[2] + corners[3])
        out[pl.ds(end + depth, depth), :] = rest
        if out.shape[0] > end + 2 * depth:
            left = out.shape[0] - end - 2 * depth
            out[pl.ds(end + 2 * depth, left), :] = jnp.zeros((left, cols), jnp.float32)


def y_kernel(slots, depth, rows, cols, now, stepped, squares, lists, y_low, y_up):
    top = (depth + 1) * rows
    _, lane = row_and_lane(rows, cols)
    low, up = ([lists[face * SPAN + k] for k in range(LINKS)] for face in (2, 3))
    rims = gather_columns(now, low, up, depth, rows, cols)
    *partials, inner_low, inner_up = gather_columns(stepped, low, up, depth, rows, cols, beside=True)
    frozen = [jnp.zeros((rows, cols), jnp.float32)] * 2
    totals = [jnp.zeros((rows, cols), jnp.float32)] * 2
    for k in range(LINKS):
        for z, at in ((0, 0), (depth - 1, top)):
            place = GROUP * k + z
            at = pl.ds(at, rows)
            moved = spin(jnp.where(lane < cols // 2, now[low[k], at, :], now[up[k], at, :]), place)
            for side in range(2):
                frozen[side] = jnp.where(lane == (place - side) % cols, moved, frozen[side])
    for z in range(depth):
        place = LINKS * GROUP + z
        moved = spin(tile(squares, z, rows), place)
        for side in range(2):
            totals[side] = jnp.where(lane == place - side, moved, totals[side])
    for side, out, inner in ((0, y_low, inner_low), (1, y_up, inner_up)):
        rest = spin(totals[side], side) - group_sum(partials[side] * partials[side])
        out[pl.ds(0, rows), :] = rims[side]
        out[pl.ds(rows, rows), :] = partials[side]
        out[pl.ds(2 * rows, rows), :] = jnp.where(in_last_group(lane), rest, inner + spin(frozen[side], side))


def in_last_group(lane):
    return (lane >= LINKS * GROUP) & (lane < (LINKS + 1) * GROUP)


def tile(ref, i, rows):
    return ref[pl.ds(i * rows, rows), :]


def y_faces(ref, tiles, lists, depth, rows, cols, replace=False, done=None):
    _, lane = row_and_lane(rows, cols)
    for k in range(LINKS):
        for side in range(2):
            c = side * (cols - 1)
            slot = lists[(2 + side) * SPAN + k]
            ats = [pl.ds((z + 1) * rows, rows) for z in range(depth)]
            old = [ref[slot, at, :] for at in ats]
            for z in range(depth):
                moved = spin(tiles[side], c - GROUP * k - z)
                ref[slot, ats[z], :] = jnp.where(lane == c, moved if replace else old[z] + moved, old[z])
            if done is not None:
                done(slot)


def second_kernel(
    slots, depth, rows, cols, stepped_in, y_low_own, y_up_own, y_low, y_up, lists, now, later
):
    for s in range(slots):
        for at in (0, (depth + 1) * rows):
            later[s, pl.ds(at, rows), :] = now[s, pl.ds(at, rows), :]
    later[slots] = jnp.zeros(((depth + 2) * rows, cols), jnp.float32)
    pairs = ((y_low_own, y_low), (y_up_own, y_up))
    own_one = [tile(own, 1, rows) + RATE * tile(got, 0, rows) for own, got in pairs]
    one = [RATE * (tile(got, 1, rows) + RATE * tile(own, 0, rows)) for own, got in pairs]
    y_faces(now, own_one, lists, depth, rows, cols, replace=True)
    step(now, later, slots, depth, rows, cols)
    y_faces(later, one, lists, depth, rows, cols)


def x_rims(own, got, k, depth):
    zero, one = x_rows(0, k, depth), x_rows(1, k, depth)
    return own[one, :] + RATE * got[zero, :], got[one, :] + RATE * own[zero, :]


def change_kernel(depth, cols, own, got, before, out):
    change = jnp.zeros((depth, cols), jnp.float32)
    for k in range(LINKS):
        own_one, _ = x_rims(own, got, k, depth)
        partial = own[x_rows(1, k, depth), :]
        change = change + (own_one * own_one - partial * partial)
    out[pl.ds(0, depth), :] = change
    out[pl.ds(depth, depth), :] = got[pl.ds(3 * LINKS * depth, depth), :]
    out[pl.ds(2 * depth, depth), :] = own[pl.ds(3 * LINKS * depth, depth), :]


def both_changes_kernel(depth, cols, own, got, before, out):
    out[pl.ds(0, 3 * depth), :] = before[...]
    change_kernel(depth, cols, own, got, None, out.at[pl.ds(3 * depth, 3 * depth), :])


def x_rim_step(padded, face, k, one, factor, outer, depth, cols):
    _, lane = row_and_lane(depth, cols)
    z_sum = padded[face, pl.ds(k, depth, stride=SPAN), :] + padded[face, pl.ds(2 * SPAN + k, depth, stride=SPAN), :]
    y_sum = jnp.where(lane == 0, 0.0, pltpu.roll(one, 1, 1)) + jnp.where(
        lane == cols - 1, 0.0, pltpu.roll(one, cols - 1, 1)
    )
    return RATE * (one * (factor + one * one) + (outer + (z_sum + y_sum)))


def y_rim_step(one, factor, outer):
    rows, cols = one.shape
    row, _ = row_and_lane(rows, cols)
    x_sum = jnp.where(row == 0, 0.0, pltpu.roll(one, 1, 0)) + jnp.where(
        row == rows - 1, 0.0, pltpu.roll(one, rows - 1, 0)
    )
    z_sum = spin(one, 1) + spin(one, -1)
    return RATE * (one * (factor + one * one) + (outer + (x_sum + z_sum)))


def third_kernel(
    slots, depth, rows, cols,
    now, later_in, x_low_own, x_up_own, x_low, x_up, changes, lists,
    later, last,
    x_own_one,
):
    last[slots] = jnp.zeros(((depth + 2) * rows, cols), jnp.float32)
    x_own_one[...] = jnp.zeros(x_own_one.shape, jnp.float32)
    for face, own, got in ((0, x_low_own, x_low), (1, x_up_own, x_up)):
        r, inner_r = (0, 1) if face == 0 else (rows - 1, rows - 2)
        rim_rows = pl.ds(rows + r, depth, stride=rows)
        inner_rows = pl.ds(rows + inner_r, depth, stride=rows)
        rims = [x_rims(own, got, k, depth) for k in range(LINKS)]
        for k in range(LINKS):
            x_own_one[face, pl.ds(SPAN + k, depth, stride=SPAN), :] = rims[k][0]

        change = changes[pl.ds(3 * face * depth, depth), :]
        scaled = 0.15 * change
        parts = [change, None, None, None]
        for first in range(0, slots, 4):
            rim = [now[first + i, rim_rows, :] for i in range(4)]
            old = [later[first + i, rim_rows, :] for i in range(4)]
            for i in range(4):
                parts[i] = rim[i] * rim[i] if parts[i] is None else parts[i] + rim[i] * rim[i]
                later[first + i, rim_rows, :] = old[i] - scaled * rim[i]
        factor = 4.5 - 1.5 * ((parts[0] + parts[1]) + (parts[2] + parts[3]))

        linked = [lists[face * SPAN + k] for k in range(LINKS)]
        beside = [later[slot, inner_rows, :] for slot in linked]
        two = []
        for k in range(LINKS):
            outer = own[x_rows(2, k, depth), :] + rims[k][1]
            two.append(x_rim_step(x_own_one, face, k, rims[k][0], factor, outer, depth, cols))
        for k in range(LINKS):
            later[linked[k], rim_rows, :] = two[k]
            later[linked[k], inner_rows, :] = beside[k] + RATE * RATE * got[x_rows(0, k, depth), :]

    step(later, last, slots, depth, rows, cols)


def rims_kernel(
    slots, depth, rows, cols,
    last_in, x_low_own, x_up_own, x_low, x_up, y_low_own, y_up_own, y_low, y_up, lists,
    last, result,
    x_one, sent,
):
    _, lane = row_and_lane(rows, cols)

    def each_unlinked(act):
        for s in range(slots):
            copy = pltpu.make_async_copy(last.at[s, pl.ds(rows, depth * rows), :], result.at[s], sent)
            pl.when(lists[4 * SPAN + s] == 0)(getattr(copy, act))

    each_unlinked("start")
    x_one[...] = jnp.zeros(x_one.shape, jnp.float32)
    for face, own, got in ((0, x_low_own, x_low), (1, x_up_own, x_up)):
        rims = [x_rims(own, got, k, depth) for k in range(LINKS)]
        total = got[pl.ds((3 * LINKS + 1) * depth, depth), :]
        for k in range(LINKS):
            total = total + rims[k][1] * rims[k][1]
            x_one[face, pl.ds(SPAN + k, depth, stride=SPAN), :] = rims[k][1]
        factor = 4.5 - 1.5 * total
        rim_rows = pl.ds(rows + (0 if face == 0 else rows - 1), depth, stride=rows)
        linked = [lists[face * SPAN + k] for k in range(LINKS)]
        old = [last[slot, rim_rows, :] for slot in linked]
        for k in range(LINKS):
            outer = got[x_rows(2, k, depth), :] + rims[k][0]
            two = x_rim_step(x_one, face, k, rims[k][1], factor, outer, depth, cols)
            last[linked[k], rim_rows, :] = old[k] + RATE * two

    twos = []
    for own, got in ((y_low_own, y_low), (y_up_own, y_up)):
        own_one = tile(own, 1, rows) + RATE * tile(got, 0, rows)
        one = tile(got, 1, rows) + RATE * tile(own, 0, rows)
        inner = tile(got, 2, rows)
        factor = 4.5 - 1.5 * group_sum(one * one + jnp.where(in_last_group(lane), inner, 0.0))
        twos.append(RATE * y_rim_step(one, factor, inner + own_one))
    y_faces(last, twos, lists, depth, rows, cols)
    each_unlinked("wait")


def last_kernel(
    slots, depth, rows, cols,
    last_in, result_in, x_low_own, x_up_own, x_low, x_up, from_left, from_right, lists,
    last, result,
    sent,
):
    _, lane = row_and_lane(depth, cols)
    scale = -1.5 * RATE * RATE
    passed_on = (from_left, from_right)
    part = lambda ref, i: ref[pl.ds(i * depth, depth), :]
    corner_cells = lambda ref: ref[pl.ds(3 * LINKS * depth, depth), :]

    def each_linked(face, act):
        for k in range(LINKS):
            slot = lists[face * SPAN + k]

            @pl.when(slot < slots)
            def _():
                copy = pltpu.make_async_copy(last.at[slot, pl.ds(rows, depth * rows), :], result.at[slot], sent)
                getattr(copy, act)()

    for face, own, got in ((0, x_low_own, x_low), (1, x_up_own, x_up)):
        total = jnp.zeros((depth, cols), jnp.float32)
        for side in range(2):
            place = side * LINKS
            term = RATE * spin(part(passed_on[side], 3 * face + 1), place - (3 - side) * LINKS)
            term = term * (2.0 * corner_cells(got) + term)
            term = jnp.where((lane >= place) & (lane < place + LINKS), term, 0.0)
            column = jnp.sum(term, axis=1, keepdims=True)
            total = total + jnp.where(lane == side * (cols - 1), column, 0.0)
        total = scale * total
        rim_rows = pl.ds(rows + (0 if face == 0 else rows - 1), depth, stride=rows)
        linked = [lists[face * SPAN + k] for k in range(LINKS)]
        old = [last[slot, rim_rows, :] for slot in linked]
        for k in range(LINKS):
            _, one = x_rims(own, got, k, depth)
            last[linked[k], rim_rows, :] = old[k] + total * one
        each_linked(face, "start")

    for side in range(2):
        c = side * (cols - 1)
        linked = [lists[(2 + side) * SPAN + k] for k in range(LINKS)]
        for face, own in ((0, x_low_own), (1, x_up_own)):
            place = (1 - side) * LINKS
            one = part(passed_on[side], 3 * face + 2) + RATE * spin(corner_cells(own), place - (2 + side) * LINKS)
            change = jnp.where(lane == cols - 1 - c, part(passed_on[side], 3 * face), 0.0)
            one = scale * one * jnp.sum(change, axis=1, keepdims=True)
            rim_rows = pl.ds(rows + (0 if face == 0 else rows - 1), depth, stride=rows)
            old = [last[slot, rim_rows, :] for slot in linked]
            for k in range(LINKS):
                last[linked[k], rim_rows, :] = old[k] + jnp.where(lane == c, spin(one, c - place - k), 0.0)
        each_linked(2 + side, "start")
    for face in range(4):
        each_linked(face, "wait")


def shifted(block, axis, distance):
    size = lax.axis_size(axis)
    return lax.ppermute(block, axis, [((i - distance) % size, i) for i in range(size)])


def on_device(order_params, grain_ids, channel_maps, zplanes):
    slots, depth, rows, cols = order_params.shape
    f32 = jnp.float32
    shape = jax.ShapeDtypeStruct
    padded = pltpu.VMEM((slots + 1, (depth + 2) * rows, cols), f32)
    planes = pltpu.VMEM((depth * rows, cols), f32)
    x_pack = shape((-(-(3 * LINKS + 2) * depth // rows) * rows, cols), f32)
    y_pack = shape((3 * rows, cols), f32)
    rims = pltpu.VMEM((2, (depth + 2) * SPAN, cols), f32)
    vmem = pl.BlockSpec(memory_space=pltpu.VMEM)
    smem = pl.BlockSpec(memory_space=pltpu.SMEM)
    hbm = pl.BlockSpec(memory_space=pltpu.HBM)
    params = pltpu.CompilerParams(vmem_limit_bytes=24 * 1024 * 1024)
    field = order_params.reshape(slots, depth * rows, cols)
    sizes = (slots, depth, rows, cols)
    work = pl.CostEstimate(flops=20 * field.size, bytes_accessed=2 * 4 * field.size, transcendentals=0)

    now, stepped, squares, x_low, x_up, lists = pl.pallas_call(
        functools.partial(first_kernel, *sizes),
        out_shape=[padded, padded, planes, x_pack, x_pack, shape((4 * SPAN + slots,), jnp.int32)],
        in_specs=[hbm] * 4,
        out_specs=[vmem] * 5 + [smem],
        scratch_shapes=[
            pltpu.VMEM(zplanes.shape, jnp.int32),
            pltpu.SMEM(grain_ids.shape, jnp.int32),
            pltpu.SMEM(channel_maps.shape, jnp.int32),
            pltpu.SMEM((2 * (slots + 1),), jnp.int32),
            pltpu.SemaphoreType.DMA((3 + depth // UNROLL,)),
        ],
        compiler_params=params,
        name="first_step",
    )(*(pltpu.with_memory_space_constraint(x, pltpu.HBM) for x in (field, zplanes, grain_ids, channel_maps)))

    from_low = shifted(x_up, "gx", 1)
    from_up = shifted(x_low, "gx", -1)

    y_low, y_up = pl.pallas_call(
        functools.partial(y_kernel, *sizes),
        out_shape=[y_pack, y_pack],
        in_specs=[vmem] * 3 + [smem],
        out_specs=[vmem] * 2,
        compiler_params=params,
        cost_estimate=work,
        name="y_rims",
    )(now, stepped, squares, lists)

    from_right = shifted(y_low, "gy", -1)
    from_left = shifted(y_up, "gy", 1)

    fixed, later = pl.pallas_call(
        functools.partial(second_kernel, *sizes),
        out_shape=[padded, padded],
        in_specs=[vmem] * 5 + [smem],
        out_specs=[vmem] * 2,
        input_output_aliases={0: 0},
        compiler_params=params,
        cost_estimate=work,
        name="second_step",
    )(stepped, y_low, y_up, from_left, from_right, lists)

    changes = later
    for body, own, got, name in (
        (change_kernel, x_low, from_low, "corners_low"),
        (both_changes_kernel, x_up, from_up, "corners_up"),
    ):
        changes = pl.pallas_call(
            functools.partial(body, depth, cols),
            out_shape=shape(((3 if body is change_kernel else 6) * depth, cols), f32),
            in_specs=[vmem] * 3,
            out_specs=vmem,
            compiler_params=params,
            name=name,
        )(own, got, changes)

    changes_from_right = shifted(changes, "gy", -1)
    changes_from_left = shifted(changes, "gy", 1)

    _, last = pl.pallas_call(
        functools.partial(third_kernel, *sizes),
        out_shape=[padded, padded],
        in_specs=[vmem] * 7 + [smem],
        out_specs=[vmem] * 2,
        scratch_shapes=[rims],
        input_output_aliases={1: 0},
        compiler_params=params,
        name="third_step",
    )(
        fixed, later, x_low, x_up, from_low, from_up, changes, lists,
    )

    out_shape = [padded, pltpu.HBM(field.shape, f32)]
    last, result = pl.pallas_call(
        functools.partial(rims_kernel, *sizes),
        out_shape=out_shape,
        in_specs=[vmem] * 9 + [smem],
        out_specs=[vmem, hbm],
        scratch_shapes=[rims, pltpu.SemaphoreType.DMA],
        input_output_aliases={0: 0},
        compiler_params=params,
        name="rims",
    )(last, x_low, x_up, from_low, from_up, y_low, y_up, from_left, from_right, lists)

    _, result = pl.pallas_call(
        functools.partial(last_kernel, *sizes),
        out_shape=out_shape,
        in_specs=[vmem, hbm] + [vmem] * 6 + [smem],
        out_specs=[vmem, hbm],
        scratch_shapes=[pltpu.SemaphoreType.DMA],
        input_output_aliases={0: 0, 1: 1},
        compiler_params=params,
        name="corners_last",
    )(last, result, x_low, x_up, from_low, from_up, changes_from_left, changes_from_right, lists)
    return result.reshape(order_params.shape)


def solution(mesh):
    in_specs = (
        P(None, None, "gx", "gy"),
        P("gx", "gy", None),
        P("gx", "gy", None, None),
        P(None, "gx", "gy"),
    )
    return jax.shard_map(
        on_device, mesh=mesh, in_specs=in_specs, out_specs=P(None, None, "gx", "gy"), check_vma=False
    )
```

```python
import functools

import jax
import jax.numpy as jnp
from jax import lax
from jax.experimental import pallas as pl
from jax.experimental.pallas import tpu as pltpu
from jax.sharding import PartitionSpec as P


LINKS = 6
SPAN = 8
GROUP = 16
RATE = 0.1
UNROLL = 2
PART = 4


def row_and_lane(rows, cols):
    row = lax.broadcasted_iota(jnp.int32, (rows, cols), 0)
    lane = lax.broadcasted_iota(jnp.int32, (rows, cols), 1)
    return row, lane


def spin(tile, amount):
    cols = tile.shape[1]
    amount = amount % cols
    return tile if amount == 0 else pltpu.roll(tile, amount, 1)


def group_sum(tile):
    shift = GROUP
    while shift < tile.shape[1]:
        tile = tile + spin(tile, shift)
        shift *= 2
    return tile


def step(src, dst, slots, depth, rows, cols, squares=None, wait=None):
    row, lane = row_and_lane(rows, cols)
    first_row, last_row = row == 0, row == rows - 1
    first_lane, last_lane = lane == 0, lane == cols - 1

    def add(parts, s, term):
        parts[s % 4] = term if parts[s % 4] is None else parts[s % 4] + term

    def total(parts):
        return (parts[0] + parts[1]) + (parts[2] + parts[3])

    def at(z):
        return pl.ds(pl.multiple_of((z + 1) * rows, rows), rows)

    def layer(z, factor):
        following, parts = [None] * 4, [None] * 4
        for s in range(slots):
            v, below, above = src[s, at(z), :], src[s, at(z - 1), :], src[s, at(z + 1), :]
            add(following, s, above * above)
            x_sum = jnp.where(first_row, 0.0, pltpu.roll(v, 1, 0)) + jnp.where(
                last_row, 0.0, pltpu.roll(v, rows - 1, 0)
            )
            y_sum = jnp.where(first_lane, 0.0, pltpu.roll(v, 1, 1)) + jnp.where(
                last_lane, 0.0, pltpu.roll(v, cols - 1, 1)
            )
            new = RATE * (v * (factor + v * v) + ((x_sum + y_sum) + (below + above)))
            dst[s, at(z), :] = new
            if squares is not None:
                add(parts, s, new * new)
        if squares is not None:
            squares[pl.ds(pl.multiple_of(z * rows, rows), rows), :] = total(parts)
        return 4.5 - 1.5 * total(following)

    def layers(i, factor):
        if wait is not None:
            turns = PART // UNROLL
            pl.when((i % turns == turns - 1) & (i < depth // UNROLL - 1))(lambda: wait(i // turns + 1))
        for j in range(UNROLL):
            factor = layer(i * UNROLL + j, factor)
        return factor

    first = [None] * 4
    for s in range(slots):
        v = src[s, at(0), :]
        add(first, s, v * v)
    lax.fori_loop(0, depth // UNROLL, layers, 4.5 - 1.5 * total(first))


def gather_columns(ref, low, up, depth, rows, cols, beside=False):
    _, lane = row_and_lane(rows, cols)
    shifts = (0, -1, 1, -2) if beside else (0, -1)

    def link(i, results):
        results = [spin(result, GROUP) for result in results]
        low_slot, up_slot = low(LINKS - 1 - i), up(LINKS - 1 - i)
        for z in range(depth):
            at = pl.ds((z + 1) * rows, rows)
            moved = spin(jnp.where(lane < cols // 2, ref[low_slot, at, :], ref[up_slot, at, :]), z)
            for j, shift in enumerate(shifts):
                results[j] = jnp.where(lane == (z + shift) % cols, moved, results[j])
        return tuple(results)

    empty = jnp.zeros((rows, cols), jnp.float32)
    results = lax.fori_loop(0, LINKS, link, (empty,) * len(shifts))
    return [spin(result, -shift) for result, shift in zip(results, shifts)]


def x_rows(part, k, depth):
    return pl.ds(part * LINKS * depth + k, depth, stride=LINKS)


def first_kernel(
    slots, depth, rows, cols,
    field, planes, grains, maps,
    now, stepped, squares, x_low, x_up, lists,
    planes_in, grains_in, maps_in, inverse, arrived,
):
    copies = [
        pltpu.make_async_copy(maps, maps_in, arrived.at[0]),
        pltpu.make_async_copy(grains, grains_in, arrived.at[1]),
        pltpu.make_async_copy(planes, planes_in, arrived.at[2]),
    ]
    part = PART * rows

    def field_part(i):
        to = pl.ds(pl.multiple_of(i * part + rows, rows), part)
        source = field.at[:, pl.ds(pl.multiple_of(i * part, rows), part), :]
        return pltpu.make_async_copy(source, now.at[pl.ds(0, slots), to, :], arrived.at[3 + i])

    for copy in copies:
        copy.start()
    for i in range(depth // PART):
        field_part(i).start()
    for ref in (now, stepped):
        ref[slots] = jnp.zeros(((depth + 2) * rows, cols), jnp.float32)

    for place in range(4 * SPAN):
        lists[place] = slots

    def empty(t, carry):
        inverse[t] = slots
        return carry

    def invert(s, carry):
        for face in (0, 2):
            partner = maps_in[0, 0, face, s]
            inverse[face // 2 * (slots + 1) + jnp.where(partner >= 0, partner, slots)] = s
        return carry

    def enlist(s, counts):
        partners = [maps_in[0, 0, face, s] for face in range(4)]
        best = jnp.maximum(jnp.maximum(partners[0], partners[1]), jnp.maximum(partners[2], partners[3]))
        lists[4 * SPAN + s] = (best >= 0).astype(jnp.int32)
        following = []
        for face in range(4):
            if face in (1, 3):
                valid = partners[face] >= 0
                slot = jnp.where(valid, s, slots)
            else:
                slot = inverse[face // 2 * (slots + 1) + s]
                valid = slot < slots
            lists[counts[face]] = slot
            following.append(counts[face] + valid.astype(jnp.int32))
        return tuple(following)

    lax.fori_loop(0, 2 * (slots + 1), empty, 0)
    copies[0].wait()
    lax.fori_loop(0, slots, invert, 0)
    lax.fori_loop(0, slots, enlist, tuple(jnp.int32(face * SPAN) for face in range(4)))

    top = (depth + 1) * rows
    copies[1].wait()
    copies[2].wait()
    for s in range(slots):
        grain = grains_in[0, 0, s]
        below = jnp.where(planes_in[0] == grain, 1.0, 0.0)
        above = jnp.where(planes_in[1] == grain, 1.0, 0.0)
        for ref in (now, stepped):
            ref[s, pl.ds(0, rows), :] = below
            ref[s, pl.ds(top, rows), :] = above
    field_part(0).wait()

    step(now, stepped, slots, depth, rows, cols, squares, lambda i: field_part(i).wait())

    linked = [[lists[face * SPAN + k] for k in range(LINKS)] for face in range(4)]
    end = 3 * LINKS * depth
    edge_row, edge_lane = row_and_lane(depth, cols)
    for face, out in ((1, x_up), (0, x_low)):
        r, inner_r = (0, 1) if face == 0 else (rows - 1, rows - 2)
        rim_rows = pl.ds(rows + r, depth, stride=rows)
        rest = squares[pl.ds(r, depth, stride=rows), :]
        for k in range(LINKS):
            slot = linked[face][k]
            partial = stepped[slot, rim_rows, :]
            inner = stepped[slot, pl.ds(rows + inner_r, depth, stride=rows), :]
            below = jnp.broadcast_to(now[slot, pl.ds(r, 1), :], (depth, cols))
            above = jnp.broadcast_to(now[slot, pl.ds(top + r, 1), :], (depth, cols))
            inner = inner + jnp.where(edge_row == 0, below, jnp.where(edge_row == depth - 1, above, 0.0))
            rest = rest - partial * partial
            out[x_rows(0, k, depth), :] = now[slot, rim_rows, :]
            out[x_rows(1, k, depth), :] = partial
            out[x_rows(2, k, depth), :] = inner
        corners = [jnp.zeros((depth, cols), jnp.float32)] * 4
        for k in range(LINKS):
            for side in range(2):
                slot = linked[2 + side][k]
                for i, ref in enumerate((stepped, now)):
                    place = (2 * i + side) * LINKS + k
                    moved = spin(ref[slot, rim_rows, :], place - side * (cols - 1))
                    corners[2 * i + side] = jnp.where(edge_lane == place, moved, corners[2 * i + side])
        out[pl.ds(end, depth), :] = (corners[0] + corners[1]) + (corners[2] + corners[3])
        out[pl.ds(end + depth, depth), :] = rest
        if out.shape[0] > end + 2 * depth:
            left = out.shape[0] - end - 2 * depth
            out[pl.ds(end + 2 * depth, left), :] = jnp.zeros((left, cols), jnp.float32)


def y_kernel(slots, depth, rows, cols, now, stepped, squares, lists, y_low, y_up):
    top = (depth + 1) * rows
    _, lane = row_and_lane(rows, cols)
    low, up = (lambda k: lists[2 * SPAN + k]), (lambda k: lists[3 * SPAN + k])
    rims = gather_columns(now, low, up, depth, rows, cols)
    *partials, inner_low, inner_up = gather_columns(stepped, low, up, depth, rows, cols, beside=True)
    frozen = [jnp.zeros((rows, cols), jnp.float32)] * 2
    totals = [jnp.zeros((rows, cols), jnp.float32)] * 2
    for k in range(LINKS):
        for z, at in ((0, 0), (depth - 1, top)):
            place = GROUP * k + z
            at = pl.ds(at, rows)
            moved = spin(jnp.where(lane < cols // 2, now[low(k), at, :], now[up(k), at, :]), place)
            for side in range(2):
                frozen[side] = jnp.where(lane == (place - side) % cols, moved, frozen[side])
    for z in range(depth):
        place = LINKS * GROUP + z
        moved = spin(tile(squares, z, rows), place)
        for side in range(2):
            totals[side] = jnp.where(lane == place - side, moved, totals[side])
    for side, out, inner in ((0, y_low, inner_low), (1, y_up, inner_up)):
        rest = spin(totals[side], side) - group_sum(partials[side] * partials[side])
        out[pl.ds(0, rows), :] = rims[side]
        out[pl.ds(rows, rows), :] = partials[side]
        out[pl.ds(2 * rows, rows), :] = jnp.where(in_last_group(lane), rest, inner + spin(frozen[side], side))


def in_last_group(lane):
    return (lane >= LINKS * GROUP) & (lane < (LINKS + 1) * GROUP)


def tile(ref, i, rows):
    return ref[pl.ds(i * rows, rows), :]


def y_faces(ref, tiles, lists, depth, rows, cols, replace=False):
    _, lane = row_and_lane(rows, cols)
    ats = [pl.ds((z + 1) * rows, rows) for z in range(depth)]

    def link(k, tiles):
        linked = [lists[(2 + side) * SPAN + k] for side in range(2)]
        old = [[ref[slot, at, :] for at in ats] for slot in linked]
        for side in range(2):
            c = side * (cols - 1)
            for z in range(depth):
                moved = spin(tiles[side], c - z)
                new = jnp.where(lane == c, moved if replace else old[side][z] + moved, old[side][z])
                ref[linked[side], ats[z], :] = new
        return tuple(spin(tile, -GROUP) for tile in tiles)

    lax.fori_loop(0, LINKS, link, tuple(tiles))


def second_kernel(
    slots, depth, rows, cols, stepped_in, y_low_own, y_up_own, y_low, y_up, lists, now, later
):
    for s in range(slots):
        for at in (0, (depth + 1) * rows):
            later[s, pl.ds(at, rows), :] = now[s, pl.ds(at, rows), :]
    later[slots] = jnp.zeros(((depth + 2) * rows, cols), jnp.float32)
    pairs = ((y_low_own, y_low), (y_up_own, y_up))
    own_one = [tile(own, 1, rows) + RATE * tile(got, 0, rows) for own, got in pairs]
    one = [RATE * (tile(got, 1, rows) + RATE * tile(own, 0, rows)) for own, got in pairs]
    y_faces(now, own_one, lists, depth, rows, cols, replace=True)
    step(now, later, slots, depth, rows, cols)
    y_faces(later, one, lists, depth, rows, cols)


def x_rims(own, got, k, depth):
    zero, one = x_rows(0, k, depth), x_rows(1, k, depth)
    return own[one, :] + RATE * got[zero, :], got[one, :] + RATE * own[zero, :]


def change_kernel(depth, cols, own, got, before, out):
    change = jnp.zeros((depth, cols), jnp.float32)
    for k in range(LINKS):
        own_one, _ = x_rims(own, got, k, depth)
        partial = own[x_rows(1, k, depth), :]
        change = change + (own_one * own_one - partial * partial)
    out[pl.ds(0, depth), :] = change
    out[pl.ds(depth, depth), :] = got[pl.ds(3 * LINKS * depth, depth), :]
    out[pl.ds(2 * depth, depth), :] = own[pl.ds(3 * LINKS * depth, depth), :]


def both_changes_kernel(depth, cols, own, got, before, out):
    out[pl.ds(0, 3 * depth), :] = before[...]
    change_kernel(depth, cols, own, got, None, out.at[pl.ds(3 * depth, 3 * depth), :])


def x_rim_step(padded, face, k, one, factor, outer, depth, cols):
    _, lane = row_and_lane(depth, cols)
    z_sum = padded[face, pl.ds(k, depth, stride=SPAN), :] + padded[face, pl.ds(2 * SPAN + k, depth, stride=SPAN), :]
    y_sum = jnp.where(lane == 0, 0.0, pltpu.roll(one, 1, 1)) + jnp.where(
        lane == cols - 1, 0.0, pltpu.roll(one, cols - 1, 1)
    )
    return RATE * (one * (factor + one * one) + (outer + (z_sum + y_sum)))


def y_rim_step(one, factor, outer):
    rows, cols = one.shape
    row, _ = row_and_lane(rows, cols)
    x_sum = jnp.where(row == 0, 0.0, pltpu.roll(one, 1, 0)) + jnp.where(
        row == rows - 1, 0.0, pltpu.roll(one, rows - 1, 0)
    )
    z_sum = spin(one, 1) + spin(one, -1)
    return RATE * (one * (factor + one * one) + (outer + (x_sum + z_sum)))


def third_kernel(
    slots, depth, rows, cols,
    now, later_in, x_low_own, x_up_own, x_low, x_up, changes, lists,
    later, last,
    x_own_one,
):
    last[slots] = jnp.zeros(((depth + 2) * rows, cols), jnp.float32)
    x_own_one[...] = jnp.zeros(x_own_one.shape, jnp.float32)
    for face, own, got in ((0, x_low_own, x_low), (1, x_up_own, x_up)):
        r, inner_r = (0, 1) if face == 0 else (rows - 1, rows - 2)
        rim_rows = pl.ds(rows + r, depth, stride=rows)
        inner_rows = pl.ds(rows + inner_r, depth, stride=rows)
        rims = [x_rims(own, got, k, depth) for k in range(LINKS)]
        for k in range(LINKS):
            x_own_one[face, pl.ds(SPAN + k, depth, stride=SPAN), :] = rims[k][0]

        change = changes[pl.ds(3 * face * depth, depth), :]
        scaled = 0.15 * change
        parts = [change, None, None, None]
        for first in range(0, slots, 4):
            rim = [now[first + i, rim_rows, :] for i in range(4)]
            old = [later[first + i, rim_rows, :] for i in range(4)]
            for i in range(4):
                parts[i] = rim[i] * rim[i] if parts[i] is None else parts[i] + rim[i] * rim[i]
                later[first + i, rim_rows, :] = old[i] - scaled * rim[i]
        factor = 4.5 - 1.5 * ((parts[0] + parts[1]) + (parts[2] + parts[3]))

        linked = [lists[face * SPAN + k] for k in range(LINKS)]
        beside = [later[slot, inner_rows, :] for slot in linked]
        two = []
        for k in range(LINKS):
            outer = own[x_rows(2, k, depth), :] + rims[k][1]
            two.append(x_rim_step(x_own_one, face, k, rims[k][0], factor, outer, depth, cols))
        for k in range(LINKS):
            later[linked[k], rim_rows, :] = two[k]
            later[linked[k], inner_rows, :] = beside[k] + RATE * RATE * got[x_rows(0, k, depth), :]

    step(later, last, slots, depth, rows, cols)


def rims_kernel(
    slots, depth, rows, cols,
    last_in, x_low_own, x_up_own, x_low, x_up, y_low_own, y_up_own, y_low, y_up, lists,
    last, result,
    x_one, sent,
):
    _, lane = row_and_lane(rows, cols)

    def each_unlinked(act):
        for s in range(slots):
            copy = pltpu.make_async_copy(last.at[s, pl.ds(rows, depth * rows), :], result.at[s], sent)
            pl.when(lists[4 * SPAN + s] == 0)(getattr(copy, act))

    each_unlinked("start")
    x_one[...] = jnp.zeros(x_one.shape, jnp.float32)
    for face, own, got in ((0, x_low_own, x_low), (1, x_up_own, x_up)):
        rims = [x_rims(own, got, k, depth) for k in range(LINKS)]
        total = got[pl.ds((3 * LINKS + 1) * depth, depth), :]
        for k in range(LINKS):
            total = total + rims[k][1] * rims[k][1]
            x_one[face, pl.ds(SPAN + k, depth, stride=SPAN), :] = rims[k][1]
        factor = 4.5 - 1.5 * total
        rim_rows = pl.ds(rows + (0 if face == 0 else rows - 1), depth, stride=rows)
        linked = [lists[face * SPAN + k] for k in range(LINKS)]
        old = [last[slot, rim_rows, :] for slot in linked]
        for k in range(LINKS):
            outer = got[x_rows(2, k, depth), :] + rims[k][0]
            two = x_rim_step(x_one, face, k, rims[k][1], factor, outer, depth, cols)
            last[linked[k], rim_rows, :] = old[k] + RATE * two

    twos = []
    for own, got in ((y_low_own, y_low), (y_up_own, y_up)):
        own_one = tile(own, 1, rows) + RATE * tile(got, 0, rows)
        one = tile(got, 1, rows) + RATE * tile(own, 0, rows)
        inner = tile(got, 2, rows)
        factor = 4.5 - 1.5 * group_sum(one * one + jnp.where(in_last_group(lane), inner, 0.0))
        twos.append(RATE * y_rim_step(one, factor, inner + own_one))
    y_faces(last, twos, lists, depth, rows, cols)
    each_unlinked("wait")


def last_kernel(
    slots, depth, rows, cols,
    last_in, result_in, x_low_own, x_up_own, x_low, x_up, from_left, from_right, lists,
    last, result,
    sent,
):
    _, lane = row_and_lane(depth, cols)
    scale = -1.5 * RATE * RATE
    passed_on = (from_left, from_right)
    part = lambda ref, i: ref[pl.ds(i * depth, depth), :]
    corner_cells = lambda ref: ref[pl.ds(3 * LINKS * depth, depth), :]

    def each_linked(face, act):
        for k in range(LINKS):
            slot = lists[face * SPAN + k]

            @pl.when(slot < slots)
            def _():
                copy = pltpu.make_async_copy(last.at[slot, pl.ds(rows, depth * rows), :], result.at[slot], sent)
                getattr(copy, act)()

    for face, own, got in ((0, x_low_own, x_low), (1, x_up_own, x_up)):
        total = jnp.zeros((depth, cols), jnp.float32)
        for side in range(2):
            place = side * LINKS
            term = RATE * spin(part(passed_on[side], 3 * face + 1), place - (3 - side) * LINKS)
            term = term * (2.0 * corner_cells(got) + term)
            term = jnp.where((lane >= place) & (lane < place + LINKS), term, 0.0)
            column = jnp.sum(term, axis=1, keepdims=True)
            total = total + jnp.where(lane == side * (cols - 1), column, 0.0)
        total = scale * total
        rim_rows = pl.ds(rows + (0 if face == 0 else rows - 1), depth, stride=rows)
        linked = [lists[face * SPAN + k] for k in range(LINKS)]
        old = [last[slot, rim_rows, :] for slot in linked]
        for k in range(LINKS):
            _, one = x_rims(own, got, k, depth)
            last[linked[k], rim_rows, :] = old[k] + total * one
        each_linked(face, "start")

    for side in range(2):
        c = side * (cols - 1)
        linked = [lists[(2 + side) * SPAN + k] for k in range(LINKS)]
        for face, own in ((0, x_low_own), (1, x_up_own)):
            place = (1 - side) * LINKS
            one = part(passed_on[side], 3 * face + 2) + RATE * spin(corner_cells(own), place - (2 + side) * LINKS)
            change = jnp.where(lane == cols - 1 - c, part(passed_on[side], 3 * face), 0.0)
            one = scale * one * jnp.sum(change, axis=1, keepdims=True)
            rim_rows = pl.ds(rows + (0 if face == 0 else rows - 1), depth, stride=rows)
            old = [last[slot, rim_rows, :] for slot in linked]
            for k in range(LINKS):
                last[linked[k], rim_rows, :] = old[k] + jnp.where(lane == c, spin(one, c - place - k), 0.0)
        each_linked(2 + side, "start")
    for face in range(4):
        each_linked(face, "wait")


def shifted(block, axis, distance):
    size = lax.axis_size(axis)
    return lax.ppermute(block, axis, [((i - distance) % size, i) for i in range(size)])


def on_device(order_params, grain_ids, channel_maps, zplanes):
    slots, depth, rows, cols = order_params.shape
    f32 = jnp.float32
    shape = jax.ShapeDtypeStruct
    padded = pltpu.VMEM((slots + 1, (depth + 2) * rows, cols), f32)
    planes = pltpu.VMEM((depth * rows, cols), f32)
    x_pack = shape((-(-(3 * LINKS + 2) * depth // rows) * rows, cols), f32)
    y_pack = shape((3 * rows, cols), f32)
    rims = pltpu.VMEM((2, (depth + 2) * SPAN, cols), f32)
    vmem = pl.BlockSpec(memory_space=pltpu.VMEM)
    smem = pl.BlockSpec(memory_space=pltpu.SMEM)
    hbm = pl.BlockSpec(memory_space=pltpu.HBM)
    params = pltpu.CompilerParams(vmem_limit_bytes=24 * 1024 * 1024)
    field = order_params.reshape(slots, depth * rows, cols)
    sizes = (slots, depth, rows, cols)
    work = pl.CostEstimate(flops=20 * field.size, bytes_accessed=2 * 4 * field.size, transcendentals=0)

    now, stepped, squares, x_low, x_up, lists = pl.pallas_call(
        functools.partial(first_kernel, *sizes),
        out_shape=[padded, padded, planes, x_pack, x_pack, shape((4 * SPAN + slots,), jnp.int32)],
        in_specs=[hbm] * 4,
        out_specs=[vmem] * 5 + [smem],
        scratch_shapes=[
            pltpu.VMEM(zplanes.shape, jnp.int32),
            pltpu.SMEM(grain_ids.shape, jnp.int32),
            pltpu.SMEM(channel_maps.shape, jnp.int32),
            pltpu.SMEM((2 * (slots + 1),), jnp.int32),
            pltpu.SemaphoreType.DMA((3 + depth // PART,)),
        ],
        compiler_params=params,
        name="first_step",
    )(*(pltpu.with_memory_space_constraint(x, pltpu.HBM) for x in (field, zplanes, grain_ids, channel_maps)))

    from_low = shifted(x_up, "gx", 1)
    from_up = shifted(x_low, "gx", -1)

    y_low, y_up = pl.pallas_call(
        functools.partial(y_kernel, *sizes),
        out_shape=[y_pack, y_pack],
        in_specs=[vmem] * 3 + [smem],
        out_specs=[vmem] * 2,
        compiler_params=params,
        cost_estimate=work,
        name="y_rims",
    )(now, stepped, squares, lists)

    from_right = shifted(y_low, "gy", -1)
    from_left = shifted(y_up, "gy", 1)

    fixed, later = pl.pallas_call(
        functools.partial(second_kernel, *sizes),
        out_shape=[padded, padded],
        in_specs=[vmem] * 5 + [smem],
        out_specs=[vmem] * 2,
        input_output_aliases={0: 0},
        compiler_params=params,
        cost_estimate=work,
        name="second_step",
    )(stepped, y_low, y_up, from_left, from_right, lists)

    changes = later
    for body, own, got, name in (
        (change_kernel, x_low, from_low, "corners_low"),
        (both_changes_kernel, x_up, from_up, "corners_up"),
    ):
        changes = pl.pallas_call(
            functools.partial(body, depth, cols),
            out_shape=shape(((3 if body is change_kernel else 6) * depth, cols), f32),
            in_specs=[vmem] * 3,
            out_specs=vmem,
            compiler_params=params,
            name=name,
        )(own, got, changes)

    changes_from_right = shifted(changes, "gy", -1)
    changes_from_left = shifted(changes, "gy", 1)

    _, last = pl.pallas_call(
        functools.partial(third_kernel, *sizes),
        out_shape=[padded, padded],
        in_specs=[vmem] * 7 + [smem],
        out_specs=[vmem] * 2,
        scratch_shapes=[rims],
        input_output_aliases={1: 0},
        compiler_params=params,
        name="third_step",
    )(
        fixed, later, x_low, x_up, from_low, from_up, changes, lists,
    )

    out_shape = [padded, pltpu.HBM(field.shape, f32)]
    last, result = pl.pallas_call(
        functools.partial(rims_kernel, *sizes),
        out_shape=out_shape,
        in_specs=[vmem] * 9 + [smem],
        out_specs=[vmem, hbm],
        scratch_shapes=[rims, pltpu.SemaphoreType.DMA],
        input_output_aliases={0: 0},
        compiler_params=params,
        name="rims",
    )(last, x_low, x_up, from_low, from_up, y_low, y_up, from_left, from_right, lists)

    _, result = pl.pallas_call(
        functools.partial(last_kernel, *sizes),
        out_shape=out_shape,
        in_specs=[vmem, hbm] + [vmem] * 6 + [smem],
        out_specs=[vmem, hbm],
        scratch_shapes=[pltpu.SemaphoreType.DMA],
        input_output_aliases={0: 0, 1: 1},
        compiler_params=params,
        name="corners_last",
    )(last, result, x_low, x_up, from_low, from_up, changes_from_left, changes_from_right, lists)
    return result.reshape(order_params.shape)


def solution(mesh):
    in_specs = (
        P(None, None, "gx", "gy"),
        P("gx", "gy", None),
        P("gx", "gy", None, None),
        P(None, "gx", "gy"),
    )
    return jax.shard_map(
        on_device, mesh=mesh, in_specs=in_specs, out_specs=P(None, None, "gx", "gy"), check_vma=False
    )
```

```python
import functools

import jax
import jax.numpy as jnp
from jax import lax
from jax.experimental import pallas as pl
from jax.experimental.pallas import tpu as pltpu
from jax.sharding import PartitionSpec as P


LINKS = 6
SPAN = 8
GROUP = 16
RATE = 0.1
PART = 4


def row_and_lane(rows, cols):
    row = lax.broadcasted_iota(jnp.int32, (rows, cols), 0)
    lane = lax.broadcasted_iota(jnp.int32, (rows, cols), 1)
    return row, lane


def spin(tile, amount):
    cols = tile.shape[1]
    amount = amount % cols
    return tile if amount == 0 else pltpu.roll(tile, amount, 1)


def group_sum(tile):
    shift = GROUP
    while shift < tile.shape[1]:
        tile = tile + spin(tile, shift)
        shift *= 2
    return tile


def step(src, dst, slots, depth, rows, cols, squares=None, wait=None):
    row, lane = row_and_lane(rows, cols)
    first_row, last_row = row == 0, row == rows - 1
    first_lane, last_lane = lane == 0, lane == cols - 1

    def add(parts, s, term):
        parts[s % 4] = term if parts[s % 4] is None else parts[s % 4] + term

    def total(parts):
        return (parts[0] + parts[1]) + (parts[2] + parts[3])

    def at(z):
        return pl.ds((z + 1) * rows, rows)

    def layer(z, factor):
        following, parts = [None] * 4, [None] * 4
        for s in range(slots):
            v, below, above = src[s, at(z), :], src[s, at(z - 1), :], src[s, at(z + 1), :]
            add(following, s, above * above)
            base = (z + 1) * rows
            x_sum = jnp.where(first_row, 0.0, src[s, pl.ds(base - 1, rows), :]) + jnp.where(
                last_row, 0.0, src[s, pl.ds(base + 1, rows), :]
            )
            y_sum = jnp.where(first_lane, 0.0, pltpu.roll(v, 1, 1)) + jnp.where(
                last_lane, 0.0, pltpu.roll(v, cols - 1, 1)
            )
            new = RATE * (v * (factor + v * v) + ((x_sum + y_sum) + (below + above)))
            dst[s, at(z), :] = new
            if squares is not None:
                add(parts, s, new * new)
        if squares is not None:
            squares[pl.ds(z * rows, rows), :] = total(parts)
        return 4.5 - 1.5 * total(following)

    first = [None] * 4
    for s in range(slots):
        v = src[s, at(0), :]
        add(first, s, v * v)
    factor = 4.5 - 1.5 * total(first)
    for z in range(depth):
        if wait is not None and z % PART == PART - 1 and z < depth - 1:
            wait(z // PART + 1)
        factor = layer(z, factor)


def gather_columns(ref, low, up, depth, rows, cols, beside=False):
    _, lane = row_and_lane(rows, cols)
    shifts = (0, -1, 1, -2) if beside else (0, -1)
    results = [jnp.zeros((rows, cols), jnp.float32)] * len(shifts)
    for k in range(LINKS):
        parts = [jnp.zeros((rows, cols), jnp.float32)] * len(shifts)
        for z in range(depth):
            at = pl.ds((z + 1) * rows, rows)
            place = GROUP * k + z
            moved = spin(jnp.where(lane < cols // 2, ref[low[k], at, :], ref[up[k], at, :]), place)
            for i, shift in enumerate(shifts):
                parts[i] = jnp.where(lane == (place + shift) % cols, moved, parts[i])
        results = [result + part for result, part in zip(results, parts)]
    return [spin(result, -shift) for result, shift in zip(results, shifts)]


def x_rows(part, k, depth):
    return pl.ds(part * LINKS * depth + k, depth, stride=LINKS)


def first_kernel(
    slots, depth, rows, cols,
    field, planes, grains, maps,
    now, stepped, squares, x_low, x_up, lists,
    planes_in, grains_in, maps_in, inverse, arrived,
):
    copies = [
        pltpu.make_async_copy(maps, maps_in, arrived.at[0]),
        pltpu.make_async_copy(grains, grains_in, arrived.at[1]),
        pltpu.make_async_copy(planes, planes_in, arrived.at[2]),
    ]
    part = PART * rows

    def field_part(i):
        to = pl.ds(i * part + rows, part)
        source = field.at[:, pl.ds(i * part, part), :]
        return pltpu.make_async_copy(source, now.at[pl.ds(0, slots), to, :], arrived.at[3 + i])

    for copy in copies:
        copy.start()
    for i in range(depth // PART):
        field_part(i).start()
    for ref in (now, stepped):
        ref[slots] = jnp.zeros(((depth + 2) * rows, cols), jnp.float32)
    for face in range(4):
        for place in range(SPAN):
            lists[face * SPAN + place] = slots
    for t in range(slots + 1):
        inverse[t] = slots
        inverse[slots + 1 + t] = slots

    copies[0].wait()
    for s in range(slots):
        for face in (0, 2):
            partner = maps_in[0, 0, face, s]
            inverse[face // 2 * (slots + 1) + jnp.where(partner >= 0, partner, slots)] = s
    counts = [jnp.int32(face * SPAN) for face in range(4)]
    for s in range(slots):
        partners = [maps_in[0, 0, face, s] for face in range(4)]
        best = jnp.maximum(jnp.maximum(partners[0], partners[1]), jnp.maximum(partners[2], partners[3]))
        lists[4 * SPAN + s] = (best >= 0).astype(jnp.int32)
        for face in range(4):
            if face in (1, 3):
                valid = partners[face] >= 0
                slot = jnp.where(valid, s, slots)
            else:
                slot = inverse[face // 2 * (slots + 1) + s]
                valid = slot < slots
            lists[counts[face]] = slot
            counts[face] = counts[face] + valid.astype(jnp.int32)

    top = (depth + 1) * rows
    copies[1].wait()
    copies[2].wait()
    for s in range(slots):
        grain = grains_in[0, 0, s]
        below = jnp.where(planes_in[0] == grain, 1.0, 0.0)
        above = jnp.where(planes_in[1] == grain, 1.0, 0.0)
        for ref in (now, stepped):
            ref[s, pl.ds(0, rows), :] = below
            ref[s, pl.ds(top, rows), :] = above
    field_part(0).wait()

    step(now, stepped, slots, depth, rows, cols, squares, lambda i: field_part(i).wait())

    linked = [[lists[face * SPAN + k] for k in range(LINKS)] for face in range(4)]
    end = 3 * LINKS * depth
    edge_row, edge_lane = row_and_lane(depth, cols)
    for face, out in ((1, x_up), (0, x_low)):
        r, inner_r = (0, 1) if face == 0 else (rows - 1, rows - 2)
        rim_rows = pl.ds(rows + r, depth, stride=rows)
        rest = squares[pl.ds(r, depth, stride=rows), :]
        for k in range(LINKS):
            slot = linked[face][k]
            partial = stepped[slot, rim_rows, :]
            inner = stepped[slot, pl.ds(rows + inner_r, depth, stride=rows), :]
            below = jnp.broadcast_to(now[slot, pl.ds(r, 1), :], (depth, cols))
            above = jnp.broadcast_to(now[slot, pl.ds(top + r, 1), :], (depth, cols))
            inner = inner + jnp.where(edge_row == 0, below, jnp.where(edge_row == depth - 1, above, 0.0))
            rest = rest - partial * partial
            out[x_rows(0, k, depth), :] = now[slot, rim_rows, :]
            out[x_rows(1, k, depth), :] = partial
            out[x_rows(2, k, depth), :] = inner
        corners = [jnp.zeros((depth, cols), jnp.float32)] * 4
        for k in range(LINKS):
            for side in range(2):
                slot = linked[2 + side][k]
                for i, ref in enumerate((stepped, now)):
                    place = (2 * i + side) * LINKS + k
                    moved = spin(ref[slot, rim_rows, :], place - side * (cols - 1))
                    corners[2 * i + side] = jnp.where(edge_lane == place, moved, corners[2 * i + side])
        out[pl.ds(end, depth), :] = (corners[0] + corners[1]) + (corners[2] + corners[3])
        out[pl.ds(end + depth, depth), :] = rest
        if out.shape[0] > end + 2 * depth:
            left = out.shape[0] - end - 2 * depth
            out[pl.ds(end + 2 * depth, left), :] = jnp.zeros((left, cols), jnp.float32)


def y_kernel(slots, depth, rows, cols, now, stepped, squares, lists, y_low, y_up):
    top = (depth + 1) * rows
    _, lane = row_and_lane(rows, cols)
    low, up = ([lists[face * SPAN + k] for k in range(LINKS)] for face in (2, 3))
    rims = gather_columns(now, low, up, depth, rows, cols)
    *partials, inner_low, inner_up = gather_columns(stepped, low, up, depth, rows, cols, beside=True)
    frozen = [jnp.zeros((rows, cols), jnp.float32)] * 2
    totals = [jnp.zeros((rows, cols), jnp.float32)] * 2
    for k in range(LINKS):
        for z, at in ((0, 0), (depth - 1, top)):
            place = GROUP * k + z
            at = pl.ds(at, rows)
            moved = spin(jnp.where(lane < cols // 2, now[low[k], at, :], now[up[k], at, :]), place)
            for side in range(2):
                frozen[side] = jnp.where(lane == (place - side) % cols, moved, frozen[side])
    for z in range(depth):
        place = LINKS * GROUP + z
        moved = spin(tile(squares, z, rows), place)
        for side in range(2):
            totals[side] = jnp.where(lane == place - side, moved, totals[side])
    for side, out, inner in ((0, y_low, inner_low), (1, y_up, inner_up)):
        rest = spin(totals[side], side) - group_sum(partials[side] * partials[side])
        out[pl.ds(0, rows), :] = rims[side]
        out[pl.ds(rows, rows), :] = partials[side]
        out[pl.ds(2 * rows, rows), :] = jnp.where(in_last_group(lane), rest, inner + spin(frozen[side], side))


def in_last_group(lane):
    return (lane >= LINKS * GROUP) & (lane < (LINKS + 1) * GROUP)


def tile(ref, i, rows):
    return ref[pl.ds(i * rows, rows), :]


def y_faces(ref, tiles, lists, depth, rows, cols, replace=False, done=None):
    _, lane = row_and_lane(rows, cols)
    for k in range(LINKS):
        for side in range(2):
            c = side * (cols - 1)
            slot = lists[(2 + side) * SPAN + k]
            ats = [pl.ds((z + 1) * rows, rows) for z in range(depth)]
            old = [ref[slot, at, :] for at in ats]
            for z in range(depth):
                moved = spin(tiles[side], c - GROUP * k - z)
                ref[slot, ats[z], :] = jnp.where(lane == c, moved if replace else old[z] + moved, old[z])
            if done is not None:
                done(slot)


def second_kernel(
    slots, depth, rows, cols, stepped_in, y_low_own, y_up_own, y_low, y_up, lists, now, later
):
    for s in range(slots):
        for at in (0, (depth + 1) * rows):
            later[s, pl.ds(at, rows), :] = now[s, pl.ds(at, rows), :]
    later[slots] = jnp.zeros(((depth + 2) * rows, cols), jnp.float32)
    pairs = ((y_low_own, y_low), (y_up_own, y_up))
    own_one = [tile(own, 1, rows) + RATE * tile(got, 0, rows) for own, got in pairs]
    one = [RATE * (tile(got, 1, rows) + RATE * tile(own, 0, rows)) for own, got in pairs]
    y_faces(now, own_one, lists, depth, rows, cols, replace=True)
    step(now, later, slots, depth, rows, cols)
    y_faces(later, one, lists, depth, rows, cols)


def x_rims(own, got, k, depth):
    zero, one = x_rows(0, k, depth), x_rows(1, k, depth)
    return own[one, :] + RATE * got[zero, :], got[one, :] + RATE * own[zero, :]


def change_kernel(depth, cols, own, got, before, out):
    change = jnp.zeros((depth, cols), jnp.float32)
    for k in range(LINKS):
        own_one, _ = x_rims(own, got, k, depth)
        partial = own[x_rows(1, k, depth), :]
        change = change + (own_one * own_one - partial * partial)
    out[pl.ds(0, depth), :] = change
    out[pl.ds(depth, depth), :] = got[pl.ds(3 * LINKS * depth, depth), :]


def both_changes_kernel(depth, cols, own, got, before, out):
    out[pl.ds(0, 2 * depth), :] = before[...]
    change_kernel(depth, cols, own, got, None, out.at[pl.ds(2 * depth, 2 * depth), :])


def x_rim_step(padded, face, k, one, factor, outer, depth, cols):
    _, lane = row_and_lane(depth, cols)
    z_sum = padded[face, pl.ds(k, depth, stride=SPAN), :] + padded[face, pl.ds(2 * SPAN + k, depth, stride=SPAN), :]
    y_sum = jnp.where(lane == 0, 0.0, pltpu.roll(one, 1, 1)) + jnp.where(
        lane == cols - 1, 0.0, pltpu.roll(one, cols - 1, 1)
    )
    return RATE * (one * (factor + one * one) + (outer + (z_sum + y_sum)))


def y_rim_step(one, factor, outer):
    rows, cols = one.shape
    row, _ = row_and_lane(rows, cols)
    x_sum = jnp.where(row == 0, 0.0, pltpu.roll(one, 1, 0)) + jnp.where(
        row == rows - 1, 0.0, pltpu.roll(one, rows - 1, 0)
    )
    z_sum = spin(one, 1) + spin(one, -1)
    return RATE * (one * (factor + one * one) + (outer + (x_sum + z_sum)))


def third_kernel(
    slots, depth, rows, cols,
    now, later_in, x_low_own, x_up_own, x_low, x_up, changes, lists,
    later, last,
    x_own_one,
):
    last[slots] = jnp.zeros(((depth + 2) * rows, cols), jnp.float32)
    x_own_one[...] = jnp.zeros(x_own_one.shape, jnp.float32)
    for face, own, got in ((0, x_low_own, x_low), (1, x_up_own, x_up)):
        r, inner_r = (0, 1) if face == 0 else (rows - 1, rows - 2)
        rim_rows = pl.ds(rows + r, depth, stride=rows)
        inner_rows = pl.ds(rows + inner_r, depth, stride=rows)
        rims = [x_rims(own, got, k, depth) for k in range(LINKS)]
        for k in range(LINKS):
            x_own_one[face, pl.ds(SPAN + k, depth, stride=SPAN), :] = rims[k][0]

        change = changes[pl.ds(2 * face * depth, depth), :]
        scaled = 0.15 * change
        parts = [change, None, None, None]
        for first in range(0, slots, 4):
            rim = [now[first + i, rim_rows, :] for i in range(4)]
            old = [later[first + i, rim_rows, :] for i in range(4)]
            for i in range(4):
                parts[i] = rim[i] * rim[i] if parts[i] is None else parts[i] + rim[i] * rim[i]
                later[first + i, rim_rows, :] = old[i] - scaled * rim[i]
        factor = 4.5 - 1.5 * ((parts[0] + parts[1]) + (parts[2] + parts[3]))

        linked = [lists[face * SPAN + k] for k in range(LINKS)]
        beside = [later[slot, inner_rows, :] for slot in linked]
        two = []
        for k in range(LINKS):
            outer = own[x_rows(2, k, depth), :] + rims[k][1]
            two.append(x_rim_step(x_own_one, face, k, rims[k][0], factor, outer, depth, cols))
        for k in range(LINKS):
            later[linked[k], rim_rows, :] = two[k]
            later[linked[k], inner_rows, :] = beside[k] + RATE * RATE * got[x_rows(0, k, depth), :]

    step(later, last, slots, depth, rows, cols)


def last_kernel(
    slots, depth, rows, cols,
    last_in, x_low_own, x_up_own, x_low, x_up, y_low_own, y_up_own, y_low, y_up, from_left, from_right,
    lists,
    last, result,
    x_one, sent,
):
    whole = last.at[pl.ds(0, slots), pl.ds(rows, depth * rows), :]

    def send(slot):
        pltpu.make_async_copy(last.at[slot, pl.ds(rows, depth * rows), :], result.at[slot], sent).start()

    def send_linked(slot):
        pl.when(slot < slots)(lambda: send(slot))

    for s in range(slots):
        pl.when(lists[4 * SPAN + s] == 0)(functools.partial(send, s))

    row, lane = row_and_lane(rows, cols)
    _, flat_lane = row_and_lane(depth, cols)
    tall_row, tall_lane = row_and_lane(GROUP, cols)
    block = LINKS * depth
    passed_on = (from_left, from_right)
    x_one[...] = jnp.zeros(x_one.shape, jnp.float32)
    for face, own, got in ((0, x_low_own, x_low), (1, x_up_own, x_up)):
        rims = [x_rims(own, got, k, depth) for k in range(LINKS)]
        total = got[pl.ds(3 * block + depth, depth), :]
        for k in range(LINKS):
            total = total + rims[k][1] * rims[k][1]
            x_one[face, pl.ds(SPAN + k, depth, stride=SPAN), :] = rims[k][1]
        corners = got[pl.ds(3 * block, depth), :]
        for side in range(2):
            place = side * LINKS
            came_from = (3 - side) * LINKS
            term = RATE * spin(passed_on[side][pl.ds((2 * face + 1) * depth, depth), :], place - came_from)
            term = term * (2.0 * corners + term)
            term = jnp.where((flat_lane >= place) & (flat_lane < place + LINKS), term, 0.0)
            column = jnp.sum(term, axis=1, keepdims=True)
            total = total + jnp.where(flat_lane == side * (cols - 1), column, 0.0)
        factor = 4.5 - 1.5 * total
        rim_rows = pl.ds(rows + (0 if face == 0 else rows - 1), depth, stride=rows)
        linked = [lists[face * SPAN + k] for k in range(LINKS)]
        old = [last[slot, rim_rows, :] for slot in linked]
        for k in range(LINKS):
            outer = got[x_rows(2, k, depth), :] + rims[k][0]
            two = x_rim_step(x_one, face, k, rims[k][1], factor, outer, depth, cols)
            last[linked[k], rim_rows, :] = old[k] + RATE * two
        for slot in linked:
            send_linked(slot)

    twos = []
    for side, own, got in ((0, y_low_own, y_low), (1, y_up_own, y_up)):
        c = side * (cols - 1)
        own_one = tile(own, 1, rows) + RATE * tile(got, 0, rows)
        one = tile(got, 1, rows) + RATE * tile(own, 0, rows)
        inner = tile(got, 2, rows)
        squares = one * one + jnp.where(in_last_group(lane), inner, 0.0)
        for face in range(2):
            change = passed_on[side][pl.ds(2 * face * depth, depth), :]
            column = jnp.sum(jnp.where(flat_lane == cols - 1 - c, change, 0.0), axis=1, keepdims=True)
            line = jnp.sum(jnp.where(tall_row == tall_lane, 1.0, 0.0)[:depth] * column, axis=0, keepdims=True)
            at_row = row == (0 if face == 0 else rows - 1)
            squares = squares + jnp.where(at_row, jnp.broadcast_to(line, (rows, cols)), 0.0)
        factor = 4.5 - 1.5 * group_sum(squares)
        twos.append(RATE * y_rim_step(one, factor, inner + own_one))
    y_faces(last, twos, lists, depth, rows, cols, done=send_linked)
    pltpu.make_async_copy(whole, result, sent).wait()


def shifted(block, axis, distance):
    size = lax.axis_size(axis)
    return lax.ppermute(block, axis, [((i - distance) % size, i) for i in range(size)])


def on_device(order_params, grain_ids, channel_maps, zplanes):
    slots, depth, rows, cols = order_params.shape
    f32 = jnp.float32
    shape = jax.ShapeDtypeStruct
    padded = pltpu.VMEM((slots + 1, (depth + 2) * rows, cols), f32)
    planes = pltpu.VMEM((depth * rows, cols), f32)
    x_pack = shape((-(-(3 * LINKS + 2) * depth // rows) * rows, cols), f32)
    y_pack = shape((3 * rows, cols), f32)
    rims = pltpu.VMEM((2, (depth + 2) * SPAN, cols), f32)
    vmem = pl.BlockSpec(memory_space=pltpu.VMEM)
    smem = pl.BlockSpec(memory_space=pltpu.SMEM)
    hbm = pl.BlockSpec(memory_space=pltpu.HBM)
    params = pltpu.CompilerParams(vmem_limit_bytes=24 * 1024 * 1024)
    field = order_params.reshape(slots, depth * rows, cols)
    sizes = (slots, depth, rows, cols)
    work = pl.CostEstimate(flops=20 * field.size, bytes_accessed=2 * 4 * field.size, transcendentals=0)

    now, stepped, squares, x_low, x_up, lists = pl.pallas_call(
        functools.partial(first_kernel, *sizes),
        out_shape=[padded, padded, planes, x_pack, x_pack, shape((4 * SPAN + slots,), jnp.int32)],
        in_specs=[hbm] * 4,
        out_specs=[vmem] * 5 + [smem],
        scratch_shapes=[
            pltpu.VMEM(zplanes.shape, jnp.int32),
            pltpu.SMEM(grain_ids.shape, jnp.int32),
            pltpu.SMEM(channel_maps.shape, jnp.int32),
            pltpu.SMEM((2 * (slots + 1),), jnp.int32),
            pltpu.SemaphoreType.DMA((3 + depth // PART,)),
        ],
        compiler_params=params,
        name="first_step",
    )(*(pltpu.with_memory_space_constraint(x, pltpu.HBM) for x in (field, zplanes, grain_ids, channel_maps)))

    from_low = shifted(x_up, "gx", 1)
    from_up = shifted(x_low, "gx", -1)

    y_low, y_up = pl.pallas_call(
        functools.partial(y_kernel, *sizes),
        out_shape=[y_pack, y_pack],
        in_specs=[vmem] * 3 + [smem],
        out_specs=[vmem] * 2,
        compiler_params=params,
        cost_estimate=work,
        name="y_rims",
    )(now, stepped, squares, lists)

    from_right = shifted(y_low, "gy", -1)
    from_left = shifted(y_up, "gy", 1)

    fixed, later = pl.pallas_call(
        functools.partial(second_kernel, *sizes),
        out_shape=[padded, padded],
        in_specs=[vmem] * 5 + [smem],
        out_specs=[vmem] * 2,
        input_output_aliases={0: 0},
        compiler_params=params,
        cost_estimate=work,
        name="second_step",
    )(stepped, y_low, y_up, from_left, from_right, lists)

    changes = later
    for body, own, got, name in (
        (change_kernel, x_low, from_low, "corners_low"),
        (both_changes_kernel, x_up, from_up, "corners_up"),
    ):
        changes = pl.pallas_call(
            functools.partial(body, depth, cols),
            out_shape=shape(((2 if body is change_kernel else 4) * depth, cols), f32),
            in_specs=[vmem] * 3,
            out_specs=vmem,
            compiler_params=params,
            name=name,
        )(own, got, changes)

    changes_from_right = shifted(changes, "gy", -1)
    changes_from_left = shifted(changes, "gy", 1)

    _, last = pl.pallas_call(
        functools.partial(third_kernel, *sizes),
        out_shape=[padded, padded],
        in_specs=[vmem] * 7 + [smem],
        out_specs=[vmem] * 2,
        scratch_shapes=[rims],
        input_output_aliases={1: 0},
        compiler_params=params,
        name="third_step",
    )(
        fixed, later, x_low, x_up, from_low, from_up, changes, lists,
    )

    _, result = pl.pallas_call(
        functools.partial(last_kernel, *sizes),
        out_shape=[padded, shape(field.shape, f32)],
        in_specs=[vmem] * 11 + [smem],
        out_specs=[vmem, hbm],
        scratch_shapes=[rims, pltpu.SemaphoreType.DMA],
        input_output_aliases={0: 0},
        compiler_params=params,
        name="last_rims",
    )(
        last, x_low, x_up, from_low, from_up,
        y_low, y_up, from_left, from_right, changes_from_left, changes_from_right, lists,
    )
    return result.reshape(order_params.shape)


def solution(mesh):
    in_specs = (
        P(None, None, "gx", "gy"),
        P("gx", "gy", None),
        P("gx", "gy", None, None),
        P(None, "gx", "gy"),
    )
    return jax.shard_map(
        on_device, mesh=mesh, in_specs=in_specs, out_specs=P(None, None, "gx", "gy"), check_vma=False
    )
```

```python
import functools

import jax
import jax.numpy as jnp
from jax import lax
from jax.experimental import pallas as pl
from jax.experimental.pallas import tpu as pltpu
from jax.sharding import PartitionSpec as P


LINKS = 6
SPAN = 8
GROUP = 16
RATE = 0.1
PART = 4


def row_and_lane(rows, cols):
    row = lax.broadcasted_iota(jnp.int32, (rows, cols), 0)
    lane = lax.broadcasted_iota(jnp.int32, (rows, cols), 1)
    return row, lane


def spin(tile, amount):
    cols = tile.shape[1]
    amount = amount % cols
    return tile if amount == 0 else pltpu.roll(tile, amount, 1)


def group_sum(tile):
    shift = GROUP
    while shift < tile.shape[1]:
        tile = tile + spin(tile, shift)
        shift *= 2
    return tile


def step(src, dst, slots, depth, rows, cols, squares=None, wait=None):
    row, lane = row_and_lane(rows, cols)
    first_row, last_row = row == 0, row == rows - 1
    first_lane, last_lane = lane == 0, lane == cols - 1

    def add(parts, s, term):
        parts[s % 4] = term if parts[s % 4] is None else parts[s % 4] + term

    def total(parts):
        return (parts[0] + parts[1]) + (parts[2] + parts[3])

    def at(z):
        return pl.ds((z + 1) * rows, rows)

    def layer(z, factor):
        following, parts = [None] * 4, [None] * 4
        for s in range(slots):
            v, below, above = src[s, at(z), :], src[s, at(z - 1), :], src[s, at(z + 1), :]
            add(following, s, above * above)
            base = (z + 1) * rows
            x_sum = jnp.where(first_row, 0.0, src[s, pl.ds(base - 1, rows), :]) + jnp.where(
                last_row, 0.0, src[s, pl.ds(base + 1, rows), :]
            )
            y_sum = jnp.where(first_lane, 0.0, pltpu.roll(v, 1, 1)) + jnp.where(
                last_lane, 0.0, pltpu.roll(v, cols - 1, 1)
            )
            new = RATE * (v * (factor + v * v) + ((x_sum + y_sum) + (below + above)))
            dst[s, at(z), :] = new
            if squares is not None:
                add(parts, s, new * new)
        if squares is not None:
            squares[pl.ds(z * rows, rows), :] = total(parts)
        return 4.5 - 1.5 * total(following)

    first = [None] * 4
    for s in range(slots):
        v = src[s, at(0), :]
        add(first, s, v * v)
    factor = 4.5 - 1.5 * total(first)
    for z in range(depth):
        if wait is not None and z % PART == PART - 1 and z < depth - 1:
            wait(z // PART + 1)
        factor = layer(z, factor)


def gather_columns(ref, low, up, depth, rows, cols, beside=False):
    _, lane = row_and_lane(rows, cols)
    shifts = (0, -1, 1, -2) if beside else (0, -1)
    results = [jnp.zeros((rows, cols), jnp.float32)] * len(shifts)
    for k in range(LINKS):
        parts = [jnp.zeros((rows, cols), jnp.float32)] * len(shifts)
        for z in range(depth):
            at = pl.ds((z + 1) * rows, rows)
            place = GROUP * k + z
            moved = spin(jnp.where(lane < cols // 2, ref[low[k], at, :], ref[up[k], at, :]), place)
            for i, shift in enumerate(shifts):
                parts[i] = jnp.where(lane == (place + shift) % cols, moved, parts[i])
        results = [result + part for result, part in zip(results, parts)]
    return [spin(result, -shift) for result, shift in zip(results, shifts)]


def x_rows(part, k, depth):
    return pl.ds(part * LINKS * depth + k, depth, stride=LINKS)


def first_kernel(
    slots, depth, rows, cols,
    field, planes, grains, maps,
    now, stepped, squares, x_low, x_up, lists,
    planes_in, grains_in, maps_in, inverse, arrived,
):
    copies = [
        pltpu.make_async_copy(maps, maps_in, arrived.at[0]),
        pltpu.make_async_copy(grains, grains_in, arrived.at[1]),
        pltpu.make_async_copy(planes, planes_in, arrived.at[2]),
    ]
    part = PART * rows

    def field_part(i):
        to = pl.ds(i * part + rows, part)
        source = field.at[:, pl.ds(i * part, part), :]
        return pltpu.make_async_copy(source, now.at[pl.ds(0, slots), to, :], arrived.at[3 + i])

    for copy in copies:
        copy.start()
    for i in range(depth // PART):
        field_part(i).start()
    for ref in (now, stepped):
        ref[slots] = jnp.zeros(((depth + 2) * rows, cols), jnp.float32)
    for face in range(4):
        for place in range(SPAN):
            lists[face * SPAN + place] = slots
    for t in range(slots + 1):
        inverse[t] = slots
        inverse[slots + 1 + t] = slots

    copies[0].wait()
    for s in range(slots):
        for face in (0, 2):
            partner = maps_in[0, 0, face, s]
            inverse[face // 2 * (slots + 1) + jnp.where(partner >= 0, partner, slots)] = s
    counts = [jnp.int32(face * SPAN) for face in range(4)]
    for s in range(slots):
        partners = [maps_in[0, 0, face, s] for face in range(4)]
        best = jnp.maximum(jnp.maximum(partners[0], partners[1]), jnp.maximum(partners[2], partners[3]))
        lists[4 * SPAN + s] = (best >= 0).astype(jnp.int32)
        for face in range(4):
            if face in (1, 3):
                valid = partners[face] >= 0
                slot = jnp.where(valid, s, slots)
            else:
                slot = inverse[face // 2 * (slots + 1) + s]
                valid = slot < slots
            lists[counts[face]] = slot
            counts[face] = counts[face] + valid.astype(jnp.int32)

    top = (depth + 1) * rows
    copies[1].wait()
    copies[2].wait()
    for s in range(slots):
        grain = grains_in[0, 0, s]
        below = jnp.where(planes_in[0] == grain, 1.0, 0.0)
        above = jnp.where(planes_in[1] == grain, 1.0, 0.0)
        for ref in (now, stepped):
            ref[s, pl.ds(0, rows), :] = below
            ref[s, pl.ds(top, rows), :] = above
    field_part(0).wait()

    step(now, stepped, slots, depth, rows, cols, squares, lambda i: field_part(i).wait())

    linked = [[lists[face * SPAN + k] for k in range(LINKS)] for face in range(4)]
    end = 3 * LINKS * depth
    edge_row, edge_lane = row_and_lane(depth, cols)
    for face, out in ((1, x_up), (0, x_low)):
        r, inner_r = (0, 1) if face == 0 else (rows - 1, rows - 2)
        rim_rows = pl.ds(rows + r, depth, stride=rows)
        rest = squares[pl.ds(r, depth, stride=rows), :]
        for k in range(LINKS):
            slot = linked[face][k]
            partial = stepped[slot, rim_rows, :]
            inner = stepped[slot, pl.ds(rows + inner_r, depth, stride=rows), :]
            below = jnp.broadcast_to(now[slot, pl.ds(r, 1), :], (depth, cols))
            above = jnp.broadcast_to(now[slot, pl.ds(top + r, 1), :], (depth, cols))
            inner = inner + jnp.where(edge_row == 0, below, jnp.where(edge_row == depth - 1, above, 0.0))
            rest = rest - partial * partial
            out[x_rows(0, k, depth), :] = now[slot, rim_rows, :]
            out[x_rows(1, k, depth), :] = partial
            out[x_rows(2, k, depth), :] = inner
        corners = [jnp.zeros((depth, cols), jnp.float32)] * 4
        for k in range(LINKS):
            for side in range(2):
                slot = linked[2 + side][k]
                for i, ref in enumerate((stepped, now)):
                    place = (2 * i + side) * LINKS + k
                    moved = spin(ref[slot, rim_rows, :], place - side * (cols - 1))
                    corners[2 * i + side] = jnp.where(edge_lane == place, moved, corners[2 * i + side])
        out[pl.ds(end, depth), :] = (corners[0] + corners[1]) + (corners[2] + corners[3])
        out[pl.ds(end + depth, depth), :] = rest
        if out.shape[0] > end + 2 * depth:
            left = out.shape[0] - end - 2 * depth
            out[pl.ds(end + 2 * depth, left), :] = jnp.zeros((left, cols), jnp.float32)


def y_kernel(slots, depth, rows, cols, now, stepped, squares, lists, y_low, y_up):
    top = (depth + 1) * rows
    _, lane = row_and_lane(rows, cols)
    low, up = ([lists[face * SPAN + k] for k in range(LINKS)] for face in (2, 3))
    rims = gather_columns(now, low, up, depth, rows, cols)
    *partials, inner_low, inner_up = gather_columns(stepped, low, up, depth, rows, cols, beside=True)
    frozen = [jnp.zeros((rows, cols), jnp.float32)] * 2
    totals = [jnp.zeros((rows, cols), jnp.float32)] * 2
    for k in range(LINKS):
        for z, at in ((0, 0), (depth - 1, top)):
            place = GROUP * k + z
            at = pl.ds(at, rows)
            moved = spin(jnp.where(lane < cols // 2, now[low[k], at, :], now[up[k], at, :]), place)
            for side in range(2):
                frozen[side] = jnp.where(lane == (place - side) % cols, moved, frozen[side])
    for z in range(depth):
        place = LINKS * GROUP + z
        moved = spin(tile(squares, z, rows), place)
        for side in range(2):
            totals[side] = jnp.where(lane == place - side, moved, totals[side])
    for side, out, inner in ((0, y_low, inner_low), (1, y_up, inner_up)):
        rest = spin(totals[side], side) - group_sum(partials[side] * partials[side])
        out[pl.ds(0, rows), :] = rims[side]
        out[pl.ds(rows, rows), :] = partials[side]
        out[pl.ds(2 * rows, rows), :] = jnp.where(in_last_group(lane), rest, inner + spin(frozen[side], side))


def in_last_group(lane):
    return (lane >= LINKS * GROUP) & (lane < (LINKS + 1) * GROUP)


def tile(ref, i, rows):
    return ref[pl.ds(i * rows, rows), :]


def y_faces(ref, tiles, lists, depth, rows, cols, replace=False):
    _, lane = row_and_lane(rows, cols)
    for k in range(LINKS):
        for side in range(2):
            c = side * (cols - 1)
            slot = lists[(2 + side) * SPAN + k]
            ats = [pl.ds((z + 1) * rows, rows) for z in range(depth)]
            old = [ref[slot, at, :] for at in ats]
            for z in range(depth):
                moved = spin(tiles[side], c - GROUP * k - z)
                ref[slot, ats[z], :] = jnp.where(lane == c, moved if replace else old[z] + moved, old[z])


def x_rims(own, got, k, depth):
    zero, one = x_rows(0, k, depth), x_rows(1, k, depth)
    return own[one, :] + RATE * got[zero, :], got[one, :] + RATE * own[zero, :]


def change_kernel(depth, cols, own, got, *refs):
    out = refs[-1]
    change = jnp.zeros((depth, cols), jnp.float32)
    for k in range(LINKS):
        own_one, _ = x_rims(own, got, k, depth)
        partial = own[x_rows(1, k, depth), :]
        change = change + (own_one * own_one - partial * partial)
    out[pl.ds(0, depth), :] = change
    out[pl.ds(depth, depth), :] = got[pl.ds(3 * LINKS * depth, depth), :]
    out[pl.ds(2 * depth, depth), :] = own[pl.ds(3 * LINKS * depth, depth), :]


def both_changes_kernel(depth, cols, own, got, before, out):
    out[pl.ds(0, 3 * depth), :] = before[...]
    change_kernel(depth, cols, own, got, out.at[pl.ds(3 * depth, 3 * depth), :])


def x_rim_step(padded, face, k, one, factor, outer, depth, cols):
    _, lane = row_and_lane(depth, cols)
    z_sum = padded[face, pl.ds(k, depth, stride=SPAN), :] + padded[face, pl.ds(2 * SPAN + k, depth, stride=SPAN), :]
    y_sum = jnp.where(lane == 0, 0.0, pltpu.roll(one, 1, 1)) + jnp.where(
        lane == cols - 1, 0.0, pltpu.roll(one, cols - 1, 1)
    )
    return RATE * (one * (factor + one * one) + (outer + (z_sum + y_sum)))


def y_rim_step(one, factor, outer):
    rows, cols = one.shape
    row, _ = row_and_lane(rows, cols)
    x_sum = jnp.where(row == 0, 0.0, pltpu.roll(one, 1, 0)) + jnp.where(
        row == rows - 1, 0.0, pltpu.roll(one, rows - 1, 0)
    )
    z_sum = spin(one, 1) + spin(one, -1)
    return RATE * (one * (factor + one * one) + (outer + (x_sum + z_sum)))


def later_kernel(
    slots, depth, rows, cols,
    stepped_in, x_low_own, x_up_own, x_low, x_up, y_low_own, y_up_own, y_low, y_up, lists, after,
    now, last,
    later, x_one,
):
    _, lane = row_and_lane(rows, cols)
    for s in range(slots):
        for at in (0, (depth + 1) * rows):
            later[s, pl.ds(at, rows), :] = now[s, pl.ds(at, rows), :]
    for ref in (later, last):
        ref[slots] = jnp.zeros(((depth + 2) * rows, cols), jnp.float32)
    x_one[...] = jnp.zeros(x_one.shape, jnp.float32)
    linked = [[lists[face * SPAN + k] for k in range(LINKS)] for face in range(2)]
    rim_rows = [pl.ds(rows + r, depth, stride=rows) for r in (0, rows - 1)]
    faces = ((0, x_low_own, x_low), (1, x_up_own, x_up))

    x_ones, x_twos = [], []
    for face, own, got in faces:
        rims = [x_rims(own, got, k, depth) for k in range(LINKS)]
        total = got[pl.ds((3 * LINKS + 1) * depth, depth), :]
        for k, (own_one, one) in enumerate(rims):
            now[linked[face][k], rim_rows[face], :] = own_one
            total = total + one * one
            x_one[face, pl.ds(SPAN + k, depth, stride=SPAN), :] = one
        factor = 4.5 - 1.5 * total
        x_ones.append([RATE * one for _, one in rims])
        two = []
        for k, (own_one, one) in enumerate(rims):
            outer = got[x_rows(2, k, depth), :] + own_one
            two.append(RATE * x_rim_step(x_one, face, k, one, factor, outer, depth, cols))
        x_twos.append(two)
    y_own_ones, y_ones, y_twos = [], [], []
    for own, got in ((y_low_own, y_low), (y_up_own, y_up)):
        own_one = tile(own, 1, rows) + RATE * tile(got, 0, rows)
        one = tile(got, 1, rows) + RATE * tile(own, 0, rows)
        inner = tile(got, 2, rows)
        factor = 4.5 - 1.5 * group_sum(one * one + jnp.where(in_last_group(lane), inner, 0.0))
        y_own_ones.append(own_one)
        y_ones.append(RATE * one)
        y_twos.append(RATE * y_rim_step(one, factor, inner + own_one))

    def add_rims(ref, x_terms, y_terms):
        for face in range(2):
            old = [ref[slot, rim_rows[face], :] for slot in linked[face]]
            for k in range(LINKS):
                ref[linked[face][k], rim_rows[face], :] = old[k] + x_terms[face][k]
        y_faces(ref, y_terms, lists, depth, rows, cols)

    y_faces(now, y_own_ones, lists, depth, rows, cols, replace=True)
    step(now, later, slots, depth, rows, cols)
    add_rims(later, x_ones, y_ones)
    step(later, last, slots, depth, rows, cols)
    add_rims(last, x_twos, y_twos)


def last_kernel(
    slots, depth, rows, cols,
    last_in, x_low_own, x_up_own, x_low, x_up, from_left, from_right, lists,
    last, result,
    sent,
):
    def send(slot):
        pltpu.make_async_copy(last.at[slot, pl.ds(rows, depth * rows), :], result.at[slot], sent).start()

    for s in range(slots):
        pl.when(lists[4 * SPAN + s] == 0)(functools.partial(send, s))

    _, lane = row_and_lane(depth, cols)
    scale = -1.5 * RATE * RATE
    passed_on = (from_left, from_right)
    part = lambda ref, i: ref[pl.ds(i * depth, depth), :]
    corner_cells = lambda ref: ref[pl.ds(3 * LINKS * depth, depth), :]
    linked = [[lists[face * SPAN + k] for k in range(LINKS)] for face in range(4)]
    rims = [pl.ds(rows + r, depth, stride=rows) for r in (0, rows - 1)]

    for face, own, got in ((0, x_low_own, x_low), (1, x_up_own, x_up)):
        total = jnp.zeros((depth, cols), jnp.float32)
        for side in range(2):
            place = side * LINKS
            term = RATE * spin(part(passed_on[side], 3 * face + 1), place - (3 - side) * LINKS)
            term = term * (2.0 * corner_cells(got) + term)
            term = jnp.where((lane >= place) & (lane < place + LINKS), term, 0.0)
            column = jnp.sum(term, axis=1, keepdims=True)
            total = total + jnp.where(lane == side * (cols - 1), column, 0.0)
        total = scale * total
        old = [last[slot, rims[face], :] for slot in linked[face]]
        for k in range(LINKS):
            _, one = x_rims(own, got, k, depth)
            last[linked[face][k], rims[face], :] = old[k] + total * one

    for side in range(2):
        c = side * (cols - 1)
        for face, own in ((0, x_low_own), (1, x_up_own)):
            place = (1 - side) * LINKS
            one = part(passed_on[side], 3 * face + 2) + RATE * spin(corner_cells(own), place - (2 + side) * LINKS)
            change = jnp.where(lane == cols - 1 - c, part(passed_on[side], 3 * face), 0.0)
            one = scale * one * jnp.sum(change, axis=1, keepdims=True)
            old = [last[slot, rims[face], :] for slot in linked[2 + side]]
            for k in range(LINKS):
                moved = jnp.where(lane == c, spin(one, c - place - k), 0.0)
                last[linked[2 + side][k], rims[face], :] = old[k] + moved
    for face in range(4):
        for slot in linked[face]:
            pl.when(slot < slots)(functools.partial(send, slot))
    pltpu.make_async_copy(last.at[pl.ds(0, slots), pl.ds(rows, depth * rows), :], result, sent).wait()


def shifted(block, axis, distance):
    size = lax.axis_size(axis)
    return lax.ppermute(block, axis, [((i - distance) % size, i) for i in range(size)])


def on_device(order_params, grain_ids, channel_maps, zplanes):
    slots, depth, rows, cols = order_params.shape
    f32 = jnp.float32
    shape = jax.ShapeDtypeStruct
    padded = pltpu.VMEM((slots + 1, (depth + 2) * rows, cols), f32)
    planes = pltpu.VMEM((depth * rows, cols), f32)
    x_pack = shape((-(-(3 * LINKS + 2) * depth // rows) * rows, cols), f32)
    y_pack = shape((3 * rows, cols), f32)
    rims = pltpu.VMEM((2, (depth + 2) * SPAN, cols), f32)
    vmem = pl.BlockSpec(memory_space=pltpu.VMEM)
    smem = pl.BlockSpec(memory_space=pltpu.SMEM)
    hbm = pl.BlockSpec(memory_space=pltpu.HBM)
    params = pltpu.CompilerParams(vmem_limit_bytes=24 * 1024 * 1024)
    field = order_params.reshape(slots, depth * rows, cols)
    sizes = (slots, depth, rows, cols)
    work = pl.CostEstimate(flops=20 * field.size, bytes_accessed=2 * 4 * field.size, transcendentals=0)

    now, stepped, squares, x_low, x_up, lists = pl.pallas_call(
        functools.partial(first_kernel, *sizes),
        out_shape=[padded, padded, planes, x_pack, x_pack, shape((4 * SPAN + slots,), jnp.int32)],
        in_specs=[hbm] * 4,
        out_specs=[vmem] * 5 + [smem],
        scratch_shapes=[
            pltpu.VMEM(zplanes.shape, jnp.int32),
            pltpu.SMEM(grain_ids.shape, jnp.int32),
            pltpu.SMEM(channel_maps.shape, jnp.int32),
            pltpu.SMEM((2 * (slots + 1),), jnp.int32),
            pltpu.SemaphoreType.DMA((3 + depth // PART,)),
        ],
        compiler_params=params,
        name="first_step",
    )(*(pltpu.with_memory_space_constraint(x, pltpu.HBM) for x in (field, zplanes, grain_ids, channel_maps)))

    from_low = shifted(x_up, "gx", 1)
    from_up = shifted(x_low, "gx", -1)

    y_low, y_up = pl.pallas_call(
        functools.partial(y_kernel, *sizes),
        out_shape=[y_pack, y_pack],
        in_specs=[vmem] * 3 + [smem],
        out_specs=[vmem] * 2,
        compiler_params=params,
        cost_estimate=work,
        name="y_rims",
    )(now, stepped, squares, lists)

    from_right = shifted(y_low, "gy", -1)
    from_left = shifted(y_up, "gy", 1)

    changes = (from_left, from_right)
    for body, own, got, name in (
        (change_kernel, x_low, from_low, "corners_low"),
        (both_changes_kernel, x_up, from_up, "corners_up"),
    ):
        changes = [
            pl.pallas_call(
                functools.partial(body, depth, cols),
                out_shape=shape(((3 if body is change_kernel else 6) * depth, cols), f32),
                in_specs=[vmem] * (2 + len(changes)),
                out_specs=vmem,
                compiler_params=params,
                name=name,
            )(own, got, *changes)
        ]
    changes = changes[0]

    changes_from_right = shifted(changes, "gy", -1)
    changes_from_left = shifted(changes, "gy", 1)

    _, last = pl.pallas_call(
        functools.partial(later_kernel, *sizes),
        out_shape=[padded, padded],
        in_specs=[vmem] * 9 + [smem, vmem],
        out_specs=[vmem] * 2,
        scratch_shapes=[padded, rims],
        input_output_aliases={0: 0},
        compiler_params=params,
        name="later_steps",
    )(stepped, x_low, x_up, from_low, from_up, y_low, y_up, from_left, from_right, lists, changes)

    _, result = pl.pallas_call(
        functools.partial(last_kernel, *sizes),
        out_shape=[padded, shape(field.shape, f32)],
        in_specs=[vmem] * 7 + [smem],
        out_specs=[vmem, hbm],
        scratch_shapes=[pltpu.SemaphoreType.DMA],
        input_output_aliases={0: 0},
        compiler_params=params,
        name="last_corners",
    )(last, x_low, x_up, from_low, from_up, changes_from_left, changes_from_right, lists)
    return result.reshape(order_params.shape)


def solution(mesh):
    in_specs = (
        P(None, None, "gx", "gy"),
        P("gx", "gy", None),
        P("gx", "gy", None, None),
        P(None, "gx", "gy"),
    )
    return jax.shard_map(
        on_device, mesh=mesh, in_specs=in_specs, out_specs=P(None, None, "gx", "gy"), check_vma=False
    )
```

```python
import functools

import jax
import jax.numpy as jnp
from jax import lax
from jax.experimental import pallas as pl
from jax.experimental.pallas import tpu as pltpu
from jax.sharding import PartitionSpec as P


LINKS = 6
SPAN = 8
GROUP = 16
RATE = 0.1
PART = 4


def row_and_lane(rows, cols):
    row = lax.broadcasted_iota(jnp.int32, (rows, cols), 0)
    lane = lax.broadcasted_iota(jnp.int32, (rows, cols), 1)
    return row, lane


def spin(tile, amount):
    cols = tile.shape[1]
    amount = amount % cols
    return tile if amount == 0 else pltpu.roll(tile, amount, 1)


def group_sum(tile):
    shift = GROUP
    while shift < tile.shape[1]:
        tile = tile + spin(tile, shift)
        shift *= 2
    return tile


def step(src, dst, slots, depth, rows, cols, squares=None, wait=None):
    row, lane = row_and_lane(rows, cols)
    first_row, last_row = row == 0, row == rows - 1
    first_lane, last_lane = lane == 0, lane == cols - 1

    def add(parts, s, term):
        parts[s % 4] = term if parts[s % 4] is None else parts[s % 4] + term

    def total(parts):
        return (parts[0] + parts[1]) + (parts[2] + parts[3])

    def at(z):
        return pl.ds((z + 1) * rows, rows)

    def layer(z, factor):
        following, parts = [None] * 4, [None] * 4
        for s in range(slots):
            v, below, above = src[s, at(z), :], src[s, at(z - 1), :], src[s, at(z + 1), :]
            add(following, s, above * above)
            base = (z + 1) * rows
            x_sum = jnp.where(first_row, 0.0, src[s, pl.ds(base - 1, rows), :]) + jnp.where(
                last_row, 0.0, src[s, pl.ds(base + 1, rows), :]
            )
            y_sum = jnp.where(first_lane, 0.0, pltpu.roll(v, 1, 1)) + jnp.where(
                last_lane, 0.0, pltpu.roll(v, cols - 1, 1)
            )
            new = RATE * (v * (factor + v * v) + ((x_sum + y_sum) + (below + above)))
            dst[s, at(z), :] = new
            if squares is not None:
                add(parts, s, new * new)
        if squares is not None:
            squares[pl.ds(z * rows, rows), :] = total(parts)
        return 4.5 - 1.5 * total(following)

    first = [None] * 4
    for s in range(slots):
        v = src[s, at(0), :]
        add(first, s, v * v)
    factor = 4.5 - 1.5 * total(first)
    for z in range(depth):
        if wait is not None and z % PART == PART - 1 and z < depth - 1:
            wait(z // PART + 1)
        factor = layer(z, factor)


def gather_columns(ref, low, up, depth, rows, cols, beside=False):
    _, lane = row_and_lane(rows, cols)
    shifts = (0, -1, 1, -2) if beside else (0, -1)
    results = [jnp.zeros((rows, cols), jnp.float32)] * len(shifts)
    for k in range(LINKS):
        parts = [jnp.zeros((rows, cols), jnp.float32)] * len(shifts)
        for z in range(depth):
            at = pl.ds((z + 1) * rows, rows)
            place = GROUP * k + z
            moved = spin(jnp.where(lane < cols // 2, ref[low[k], at, :], ref[up[k], at, :]), place)
            for i, shift in enumerate(shifts):
                parts[i] = jnp.where(lane == (place + shift) % cols, moved, parts[i])
        results = [result + part for result, part in zip(results, parts)]
    return [spin(result, -shift) for result, shift in zip(results, shifts)]


def x_rows(part, k, depth):
    return pl.ds(part * LINKS * depth + k, depth, stride=LINKS)


def first_kernel(
    slots, depth, rows, cols,
    field, planes, grains, maps,
    now, stepped, squares, x_low, x_up, lists,
    planes_in, grains_in, maps_in, inverse, arrived,
):
    copies = [
        pltpu.make_async_copy(maps, maps_in, arrived.at[0]),
        pltpu.make_async_copy(grains, grains_in, arrived.at[1]),
        pltpu.make_async_copy(planes, planes_in, arrived.at[2]),
    ]
    part = PART * rows

    def field_part(i):
        to = pl.ds(i * part + rows, part)
        source = field.at[:, pl.ds(i * part, part), :]
        return pltpu.make_async_copy(source, now.at[pl.ds(0, slots), to, :], arrived.at[3 + i])

    for copy in copies:
        copy.start()
    for i in range(depth // PART):
        field_part(i).start()
    for ref in (now, stepped):
        ref[slots] = jnp.zeros(((depth + 2) * rows, cols), jnp.float32)
    for face in range(4):
        for place in range(SPAN):
            lists[face * SPAN + place] = slots
    for t in range(slots + 1):
        inverse[t] = slots
        inverse[slots + 1 + t] = slots

    copies[0].wait()
    for s in range(slots):
        for face in (0, 2):
            partner = maps_in[0, 0, face, s]
            inverse[face // 2 * (slots + 1) + jnp.where(partner >= 0, partner, slots)] = s
    counts = [jnp.int32(face * SPAN) for face in range(4)]
    for s in range(slots):
        partners = [maps_in[0, 0, face, s] for face in range(4)]
        best = jnp.maximum(jnp.maximum(partners[0], partners[1]), jnp.maximum(partners[2], partners[3]))
        lists[4 * SPAN + s] = (best >= 0).astype(jnp.int32)
        for face in range(4):
            if face in (1, 3):
                valid = partners[face] >= 0
                slot = jnp.where(valid, s, slots)
            else:
                slot = inverse[face // 2 * (slots + 1) + s]
                valid = slot < slots
            lists[counts[face]] = slot
            counts[face] = counts[face] + valid.astype(jnp.int32)

    top = (depth + 1) * rows
    copies[1].wait()
    copies[2].wait()
    for s in range(slots):
        grain = grains_in[0, 0, s]
        below = jnp.where(planes_in[0] == grain, 1.0, 0.0)
        above = jnp.where(planes_in[1] == grain, 1.0, 0.0)
        for ref in (now, stepped):
            ref[s, pl.ds(0, rows), :] = below
            ref[s, pl.ds(top, rows), :] = above
    field_part(0).wait()

    step(now, stepped, slots, depth, rows, cols, squares, lambda i: field_part(i).wait())

    linked = [[lists[face * SPAN + k] for k in range(LINKS)] for face in range(4)]
    end = 3 * LINKS * depth
    edge_row, edge_lane = row_and_lane(depth, cols)
    for face, out in ((1, x_up), (0, x_low)):
        r, inner_r = (0, 1) if face == 0 else (rows - 1, rows - 2)
        rim_rows = pl.ds(rows + r, depth, stride=rows)
        rest = squares[pl.ds(r, depth, stride=rows), :]
        for k in range(LINKS):
            slot = linked[face][k]
            partial = stepped[slot, rim_rows, :]
            inner = stepped[slot, pl.ds(rows + inner_r, depth, stride=rows), :]
            below = jnp.broadcast_to(now[slot, pl.ds(r, 1), :], (depth, cols))
            above = jnp.broadcast_to(now[slot, pl.ds(top + r, 1), :], (depth, cols))
            inner = inner + jnp.where(edge_row == 0, below, jnp.where(edge_row == depth - 1, above, 0.0))
            rest = rest - partial * partial
            out[x_rows(0, k, depth), :] = now[slot, rim_rows, :]
            out[x_rows(1, k, depth), :] = partial
            out[x_rows(2, k, depth), :] = inner
        corners = [jnp.zeros((depth, cols), jnp.float32)] * 4
        for k in range(LINKS):
            for side in range(2):
                slot = linked[2 + side][k]
                for i, ref in enumerate((stepped, now)):
                    place = (2 * i + side) * LINKS + k
                    moved = spin(ref[slot, rim_rows, :], place - side * (cols - 1))
                    corners[2 * i + side] = jnp.where(edge_lane == place, moved, corners[2 * i + side])
        out[pl.ds(end, depth), :] = (corners[0] + corners[1]) + (corners[2] + corners[3])
        out[pl.ds(end + depth, depth), :] = rest
        if out.shape[0] > end + 2 * depth:
            left = out.shape[0] - end - 2 * depth
            out[pl.ds(end + 2 * depth, left), :] = jnp.zeros((left, cols), jnp.float32)


def y_kernel(slots, depth, rows, cols, now, stepped, squares, lists, y_low, y_up):
    top = (depth + 1) * rows
    _, lane = row_and_lane(rows, cols)
    low, up = ([lists[face * SPAN + k] for k in range(LINKS)] for face in (2, 3))
    rims = gather_columns(now, low, up, depth, rows, cols)
    *partials, inner_low, inner_up = gather_columns(stepped, low, up, depth, rows, cols, beside=True)
    frozen = [jnp.zeros((rows, cols), jnp.float32)] * 2
    totals = [jnp.zeros((rows, cols), jnp.float32)] * 2
    for k in range(LINKS):
        for z, at in ((0, 0), (depth - 1, top)):
            place = GROUP * k + z
            at = pl.ds(at, rows)
            moved = spin(jnp.where(lane < cols // 2, now[low[k], at, :], now[up[k], at, :]), place)
            for side in range(2):
                frozen[side] = jnp.where(lane == (place - side) % cols, moved, frozen[side])
    for z in range(depth):
        place = LINKS * GROUP + z
        moved = spin(tile(squares, z, rows), place)
        for side in range(2):
            totals[side] = jnp.where(lane == place - side, moved, totals[side])
    for side, out, inner in ((0, y_low, inner_low), (1, y_up, inner_up)):
        rest = spin(totals[side], side) - group_sum(partials[side] * partials[side])
        out[pl.ds(0, rows), :] = rims[side]
        out[pl.ds(rows, rows), :] = partials[side]
        out[pl.ds(2 * rows, rows), :] = jnp.where(in_last_group(lane), rest, inner + spin(frozen[side], side))


def in_last_group(lane):
    return (lane >= LINKS * GROUP) & (lane < (LINKS + 1) * GROUP)


def tile(ref, i, rows):
    return ref[pl.ds(i * rows, rows), :]


def y_faces(ref, tiles, lists, depth, rows, cols, replace=False):
    _, lane = row_and_lane(rows, cols)
    for k in range(LINKS):
        for side in range(2):
            c = side * (cols - 1)
            slot = lists[(2 + side) * SPAN + k]
            ats = [pl.ds((z + 1) * rows, rows) for z in range(depth)]
            old = [ref[slot, at, :] for at in ats]
            for z in range(depth):
                moved = spin(tiles[side], c - GROUP * k - z)
                ref[slot, ats[z], :] = jnp.where(lane == c, moved if replace else old[z] + moved, old[z])


def x_rims(own, got, k, depth):
    zero, one = x_rows(0, k, depth), x_rows(1, k, depth)
    return own[one, :] + RATE * got[zero, :], got[one, :] + RATE * own[zero, :]


def change_kernel(depth, cols, own, got, *refs):
    out = refs[-1]
    change = jnp.zeros((depth, cols), jnp.float32)
    for k in range(LINKS):
        own_one, _ = x_rims(own, got, k, depth)
        partial = own[x_rows(1, k, depth), :]
        change = change + (own_one * own_one - partial * partial)
    out[pl.ds(0, depth), :] = change
    out[pl.ds(depth, depth), :] = got[pl.ds(3 * LINKS * depth, depth), :]
    out[pl.ds(2 * depth, depth), :] = own[pl.ds(3 * LINKS * depth, depth), :]


def both_changes_kernel(depth, cols, own, got, before, out):
    out[pl.ds(0, 3 * depth), :] = before[...]
    change_kernel(depth, cols, own, got, out.at[pl.ds(3 * depth, 3 * depth), :])


def x_rim_step(padded, face, k, one, factor, outer, depth, cols):
    _, lane = row_and_lane(depth, cols)
    z_sum = padded[face, pl.ds(k, depth, stride=SPAN), :] + padded[face, pl.ds(2 * SPAN + k, depth, stride=SPAN), :]
    y_sum = jnp.where(lane == 0, 0.0, pltpu.roll(one, 1, 1)) + jnp.where(
        lane == cols - 1, 0.0, pltpu.roll(one, cols - 1, 1)
    )
    return RATE * (one * (factor + one * one) + (outer + (z_sum + y_sum)))


def y_rim_step(one, factor, outer):
    rows, cols = one.shape
    row, _ = row_and_lane(rows, cols)
    x_sum = jnp.where(row == 0, 0.0, pltpu.roll(one, 1, 0)) + jnp.where(
        row == rows - 1, 0.0, pltpu.roll(one, rows - 1, 0)
    )
    z_sum = spin(one, 1) + spin(one, -1)
    return RATE * (one * (factor + one * one) + (outer + (x_sum + z_sum)))


def later_kernel(
    slots, depth, rows, cols,
    stepped_in, x_low_own, x_up_own, x_low, x_up, y_low_own, y_up_own, y_low, y_up, lists, after,
    now, last,
    later, x_one,
):
    _, lane = row_and_lane(rows, cols)
    for s in range(slots):
        for at in (0, (depth + 1) * rows):
            later[s, pl.ds(at, rows), :] = now[s, pl.ds(at, rows), :]
    for ref in (later, last):
        ref[slots] = jnp.zeros(((depth + 2) * rows, cols), jnp.float32)
    x_one[...] = jnp.zeros(x_one.shape, jnp.float32)
    linked = [[lists[face * SPAN + k] for k in range(LINKS)] for face in range(2)]
    rim_rows = [pl.ds(rows + r, depth, stride=rows) for r in (0, rows - 1)]
    faces = ((0, x_low_own, x_low), (1, x_up_own, x_up))

    x_ones, x_twos = [], []
    for face, own, got in faces:
        rims = [x_rims(own, got, k, depth) for k in range(LINKS)]
        total = got[pl.ds((3 * LINKS + 1) * depth, depth), :]
        for k, (own_one, one) in enumerate(rims):
            now[linked[face][k], rim_rows[face], :] = own_one
            total = total + one * one
            x_one[face, pl.ds(SPAN + k, depth, stride=SPAN), :] = one
        factor = 4.5 - 1.5 * total
        x_ones.append([RATE * one for _, one in rims])
        two = []
        for k, (own_one, one) in enumerate(rims):
            outer = got[x_rows(2, k, depth), :] + own_one
            two.append(RATE * x_rim_step(x_one, face, k, one, factor, outer, depth, cols))
        x_twos.append(two)
    y_own_ones, y_ones, y_twos = [], [], []
    for own, got in ((y_low_own, y_low), (y_up_own, y_up)):
        own_one = tile(own, 1, rows) + RATE * tile(got, 0, rows)
        one = tile(got, 1, rows) + RATE * tile(own, 0, rows)
        inner = tile(got, 2, rows)
        factor = 4.5 - 1.5 * group_sum(one * one + jnp.where(in_last_group(lane), inner, 0.0))
        y_own_ones.append(own_one)
        y_ones.append(RATE * one)
        y_twos.append(RATE * y_rim_step(one, factor, inner + own_one))

    def add_rims(ref, x_terms, y_terms):
        for face in range(2):
            old = [ref[slot, rim_rows[face], :] for slot in linked[face]]
            for k in range(LINKS):
                ref[linked[face][k], rim_rows[face], :] = old[k] + x_terms[face][k]
        y_faces(ref, y_terms, lists, depth, rows, cols)

    y_faces(now, y_own_ones, lists, depth, rows, cols, replace=True)
    step(now, later, slots, depth, rows, cols)
    add_rims(later, x_ones, y_ones)
    step(later, last, slots, depth, rows, cols)
    add_rims(last, x_twos, y_twos)


def last_kernel(
    slots, depth, rows, cols,
    last_in, x_low_own, x_up_own, x_low, x_up, from_left, from_right, lists,
    last, result,
    sent,
):
    _, lane = row_and_lane(depth, cols)
    scale = -1.5 * RATE * RATE
    passed_on = (from_left, from_right)
    part = lambda ref, i: ref[pl.ds(i * depth, depth), :]
    corner_cells = lambda ref: ref[pl.ds(3 * LINKS * depth, depth), :]
    linked = [[lists[face * SPAN + k] for k in range(LINKS)] for face in range(4)]
    rims = [pl.ds(rows + r, depth, stride=rows) for r in (0, rows - 1)]

    for face, own, got in ((0, x_low_own, x_low), (1, x_up_own, x_up)):
        total = jnp.zeros((depth, cols), jnp.float32)
        for side in range(2):
            place = side * LINKS
            term = RATE * spin(part(passed_on[side], 3 * face + 1), place - (3 - side) * LINKS)
            term = term * (2.0 * corner_cells(got) + term)
            term = jnp.where((lane >= place) & (lane < place + LINKS), term, 0.0)
            column = jnp.sum(term, axis=1, keepdims=True)
            total = total + jnp.where(lane == side * (cols - 1), column, 0.0)
        total = scale * total
        old = [last[slot, rims[face], :] for slot in linked[face]]
        for k in range(LINKS):
            _, one = x_rims(own, got, k, depth)
            last[linked[face][k], rims[face], :] = old[k] + total * one

    for side in range(2):
        c = side * (cols - 1)
        for face, own in ((0, x_low_own), (1, x_up_own)):
            place = (1 - side) * LINKS
            one = part(passed_on[side], 3 * face + 2) + RATE * spin(corner_cells(own), place - (2 + side) * LINKS)
            change = jnp.where(lane == cols - 1 - c, part(passed_on[side], 3 * face), 0.0)
            one = scale * one * jnp.sum(change, axis=1, keepdims=True)
            old = [last[slot, rims[face], :] for slot in linked[2 + side]]
            for k in range(LINKS):
                moved = jnp.where(lane == c, spin(one, c - place - k), 0.0)
                last[linked[2 + side][k], rims[face], :] = old[k] + moved
    copy = pltpu.make_async_copy(last.at[pl.ds(0, slots), pl.ds(rows, depth * rows), :], result, sent)
    copy.start()
    copy.wait()


def shifted(block, axis, distance):
    size = lax.axis_size(axis)
    return lax.ppermute(block, axis, [((i - distance) % size, i) for i in range(size)])


def on_device(order_params, grain_ids, channel_maps, zplanes):
    slots, depth, rows, cols = order_params.shape
    f32 = jnp.float32
    shape = jax.ShapeDtypeStruct
    padded = pltpu.VMEM((slots + 1, (depth + 2) * rows, cols), f32)
    planes = pltpu.VMEM((depth * rows, cols), f32)
    x_pack = shape((-(-(3 * LINKS + 2) * depth // rows) * rows, cols), f32)
    y_pack = shape((3 * rows, cols), f32)
    rims = pltpu.VMEM((2, (depth + 2) * SPAN, cols), f32)
    vmem = pl.BlockSpec(memory_space=pltpu.VMEM)
    smem = pl.BlockSpec(memory_space=pltpu.SMEM)
    hbm = pl.BlockSpec(memory_space=pltpu.HBM)
    params = pltpu.CompilerParams(vmem_limit_bytes=24 * 1024 * 1024)
    field = order_params.reshape(slots, depth * rows, cols)
    sizes = (slots, depth, rows, cols)
    work = pl.CostEstimate(flops=20 * field.size, bytes_accessed=2 * 4 * field.size, transcendentals=0)

    now, stepped, squares, x_low, x_up, lists = pl.pallas_call(
        functools.partial(first_kernel, *sizes),
        out_shape=[padded, padded, planes, x_pack, x_pack, shape((4 * SPAN + slots,), jnp.int32)],
        in_specs=[hbm] * 4,
        out_specs=[vmem] * 5 + [smem],
        scratch_shapes=[
            pltpu.VMEM(zplanes.shape, jnp.int32),
            pltpu.SMEM(grain_ids.shape, jnp.int32),
            pltpu.SMEM(channel_maps.shape, jnp.int32),
            pltpu.SMEM((2 * (slots + 1),), jnp.int32),
            pltpu.SemaphoreType.DMA((3 + depth // PART,)),
        ],
        compiler_params=params,
        name="first_step",
    )(*(pltpu.with_memory_space_constraint(x, pltpu.HBM) for x in (field, zplanes, grain_ids, channel_maps)))

    from_low = shifted(x_up, "gx", 1)
    from_up = shifted(x_low, "gx", -1)

    y_low, y_up = pl.pallas_call(
        functools.partial(y_kernel, *sizes),
        out_shape=[y_pack, y_pack],
        in_specs=[vmem] * 3 + [smem],
        out_specs=[vmem] * 2,
        compiler_params=params,
        cost_estimate=work,
        name="y_rims",
    )(now, stepped, squares, lists)

    from_right = shifted(y_low, "gy", -1)
    from_left = shifted(y_up, "gy", 1)

    changes = (from_left, from_right)
    for body, own, got, name in (
        (change_kernel, x_low, from_low, "corners_low"),
        (both_changes_kernel, x_up, from_up, "corners_up"),
    ):
        changes = [
            pl.pallas_call(
                functools.partial(body, depth, cols),
                out_shape=shape(((3 if body is change_kernel else 6) * depth, cols), f32),
                in_specs=[vmem] * (2 + len(changes)),
                out_specs=vmem,
                compiler_params=params,
                name=name,
            )(own, got, *changes)
        ]
    changes = changes[0]

    changes_from_right = shifted(changes, "gy", -1)
    changes_from_left = shifted(changes, "gy", 1)

    _, last = pl.pallas_call(
        functools.partial(later_kernel, *sizes),
        out_shape=[padded, padded],
        in_specs=[vmem] * 9 + [smem, vmem],
        out_specs=[vmem] * 2,
        scratch_shapes=[padded, rims],
        input_output_aliases={0: 0},
        compiler_params=params,
        name="later_steps",
    )(stepped, x_low, x_up, from_low, from_up, y_low, y_up, from_left, from_right, lists, changes)

    _, result = pl.pallas_call(
        functools.partial(last_kernel, *sizes),
        out_shape=[padded, shape(field.shape, f32)],
        in_specs=[vmem] * 7 + [smem],
        out_specs=[vmem, hbm],
        scratch_shapes=[pltpu.SemaphoreType.DMA],
        input_output_aliases={0: 0},
        compiler_params=params,
        name="last_corners",
    )(last, x_low, x_up, from_low, from_up, changes_from_left, changes_from_right, lists)
    return result.reshape(order_params.shape)


def solution(mesh):
    in_specs = (
        P(None, None, "gx", "gy"),
        P("gx", "gy", None),
        P("gx", "gy", None, None),
        P(None, "gx", "gy"),
    )
    return jax.shard_map(
        on_device, mesh=mesh, in_specs=in_specs, out_specs=P(None, None, "gx", "gy"), check_vma=False
    )
```

```python
import functools

import jax
import jax.numpy as jnp
from jax import lax
from jax.experimental import pallas as pl
from jax.experimental.pallas import tpu as pltpu
from jax.sharding import PartitionSpec as P


LINKS = 6
SPAN = 8
GROUP = 16
RATE = 0.1
PART = 4


def row_and_lane(rows, cols):
    row = lax.broadcasted_iota(jnp.int32, (rows, cols), 0)
    lane = lax.broadcasted_iota(jnp.int32, (rows, cols), 1)
    return row, lane


def spin(tile, amount):
    cols = tile.shape[1]
    amount = amount % cols
    return tile if amount == 0 else pltpu.roll(tile, amount, 1)


def group_sum(tile):
    shift = GROUP
    while shift < tile.shape[1]:
        tile = tile + spin(tile, shift)
        shift *= 2
    return tile


def step(src, dst, slots, depth, rows, cols, squares=None, wait=None):
    row, lane = row_and_lane(rows, cols)
    first_row, last_row = row == 0, row == rows - 1
    first_lane, last_lane = lane == 0, lane == cols - 1

    def add(parts, s, term):
        parts[s % 4] = term if parts[s % 4] is None else parts[s % 4] + term

    def total(parts):
        return (parts[0] + parts[1]) + (parts[2] + parts[3])

    def at(z):
        return pl.ds((z + 1) * rows, rows)

    def layer(z, factor):
        following, parts = [None] * 4, [None] * 4
        for s in range(slots):
            v, below, above = src[s, at(z), :], src[s, at(z - 1), :], src[s, at(z + 1), :]
            add(following, s, above * above)
            base = (z + 1) * rows
            x_sum = jnp.where(first_row, 0.0, src[s, pl.ds(base - 1, rows), :]) + jnp.where(
                last_row, 0.0, src[s, pl.ds(base + 1, rows), :]
            )
            y_sum = jnp.where(first_lane, 0.0, pltpu.roll(v, 1, 1)) + jnp.where(
                last_lane, 0.0, pltpu.roll(v, cols - 1, 1)
            )
            new = RATE * (v * (factor + v * v) + ((x_sum + y_sum) + (below + above)))
            dst[s, at(z), :] = new
            if squares is not None:
                add(parts, s, new * new)
        if squares is not None:
            squares[pl.ds(z * rows, rows), :] = total(parts)
        return 4.5 - 1.5 * total(following)

    first = [None] * 4
    for s in range(slots):
        v = src[s, at(0), :]
        add(first, s, v * v)
    factor = 4.5 - 1.5 * total(first)
    for z in range(depth):
        if wait is not None and z % PART == PART - 1 and z < depth - 1:
            wait(z // PART + 1)
        factor = layer(z, factor)


def gather_columns(ref, low, up, depth, rows, cols, beside=False):
    _, lane = row_and_lane(rows, cols)
    shifts = (0, -1, 1, -2) if beside else (0, -1)
    results = [jnp.zeros((rows, cols), jnp.float32)] * len(shifts)
    for k in range(LINKS):
        parts = [jnp.zeros((rows, cols), jnp.float32)] * len(shifts)
        for z in range(depth):
            at = pl.ds((z + 1) * rows, rows)
            place = GROUP * k + z
            moved = spin(jnp.where(lane < cols // 2, ref[low[k], at, :], ref[up[k], at, :]), place)
            for i, shift in enumerate(shifts):
                parts[i] = jnp.where(lane == (place + shift) % cols, moved, parts[i])
        results = [result + part for result, part in zip(results, parts)]
    return [spin(result, -shift) for result, shift in zip(results, shifts)]


def x_rows(part, k, depth):
    return pl.ds(part * LINKS * depth + k, depth, stride=LINKS)


def first_kernel(
    slots, depth, rows, cols,
    field, planes, grains, maps,
    now, stepped, squares, x_low, x_up, lists,
    planes_in, grains_in, maps_in, inverse, arrived,
):
    copies = [
        pltpu.make_async_copy(maps, maps_in, arrived.at[0]),
        pltpu.make_async_copy(grains, grains_in, arrived.at[1]),
        pltpu.make_async_copy(planes, planes_in, arrived.at[2]),
    ]
    part = PART * rows

    def field_part(i):
        to = pl.ds(i * part + rows, part)
        source = field.at[:, pl.ds(i * part, part), :]
        return pltpu.make_async_copy(source, now.at[pl.ds(0, slots), to, :], arrived.at[3 + i])

    for copy in copies:
        copy.start()
    for i in range(depth // PART):
        field_part(i).start()
    for ref in (now, stepped):
        ref[slots] = jnp.zeros(((depth + 2) * rows, cols), jnp.float32)
    for face in range(4):
        for place in range(SPAN):
            lists[face * SPAN + place] = slots
    for t in range(slots + 1):
        inverse[t] = slots
        inverse[slots + 1 + t] = slots

    copies[0].wait()
    for s in range(slots):
        for face in (0, 2):
            partner = maps_in[0, 0, face, s]
            inverse[face // 2 * (slots + 1) + jnp.where(partner >= 0, partner, slots)] = s
    counts = [jnp.int32(face * SPAN) for face in range(4)]
    for s in range(slots):
        partners = [maps_in[0, 0, face, s] for face in range(4)]
        best = jnp.maximum(jnp.maximum(partners[0], partners[1]), jnp.maximum(partners[2], partners[3]))
        lists[4 * SPAN + s] = (best >= 0).astype(jnp.int32)
        for face in range(4):
            if face in (1, 3):
                valid = partners[face] >= 0
                slot = jnp.where(valid, s, slots)
            else:
                slot = inverse[face // 2 * (slots + 1) + s]
                valid = slot < slots
            lists[counts[face]] = slot
            counts[face] = counts[face] + valid.astype(jnp.int32)

    top = (depth + 1) * rows
    copies[1].wait()
    copies[2].wait()
    for s in range(slots):
        grain = grains_in[0, 0, s]
        below = jnp.where(planes_in[0] == grain, 1.0, 0.0)
        above = jnp.where(planes_in[1] == grain, 1.0, 0.0)
        for ref in (now, stepped):
            ref[s, pl.ds(0, rows), :] = below
            ref[s, pl.ds(top, rows), :] = above
    field_part(0).wait()

    step(now, stepped, slots, depth, rows, cols, squares, lambda i: field_part(i).wait())

    linked = [[lists[face * SPAN + k] for k in range(LINKS)] for face in range(4)]
    end = 3 * LINKS * depth
    edge_row, edge_lane = row_and_lane(depth, cols)
    for face, out in ((1, x_up), (0, x_low)):
        r, inner_r = (0, 1) if face == 0 else (rows - 1, rows - 2)
        rim_rows = pl.ds(rows + r, depth, stride=rows)
        rest = squares[pl.ds(r, depth, stride=rows), :]
        for k in range(LINKS):
            slot = linked[face][k]
            partial = stepped[slot, rim_rows, :]
            inner = stepped[slot, pl.ds(rows + inner_r, depth, stride=rows), :]
            below = jnp.broadcast_to(now[slot, pl.ds(r, 1), :], (depth, cols))
            above = jnp.broadcast_to(now[slot, pl.ds(top + r, 1), :], (depth, cols))
            inner = inner + jnp.where(edge_row == 0, below, jnp.where(edge_row == depth - 1, above, 0.0))
            rest = rest - partial * partial
            out[x_rows(0, k, depth), :] = now[slot, rim_rows, :]
            out[x_rows(1, k, depth), :] = partial
            out[x_rows(2, k, depth), :] = inner
        corners = [jnp.zeros((depth, cols), jnp.float32)] * 4
        for k in range(LINKS):
            for side in range(2):
                slot = linked[2 + side][k]
                for i, ref in enumerate((stepped, now)):
                    place = (2 * i + side) * LINKS + k
                    moved = spin(ref[slot, rim_rows, :], place - side * (cols - 1))
                    corners[2 * i + side] = jnp.where(edge_lane == place, moved, corners[2 * i + side])
        out[pl.ds(end, depth), :] = (corners[0] + corners[1]) + (corners[2] + corners[3])
        out[pl.ds(end + depth, depth), :] = rest
        if out.shape[0] > end + 2 * depth:
            left = out.shape[0] - end - 2 * depth
            out[pl.ds(end + 2 * depth, left), :] = jnp.zeros((left, cols), jnp.float32)


def y_kernel(slots, depth, rows, cols, now, stepped, squares, lists, y_low, y_up):
    top = (depth + 1) * rows
    _, lane = row_and_lane(rows, cols)
    low, up = ([lists[face * SPAN + k] for k in range(LINKS)] for face in (2, 3))
    rims = gather_columns(now, low, up, depth, rows, cols)
    *partials, inner_low, inner_up = gather_columns(stepped, low, up, depth, rows, cols, beside=True)
    frozen = [jnp.zeros((rows, cols), jnp.float32)] * 2
    totals = [jnp.zeros((rows, cols), jnp.float32)] * 2
    for k in range(LINKS):
        for z, at in ((0, 0), (depth - 1, top)):
            place = GROUP * k + z
            at = pl.ds(at, rows)
            moved = spin(jnp.where(lane < cols // 2, now[low[k], at, :], now[up[k], at, :]), place)
            for side in range(2):
                frozen[side] = jnp.where(lane == (place - side) % cols, moved, frozen[side])
    for z in range(depth):
        place = LINKS * GROUP + z
        moved = spin(tile(squares, z, rows), place)
        for side in range(2):
            totals[side] = jnp.where(lane == place - side, moved, totals[side])
    for side, out, inner in ((0, y_low, inner_low), (1, y_up, inner_up)):
        rest = spin(totals[side], side) - group_sum(partials[side] * partials[side])
        out[pl.ds(0, rows), :] = rims[side]
        out[pl.ds(rows, rows), :] = partials[side]
        out[pl.ds(2 * rows, rows), :] = jnp.where(in_last_group(lane), rest, inner + spin(frozen[side], side))


def in_last_group(lane):
    return (lane >= LINKS * GROUP) & (lane < (LINKS + 1) * GROUP)


def tile(ref, i, rows):
    return ref[pl.ds(i * rows, rows), :]


def y_faces(ref, tiles, lists, depth, rows, cols, replace=False):
    _, lane = row_and_lane(rows, cols)
    for k in range(LINKS):
        for side in range(2):
            c = side * (cols - 1)
            slot = lists[(2 + side) * SPAN + k]
            ats = [pl.ds((z + 1) * rows, rows) for z in range(depth)]
            old = [ref[slot, at, :] for at in ats]
            for z in range(depth):
                moved = spin(tiles[side], c - GROUP * k - z)
                ref[slot, ats[z], :] = jnp.where(lane == c, moved if replace else old[z] + moved, old[z])


def x_rims(own, got, k, depth):
    zero, one = x_rows(0, k, depth), x_rows(1, k, depth)
    return own[one, :] + RATE * got[zero, :], got[one, :] + RATE * own[zero, :]


def change_kernel(depth, cols, own, got, *refs):
    out = refs[-1]
    change = jnp.zeros((depth, cols), jnp.float32)
    for k in range(LINKS):
        own_one, _ = x_rims(own, got, k, depth)
        partial = own[x_rows(1, k, depth), :]
        change = change + (own_one * own_one - partial * partial)
    out[pl.ds(0, depth), :] = change
    out[pl.ds(depth, depth), :] = got[pl.ds(3 * LINKS * depth, depth), :]
    out[pl.ds(2 * depth, depth), :] = own[pl.ds(3 * LINKS * depth, depth), :]


def both_changes_kernel(depth, cols, own, got, before, out):
    out[pl.ds(0, 3 * depth), :] = before[...]
    change_kernel(depth, cols, own, got, out.at[pl.ds(3 * depth, 3 * depth), :])


def x_rim_step(padded, face, k, one, factor, outer, depth, cols):
    _, lane = row_and_lane(depth, cols)
    z_sum = padded[face, pl.ds(k, depth, stride=SPAN), :] + padded[face, pl.ds(2 * SPAN + k, depth, stride=SPAN), :]
    y_sum = jnp.where(lane == 0, 0.0, pltpu.roll(one, 1, 1)) + jnp.where(
        lane == cols - 1, 0.0, pltpu.roll(one, cols - 1, 1)
    )
    return RATE * (one * (factor + one * one) + (outer + (z_sum + y_sum)))


def y_rim_step(one, factor, outer):
    rows, cols = one.shape
    row, _ = row_and_lane(rows, cols)
    x_sum = jnp.where(row == 0, 0.0, pltpu.roll(one, 1, 0)) + jnp.where(
        row == rows - 1, 0.0, pltpu.roll(one, rows - 1, 0)
    )
    z_sum = spin(one, 1) + spin(one, -1)
    return RATE * (one * (factor + one * one) + (outer + (x_sum + z_sum)))


def later_kernel(
    slots, depth, rows, cols,
    stepped_in, x_low_own, x_up_own, x_low, x_up, y_low_own, y_up_own, y_low, y_up, lists, after,
    now, last,
    later, x_one,
):
    _, lane = row_and_lane(rows, cols)
    for s in range(slots):
        for at in (0, (depth + 1) * rows):
            later[s, pl.ds(at, rows), :] = now[s, pl.ds(at, rows), :]
    for ref in (later, last):
        ref[slots] = jnp.zeros(((depth + 2) * rows, cols), jnp.float32)
    x_one[...] = jnp.zeros(x_one.shape, jnp.float32)
    linked = [[lists[face * SPAN + k] for k in range(LINKS)] for face in range(2)]
    rim_rows = [pl.ds(rows + r, depth, stride=rows) for r in (0, rows - 1)]
    faces = ((0, x_low_own, x_low), (1, x_up_own, x_up))

    x_ones, x_twos = [], []
    for face, own, got in faces:
        rims = [x_rims(own, got, k, depth) for k in range(LINKS)]
        total = got[pl.ds((3 * LINKS + 1) * depth, depth), :]
        for k, (own_one, one) in enumerate(rims):
            now[linked[face][k], rim_rows[face], :] = own_one
            total = total + one * one
            x_one[face, pl.ds(SPAN + k, depth, stride=SPAN), :] = one
        factor = 4.5 - 1.5 * total
        x_ones.append([RATE * one for _, one in rims])
        two = []
        for k, (own_one, one) in enumerate(rims):
            outer = got[x_rows(2, k, depth), :] + own_one
            two.append(RATE * x_rim_step(x_one, face, k, one, factor, outer, depth, cols))
        x_twos.append(two)
    y_own_ones, y_ones, y_twos = [], [], []
    for own, got in ((y_low_own, y_low), (y_up_own, y_up)):
        own_one = tile(own, 1, rows) + RATE * tile(got, 0, rows)
        one = tile(got, 1, rows) + RATE * tile(own, 0, rows)
        inner = tile(got, 2, rows)
        factor = 4.5 - 1.5 * group_sum(one * one + jnp.where(in_last_group(lane), inner, 0.0))
        y_own_ones.append(own_one)
        y_ones.append(RATE * one)
        y_twos.append(RATE * y_rim_step(one, factor, inner + own_one))

    def add_rims(ref, x_terms, y_terms):
        for face in range(2):
            old = [ref[slot, rim_rows[face], :] for slot in linked[face]]
            for k in range(LINKS):
                ref[linked[face][k], rim_rows[face], :] = old[k] + x_terms[face][k]
        y_faces(ref, y_terms, lists, depth, rows, cols)

    y_faces(now, y_own_ones, lists, depth, rows, cols, replace=True)
    step(now, later, slots, depth, rows, cols)
    add_rims(later, x_ones, y_ones)
    step(later, last, slots, depth, rows, cols)
    add_rims(last, x_twos, y_twos)


def last_kernel(
    slots, depth, rows, cols,
    last_in, x_low_own, x_up_own, x_low, x_up, from_left, from_right, lists,
    last, result,
    sent,
):
    def send(slot):
        pltpu.make_async_copy(last.at[slot, pl.ds(rows, depth * rows), :], result.at[slot], sent).start()

    for s in range(slots):
        pl.when(lists[4 * SPAN + s] == 0)(functools.partial(send, s))

    _, lane = row_and_lane(depth, cols)
    scale = -1.5 * RATE * RATE
    passed_on = (from_left, from_right)
    part = lambda ref, i: ref[pl.ds(i * depth, depth), :]
    corner_cells = lambda ref: ref[pl.ds(3 * LINKS * depth, depth), :]
    linked = [[lists[face * SPAN + k] for k in range(LINKS)] for face in range(4)]
    rims = [pl.ds(rows + r, depth, stride=rows) for r in (0, rows - 1)]

    for face, own, got in ((0, x_low_own, x_low), (1, x_up_own, x_up)):
        total = jnp.zeros((depth, cols), jnp.float32)
        for side in range(2):
            place = side * LINKS
            term = RATE * spin(part(passed_on[side], 3 * face + 1), place - (3 - side) * LINKS)
            term = term * (2.0 * corner_cells(got) + term)
            term = jnp.where((lane >= place) & (lane < place + LINKS), term, 0.0)
            column = jnp.sum(term, axis=1, keepdims=True)
            total = total + jnp.where(lane == side * (cols - 1), column, 0.0)
        total = scale * total
        old = [last[slot, rims[face], :] for slot in linked[face]]
        for k in range(LINKS):
            _, one = x_rims(own, got, k, depth)
            last[linked[face][k], rims[face], :] = old[k] + total * one

    for face in (0, 1):
        for slot in linked[face]:
            pl.when(slot < slots)(functools.partial(send, slot))

    for side in range(2):
        c = side * (cols - 1)
        for face, own in ((0, x_low_own), (1, x_up_own)):
            place = (1 - side) * LINKS
            one = part(passed_on[side], 3 * face + 2) + RATE * spin(corner_cells(own), place - (2 + side) * LINKS)
            change = jnp.where(lane == cols - 1 - c, part(passed_on[side], 3 * face), 0.0)
            one = scale * one * jnp.sum(change, axis=1, keepdims=True)
            old = [last[slot, rims[face], :] for slot in linked[2 + side]]
            for k in range(LINKS):
                moved = jnp.where(lane == c, spin(one, c - place - k), 0.0)
                last[linked[2 + side][k], rims[face], :] = old[k] + moved
    for face in (2, 3):
        for slot in linked[face]:
            pl.when(slot < slots)(functools.partial(send, slot))
    pltpu.make_async_copy(last.at[pl.ds(0, slots), pl.ds(rows, depth * rows), :], result, sent).wait()


def shifted(block, axis, distance):
    size = lax.axis_size(axis)
    return lax.ppermute(block, axis, [((i - distance) % size, i) for i in range(size)])


def on_device(order_params, grain_ids, channel_maps, zplanes):
    slots, depth, rows, cols = order_params.shape
    f32 = jnp.float32
    shape = jax.ShapeDtypeStruct
    padded = pltpu.VMEM((slots + 1, (depth + 2) * rows, cols), f32)
    planes = pltpu.VMEM((depth * rows, cols), f32)
    x_pack = shape((-(-(3 * LINKS + 2) * depth // rows) * rows, cols), f32)
    y_pack = shape((3 * rows, cols), f32)
    rims = pltpu.VMEM((2, (depth + 2) * SPAN, cols), f32)
    vmem = pl.BlockSpec(memory_space=pltpu.VMEM)
    smem = pl.BlockSpec(memory_space=pltpu.SMEM)
    hbm = pl.BlockSpec(memory_space=pltpu.HBM)
    params = pltpu.CompilerParams(vmem_limit_bytes=24 * 1024 * 1024)
    field = order_params.reshape(slots, depth * rows, cols)
    sizes = (slots, depth, rows, cols)
    work = pl.CostEstimate(flops=20 * field.size, bytes_accessed=2 * 4 * field.size, transcendentals=0)

    now, stepped, squares, x_low, x_up, lists = pl.pallas_call(
        functools.partial(first_kernel, *sizes),
        out_shape=[padded, padded, planes, x_pack, x_pack, shape((4 * SPAN + slots,), jnp.int32)],
        in_specs=[hbm] * 4,
        out_specs=[vmem] * 5 + [smem],
        scratch_shapes=[
            pltpu.VMEM(zplanes.shape, jnp.int32),
            pltpu.SMEM(grain_ids.shape, jnp.int32),
            pltpu.SMEM(channel_maps.shape, jnp.int32),
            pltpu.SMEM((2 * (slots + 1),), jnp.int32),
            pltpu.SemaphoreType.DMA((3 + depth // PART,)),
        ],
        compiler_params=params,
        name="first_step",
    )(*(pltpu.with_memory_space_constraint(x, pltpu.HBM) for x in (field, zplanes, grain_ids, channel_maps)))

    from_low = shifted(x_up, "gx", 1)
    from_up = shifted(x_low, "gx", -1)

    y_low, y_up = pl.pallas_call(
        functools.partial(y_kernel, *sizes),
        out_shape=[y_pack, y_pack],
        in_specs=[vmem] * 3 + [smem],
        out_specs=[vmem] * 2,
        compiler_params=params,
        cost_estimate=work,
        name="y_rims",
    )(now, stepped, squares, lists)

    from_right = shifted(y_low, "gy", -1)
    from_left = shifted(y_up, "gy", 1)

    changes = (from_left, from_right)
    for body, own, got, name in (
        (change_kernel, x_low, from_low, "corners_low"),
        (both_changes_kernel, x_up, from_up, "corners_up"),
    ):
        changes = [
            pl.pallas_call(
                functools.partial(body, depth, cols),
                out_shape=shape(((3 if body is change_kernel else 6) * depth, cols), f32),
                in_specs=[vmem] * (2 + len(changes)),
                out_specs=vmem,
                compiler_params=params,
                name=name,
            )(own, got, *changes)
        ]
    changes = changes[0]

    changes_from_right = shifted(changes, "gy", -1)
    changes_from_left = shifted(changes, "gy", 1)

    _, last = pl.pallas_call(
        functools.partial(later_kernel, *sizes),
        out_shape=[padded, padded],
        in_specs=[vmem] * 9 + [smem, vmem],
        out_specs=[vmem] * 2,
        scratch_shapes=[padded, rims],
        input_output_aliases={0: 0},
        compiler_params=params,
        name="later_steps",
    )(stepped, x_low, x_up, from_low, from_up, y_low, y_up, from_left, from_right, lists, changes)

    _, result = pl.pallas_call(
        functools.partial(last_kernel, *sizes),
        out_shape=[padded, shape(field.shape, f32)],
        in_specs=[vmem] * 7 + [smem],
        out_specs=[vmem, hbm],
        scratch_shapes=[pltpu.SemaphoreType.DMA],
        input_output_aliases={0: 0},
        compiler_params=params,
        name="last_corners",
    )(last, x_low, x_up, from_low, from_up, changes_from_left, changes_from_right, lists)
    return result.reshape(order_params.shape)


def solution(mesh):
    in_specs = (
        P(None, None, "gx", "gy"),
        P("gx", "gy", None),
        P("gx", "gy", None, None),
        P(None, "gx", "gy"),
    )
    return jax.shard_map(
        on_device, mesh=mesh, in_specs=in_specs, out_specs=P(None, None, "gx", "gy"), check_vma=False
    )
```
